32 devices in a mesh: groups: 2 (over x), cache: 8 (over z, y), serve: 2 (over core).
Axes of the slice: x: 2, y: 2, z: 4, core: 2. Of those that a mesh axis runs over, the one named last changes fastest.
Arguments:
- candidates: bfloat16 [128, 16, 1024], P(('groups', 'cache'), 'serve'), parts along dimension 0
- input_gain: bfloat16 [1024], replicated, may hold values from 0.5 to 1.5
- w_in: bfloat16 [1024, 4, 1024], P(None, None, 'serve'), may hold values from -0.1875 to 0.1875
- w_out: bfloat16 [1024, 1024], P('serve'), may hold values from -0.1875 to 0.1875
- hist_keys: bfloat16 [16, 2048, 1024], P(('groups', 'cache'), None, 'serve'), parts along dimension 0, may hold values from -6 to 6
- hist_values: bfloat16 [16, 2048, 1024], P(('groups', 'cache'), None, 'serve'), parts along dimension 0, may hold values from -0.59765625 to 0.59765625
- request_session: int32 [128, 1], P('groups'), parts along dimension 0, may hold values from 0 to 7; in each aligned block of 8 rows (0 to 7, 8 to 15, ...) at most 2 rows name the same one
- hist_len: int32 [16], P('groups'), parts along dimension 0, may hold values from 1 to 2048, as said below
- block_mask: int32 [128, 32], P('groups'), parts along dimension 0, may hold values 0 or 1
Outputs:
- layer_out: bfloat16 [128, 16, 1024], P(('groups', 'cache'), 'serve'), parts along dimension 0
The draws below stay inside these ranges and needn't reach their ends.
There are 2 independent parts, one for each index of `groups`. The reference program is written for one: setup_inputs(seed, part) draws one part's arguments, and reference() takes and returns one part's arrays. A program takes and returns all parts, laid end to end along the dimension named above; an argument that names none is the same for every part. Nothing has to cross between parts.
Inputs may be any that keep to these rules, and one draw needn't show every extreme that they name: `request_session`: among the 8 requests of one index of cache no session is named more than 2 times, and in some such block one session is named exactly 2 times. `hist_len`: some session has all 2048 rows valid.
All inputs are finite; a program needn't handle non-finite values.
Results may differ from the reference program's by a relative error of at most 0.005.
Values may be sent and summed in bfloat16 or wider, within the bound.
No kernel may reach another device: no remote copies, remote signals or barrier semaphores. Data moves between devices by JAX's collectives and lax.ppermute only.
A program may use at most 128 MiB of HBM per device.

```python
import math
import jax
import jax.numpy as jnp
import numpy as np
from jax import lax

HEADS = 8
HD = 128
D = 1024
CAND = 16
HIST = 2048
BLK = 64
CAP = 2
SESSIONS = 8
REQ_DEV = 8
REQUESTS = 64


def draw_candidates(key, part):
    key = jax.random.fold_in(key, 11)
    base_key, column_key, row_key = jax.random.split(key, 3)
    column_scale = jnp.exp(jax.random.uniform(column_key, (D,), jnp.float32, -1.2, 1.2))
    row_scale = jnp.exp(jax.random.uniform(row_key, (REQUESTS, CAND, 1), jnp.float32, -1.2, 1.2))
    base = jax.random.normal(base_key, (REQUESTS, CAND, D), jnp.float32)
    return (base * column_scale * row_scale).astype(jnp.bfloat16)


def draw_hist_len(key, part):
    key = jax.random.fold_in(key, 23)
    length_key, spot_key = jax.random.split(key)
    lengths = jax.random.randint(length_key, (SESSIONS,), 1, HIST + 1)
    spot = jax.random.randint(spot_key, (), 0, SESSIONS)
    return jnp.where(jnp.arange(SESSIONS) == spot, HIST, lengths).astype(jnp.int32)


def touch_ends(array, key, least, high):
    index_at = [jax.random.randint(jax.random.fold_in(key, axis), (), 0, length) for axis, length in enumerate(array.shape)]
    widest = array.shape.index(max(array.shape))
    neighbour = index_at[:widest] + [(index_at[widest] + 1) % array.shape[widest]] + index_at[widest + 1:]
    return array.at[tuple(index_at)].set(least).at[tuple(neighbour)].set(high)


def levels(rng, extent, shards, low, high):
    def one(position, shards_of):
        heights = jax.random.uniform(jax.random.fold_in(jax.random.fold_in(rng, 6), position), (shards_of,), jnp.float32, low / len(shards), high / len(shards))
        return jnp.repeat(jnp.exp(heights), extent[position] // shards_of).reshape((-1,) + (1,) * (len(extent) - position - 1))

    loudness = one(*shards[0])
    for cut in shards[1:]:
        loudness = loudness * one(*cut)
    return loudness


def assign_block(key, own, number, rows, count, top, bound, slope):
    ranking = jax.random.permutation(key, count)
    crowded, usual = portions_of(count, rows * top, bound, slope, True), portions_of(count, rows * top, bound, slope, False)
    places = jnp.arange(count)

    def named(sizes, offset_by):
        used = int((sizes > 0).sum())
        fixed = max(1, used // 4)
        passed = fixed + (places - fixed + offset_by * (used - fixed)) % max(1, count - fixed)
        return jnp.zeros((count,), jnp.int32).at[ranking[jnp.where(places < fixed, places, passed)]].set(jnp.asarray(sizes, jnp.int32))

    sizes = jnp.where(number % 4 == 0, named(crowded, number // 4), named(usual, number - number // 4 - 1))
    mixed = jax.random.permutation(jax.random.fold_in(own, 3), count)
    source_of, sink = mixed[0:count // 2 * 2:2], mixed[1:count // 2 * 2:2]
    slack = jnp.minimum(sizes[source_of] - 1, bound - sizes[sink]) // 2
    slack = jnp.where((source_of == ranking[0]) | (sink == ranking[0]) | (sizes[sink] == 0), 0, jnp.maximum(slack, 0))
    passed = jax.random.randint(jax.random.fold_in(own, 4), (count // 2,), 0, 1 << 20) % (slack + 1)
    sizes = sizes.at[source_of].add(-passed).at[sink].add(passed)
    items = jnp.searchsorted(jnp.cumsum(sizes), jnp.arange(rows * top), side="right").astype(jnp.int32)
    listing = items.reshape(top, rows).T
    listing = listing[jax.random.permutation(jax.random.fold_in(own, 1), rows)]
    offset_by = jax.random.randint(jax.random.fold_in(own, 2), (rows, 1), 0, top)
    return jnp.take_along_axis(listing, (jnp.arange(top)[None, :] + offset_by) % top, axis=1)


def portions_of(number_of, total, bound, lean, full):
    weights = [(1 << 20) // math.isqrt(rank ** lean) + 1 for rank in range(1, number_of + 1)]
    largest = bound if full else min(bound, max(-(-total // number_of), total * weights[0] // sum(weights)))
    least = 1 if total - largest >= number_of - 1 else 0
    holding, rest = [largest] + [least] * (number_of - 1), total - largest - least * (number_of - 1)
    while rest > 0:
        movable = [i for i in range(1, number_of) if holding[i] < largest] or [i for i in range(1, number_of) if holding[i] < bound]
        mass, remaining = sum([weights[i] for i in movable]), rest
        for i in movable:
            more = min(bound - holding[i], max(1, remaining * weights[i] // mass), rest)
            holding[i] = holding[i] + more
            rest = rest - more
    return np.array(holding)


def scatter_about(rng, dims, spread, most, cuts=(), kind=jnp.bfloat16):
    level = levels(rng, dims, cuts, -0.22, 0.18) if cuts else 1.0
    array = jax.random.normal(rng, dims, jnp.float32) * spread * level
    return jnp.minimum(jnp.maximum(array, -most), most).astype(kind)


def setup_inputs(seed: int = 0, part: int = 0) -> dict:
    key_of = jax.random.split(jax.random.key(seed), 10)
    own_keys = jax.random.split(jax.random.fold_in(key_of[9], part), 10)
    candidates = draw_candidates(jax.random.fold_in(jax.random.fold_in(key_of[9], part), 71), part)
    input_gain = jnp.clip(1.0 + 0.1 * jax.random.normal(key_of[1], (D,), jnp.float32), 0.5, 1.5).astype(jnp.bfloat16)
    w_in = scatter_about(key_of[2], (D, 4, D), D ** -0.5, 0.1875, ((2, 2),))
    w_out = scatter_about(key_of[3], (D, D), D ** -0.5, 0.1875, ((0, 2),))
    hist_keys = scatter_about(own_keys[4], (SESSIONS, HIST, D), 1.0, 6.0, ((0, 8), (2, 2)))
    hist_values = scatter_about(own_keys[5], (SESSIONS, HIST, D), 0.1, 0.59765625, ((0, 8), (2, 2)))
    request_session_keys = jax.random.split(jax.random.fold_in(own_keys[6], 1), REQUESTS // REQ_DEV)
    request_session_turns = jax.random.permutation(jax.random.fold_in(own_keys[6], 3), REQUESTS // REQ_DEV)
    request_session = jax.vmap(lambda own, number: assign_block(jax.random.fold_in(own_keys[6], 2), own, number, REQ_DEV, SESSIONS, 1, CAP, 2))(request_session_keys, request_session_turns).reshape((REQUESTS, 1))
    hist_len = draw_hist_len(jax.random.fold_in(jax.random.fold_in(key_of[9], part), 71), part)
    block_mask = touch_ends((jax.random.randint(own_keys[8], (REQUESTS, HIST // BLK), 0, 4) < 3).astype(jnp.int32), jax.random.fold_in(own_keys[8], 1), 0, 1)
    return dict(candidates=candidates, input_gain=input_gain, w_in=w_in, w_out=w_out, hist_keys=hist_keys, hist_values=hist_values, request_session=request_session, hist_len=hist_len, block_mask=block_mask)


def reference(candidates, input_gain, w_in, w_out, hist_keys, hist_values, request_session, hist_len, block_mask):
    own_rows = candidates.astype(jnp.float32)
    mean_square = lax.optimization_barrier(jnp.mean(own_rows * own_rows, axis=-1, keepdims=True))
    normed = (own_rows * lax.rsqrt(mean_square + 1e-06) * input_gain.astype(jnp.float32)).astype(jnp.bfloat16)
    projected = jnp.dot(normed.reshape(REQUESTS * CAND, D), w_in.reshape(D, 4 * D), preferred_element_type=jnp.float32)
    activated = jax.nn.silu(projected).astype(jnp.bfloat16).reshape(REQUESTS, CAND, 4, HEADS, HD)
    queries = activated[:, :, 0]
    keys_self = activated[:, :, 1]
    values_self = activated[:, :, 2]
    gate_values = activated[:, :, 3]
    score_scale = HD ** (-0.5)

    def per_request(inputs):
        query_rows, session, mask_row = inputs
        length = lax.dynamic_index_in_dim(hist_len, session, 0, keepdims=False)
        key_rows = lax.dynamic_index_in_dim(hist_keys, session, 0, keepdims=False).reshape(HIST, HEADS, HD)
        value_rows = lax.dynamic_index_in_dim(hist_values, session, 0, keepdims=False).reshape(HIST, HEADS, HD)
        positions = jnp.arange(HIST, dtype=jnp.int32)
        visible = (positions < length) & (jnp.repeat(mask_row, BLK) == 1)
        scores = jnp.einsum('chd,khd->hck', query_rows.astype(jnp.float32), key_rows.astype(jnp.float32)) * score_scale
        weights = jnp.where(visible[None, None, :], jax.nn.silu(scores), 0.0).astype(jnp.bfloat16)
        return jnp.einsum('hck,khd->chd', weights.astype(jnp.float32), value_rows.astype(jnp.float32))
    attended = lax.map(per_request, (queries, request_session[:, 0], block_mask))
    self_score = lax.optimization_barrier(jnp.sum(queries.astype(jnp.float32) * keys_self.astype(jnp.float32), axis=-1, keepdims=True)) * score_scale
    attended = attended + jax.nn.silu(self_score) * values_self.astype(jnp.float32)
    level = lax.rsqrt(lax.optimization_barrier(jnp.mean(attended * attended, axis=-1, keepdims=True)) + 1e-06)
    mixed = (attended * level * gate_values.astype(jnp.float32)).astype(jnp.bfloat16).reshape(REQUESTS * CAND, D)
    result = jnp.dot(mixed, w_out, preferred_element_type=jnp.float32).reshape(REQUESTS, CAND, D)
    return (result + own_rows).astype(jnp.bfloat16)
```

```python
import functools

import jax
import jax.numpy as jnp
from jax import lax
from jax.experimental import pallas as pl
from jax.experimental.pallas import tpu as pltpu
from jax.sharding import PartitionSpec as P

HD = 128
BLK = 64
CAP = 2
EPS = 1e-06
SCALE = HD ** (-0.5)
HIDE = -1e30
VMEM_LIMIT = 48 * 1024 * 1024

vmem = pl.BlockSpec(memory_space=pltpu.VMEM)
smem = pl.BlockSpec(memory_space=pltpu.SMEM)


def silu(x):
    half = x * 0.5
    return half + half * jnp.tanh(half)


def kernel_call(body, out_shape, in_specs, scratch_shapes=(), flops=0, moved=0):
    return pl.pallas_call(
        body,
        out_shape=out_shape,
        in_specs=in_specs,
        out_specs=jax.tree.map(lambda _: vmem, out_shape),
        scratch_shapes=scratch_shapes,
        cost_estimate=pl.CostEstimate(flops=flops, bytes_accessed=moved, transcendentals=0),
        compiler_params=pltpu.CompilerParams(vmem_limit_bytes=VMEM_LIMIT),
    )


def normed_rows(rows_ref, gain):
    rows = rows_ref[...].astype(jnp.float32)
    count, cands, width = rows.shape
    rows = rows.reshape(count * cands, width)
    mean_square = jnp.mean(rows * rows, axis=-1, keepdims=True)
    return (rows * lax.rsqrt(mean_square + EPS) * gain).astype(jnp.bfloat16)


def own_slots(sess_ref, req_count):
    base = lax.axis_index("cache") * req_count
    sessions = [sess_ref[base + request] for request in range(req_count)]
    slots = []
    for request in range(req_count):
        place = 0
        for earlier in range(request):
            place = place + (sessions[earlier] == sessions[request]).astype(jnp.int32)
        slots.append((sessions[request], place))
    return slots


def query_kernel(sess_ref, own_ref, other_ref, gain_ref, wq_ref, slots_ref, queries_ref, normed_ref):
    req_count, half_cands, _ = own_ref.shape
    rows = req_count * half_cands
    gain = gain_ref[...].astype(jnp.float32)
    normed_ref[:rows, :] = normed_rows(own_ref, gain)
    normed_ref[rows:, :] = normed_rows(other_ref, gain)
    slots_ref[...] = jnp.zeros_like(slots_ref)
    queries = silu(jnp.dot(normed_ref[...], wq_ref[...], preferred_element_type=jnp.float32))
    queries_ref[...] = queries.astype(jnp.bfloat16)
    slots = own_slots(sess_ref, req_count)
    for request in range(req_count):
        session, place = slots[request]
        low = request * half_cands
        slot = jnp.concatenate([queries[low : low + half_cands], queries[rows + low : rows + low + half_cands]], axis=0)
        slots_ref[session * CAP + place] = slot.astype(jnp.bfloat16)


def self_kernel(
    sess_ref, len_ref, mask_ref, normed_ref, queries_ref, wkvu_ref,
    keep_ref, send_ref, hide_rows_ref, hide_cols_ref, seen_ref, marks_ref,
):
    rows2, width = queries_ref.shape
    rows = rows2 // 2
    normed = normed_ref[...]
    me = lax.axis_index("cache")
    keys = silu(jnp.dot(normed, wkvu_ref[0], preferred_element_type=jnp.float32)).astype(jnp.bfloat16)
    products = queries_ref[...].astype(jnp.float32) * keys.astype(jnp.float32)
    values = silu(jnp.dot(normed, wkvu_ref[1], preferred_element_type=jnp.float32)).astype(jnp.bfloat16)
    gates = silu(jnp.dot(normed, wkvu_ref[2], preferred_element_type=jnp.float32)).astype(jnp.bfloat16)
    for low in range(0, width, HD):
        score = jnp.sum(products[:, low : low + HD], axis=-1, keepdims=True) * SCALE
        own_term = (silu(score) * values[:, low : low + HD].astype(jnp.float32)).astype(jnp.bfloat16)
        keep_ref[0, :, low : low + HD] = own_term[:rows]
        send_ref[0, :, low : low + HD] = own_term[rows:]
    keep_ref[1] = gates[:rows]
    send_ref[1] = gates[rows:]

    owners = seen_ref.shape[0]
    requests, blocks = mask_ref.shape
    per_owner = requests // owners
    marks_ref[...] = jnp.zeros_like(marks_ref)
    lane = lax.broadcasted_iota(jnp.int32, (1, HD), 1)
    for owner in range(owners):
        seen_ref[owner] = 0

    def one_request(request, carry):
        owner = request // per_owner

        @pl.when(sess_ref[request] == me)
        def _():
            place = seen_ref[owner]
            seen_ref[owner] = place + 1
            marks_ref[pl.ds(owner * CAP + place, 1), :blocks] = mask_ref[pl.ds(request, 1), :]

        return carry

    lax.fori_loop(0, requests, one_request, 0)
    hidden = jnp.where(lane == blocks, 1.0, jnp.where(lane < blocks, 1.0 - marks_ref[...].astype(jnp.float32), 0.0))
    slots = owners * CAP
    per_slot = hide_rows_ref.shape[0] // slots
    hide_rows_ref[...] = (
        jnp.broadcast_to((hidden * HIDE)[:, None, :], (slots, per_slot, HD)).reshape(slots * per_slot, HD)
    ).astype(jnp.bfloat16)
    hist_rows = hide_cols_ref.shape[0]
    at_row = lax.broadcasted_iota(jnp.int32, (hist_rows, HD), 0)
    at_lane = lax.broadcasted_iota(jnp.int32, (hist_rows, HD), 1)
    length = len_ref[me]
    hide_cols_ref[...] = jnp.where(
        (at_lane == at_row // BLK) | ((at_lane == blocks) & (at_row >= length)), 1.0, 0.0
    ).astype(jnp.bfloat16)


def history_kernel(slots_ref, hide_rows_ref, hide_cols_ref, keys_ref, values_ref, out_ref):
    owners, rows_per_owner, width = slots_ref.shape
    hist_rows = keys_ref.shape[0]
    serve = lax.axis_index("serve")
    span = min(256, hist_rows)
    per_step = max(1, min(owners, 256 // rows_per_owner))
    rows = per_step * rows_per_owner
    half = rows_per_owner // CAP // 2

    def one_step(step):
        first = step * per_step
        queries = slots_ref[pl.ds(first, per_step)].reshape(rows, width)
        hide_rows = hide_rows_ref[pl.ds(pl.multiple_of(step * rows, rows), rows), :]
        for low in range(0, width, HD):
            lhs = jnp.concatenate([queries[:, low : low + HD], hide_rows], axis=1)
            total = None
            for start in range(0, hist_rows, span):
                rhs = jnp.concatenate(
                    [keys_ref[start : start + span, low : low + HD], hide_cols_ref[start : start + span, :]], axis=1
                )
                scores = lax.dot_general(lhs, rhs, (((1,), (1,)), ((), ())), preferred_element_type=jnp.float32)
                weights = silu(scores * SCALE).astype(jnp.bfloat16)
                term = jnp.dot(
                    weights, values_ref[start : start + span, low : low + HD], preferred_element_type=jnp.float32
                )
                total = term if total is None else total + term
            parts = total.reshape(per_step, CAP, 2, half, HD)
            for owner in range(per_step):
                own = parts[owner, :, 0].reshape(CAP * half, HD)
                other = parts[owner, :, 1].reshape(CAP * half, HD)
                out_ref[first + owner, 0, :, low : low + HD] = jnp.where(serve == 0, own, other).astype(jnp.bfloat16)
                out_ref[first + owner, 1, :, low : low + HD] = jnp.where(serve == 0, other, own).astype(jnp.bfloat16)

    if owners == per_step:
        one_step(0)
    else:
        pl.loop(0, owners // per_step)(one_step)


def output_kernel(sess_ref, own_ref, returned_ref, keep_ref, got_ref, w_own_ref, w_other_ref, out_ref):
    req_count, half_cands, model_width = own_ref.shape
    width = keep_ref.shape[2]
    slots = own_slots(sess_ref, req_count)
    serve = lax.axis_index("serve")
    picked = ([], [])
    for request in range(req_count):
        session, place = slots[request]
        halves = [returned_ref[session, side].astype(jnp.float32) for side in range(2)]
        for side in range(2):
            both = jnp.where(serve == side, halves[0], halves[1])
            rows = both[:half_cands]
            for at in range(1, CAP):
                rows = jnp.where(place == at, both[at * half_cands : (at + 1) * half_cands], rows)
            picked[side].append(rows)
    total = own_ref[...].astype(jnp.float32).reshape(req_count * half_cands, model_width)
    for side, (extra_ref, w_ref) in enumerate(((keep_ref, w_own_ref), (got_ref, w_other_ref))):
        attended = jnp.concatenate(picked[side], axis=0) + extra_ref[0].astype(jnp.float32)
        gates = extra_ref[1].astype(jnp.float32)
        mixed = []
        for low in range(0, width, HD):
            head = attended[:, low : low + HD]
            level = lax.rsqrt(jnp.mean(head * head, axis=-1, keepdims=True) + EPS)
            mixed.append((head * level * gates[:, low : low + HD]).astype(jnp.bfloat16))
        total = total + jnp.dot(jnp.concatenate(mixed, axis=1), w_ref[...], preferred_element_type=jnp.float32)
    out_ref[...] = total.reshape(req_count, half_cands, model_width).astype(jnp.bfloat16)


def body(candidates, input_gain, w_in, w_out, hist_keys, hist_values, request_session, hist_len, block_mask):
    owners = lax.axis_size("cache")
    req_count, half_cands, model_width = candidates.shape
    width = w_in.shape[2]
    cand_count = 2 * half_cands
    rows = req_count * half_cands
    hist_rows = hist_keys.shape[1]
    swap = [(0, 1), (1, 0)]
    bf16 = functools.partial(jax.ShapeDtypeStruct, dtype=jnp.bfloat16)
    sessions = request_session.reshape(-1)

    other = lax.ppermute(candidates, "serve", swap)
    slots, queries, normed = kernel_call(
        query_kernel,
        (bf16((owners * CAP, cand_count, width)), bf16((2 * rows, width)), bf16((2 * rows, model_width))),
        [smem, vmem, vmem, vmem, vmem],
        flops=4 * rows * model_width * width,
        moved=2 * model_width * width,
    )(sessions, candidates, other, input_gain.reshape(1, -1), w_in[:, 0, :])
    sent = lax.all_to_all(
        slots.reshape(owners, CAP * cand_count, width), "cache", split_axis=0, concat_axis=0, tiled=True
    )
    slot_rows = owners * CAP * cand_count
    keep, send, hide_rows, hide_cols = kernel_call(
        self_kernel,
        (bf16((2, rows, width)), bf16((2, rows, width)), bf16((slot_rows, HD)), bf16((hist_rows, HD))),
        [smem, smem, vmem, vmem, vmem, vmem],
        [pltpu.SMEM((owners,), jnp.int32), pltpu.VMEM((owners * CAP, HD), jnp.int32)],
        flops=12 * rows * model_width * width,
        moved=6 * model_width * width,
    )(sessions, hist_len, block_mask, normed, queries, jnp.transpose(w_in[:, 1:, :], (1, 0, 2)))
    got = lax.ppermute(send, "serve", swap)
    w_other = lax.ppermute(w_out, "serve", swap)
    attended = kernel_call(
        history_kernel,
        bf16((owners, 2, CAP * half_cands, width)),
        [vmem] * 5,
        flops=8 * slot_rows * hist_rows * width,
        moved=4 * hist_rows * width,
    )(sent, hide_rows, hide_cols, hist_keys.reshape(hist_rows, width), hist_values.reshape(hist_rows, width))
    returned = lax.all_to_all(
        attended.reshape(owners * 2, CAP * half_cands, width), ("cache", "serve"), split_axis=0, concat_axis=0, tiled=True
    ).reshape(owners, 2, CAP * half_cands, width)
    return kernel_call(
        output_kernel,
        bf16((req_count, half_cands, model_width)),
        [smem] + [vmem] * 6,
        flops=8 * rows * model_width * width,
        moved=4 * model_width * width,
    )(sessions, candidates, returned, keep, got, w_out, w_other)


def solution(mesh):
    placed = (
        P(("groups", "cache"), "serve", None),
        P(),
        P(None, None, "serve"),
        P("serve", None),
        P(("groups", "cache"), None, "serve"),
        P(("groups", "cache"), None, "serve"),
        P("groups", None),
        P("groups"),
        P("groups", None),
    )
    return jax.shard_map(
        body,
        mesh=mesh,
        in_specs=placed,
        out_specs=P(("groups", "cache"), "serve", None),
        check_vma=False,
    )
```

```python
import functools

import jax
import jax.numpy as jnp
from jax import lax
from jax.experimental import pallas as pl
from jax.experimental.pallas import tpu as pltpu
from jax.sharding import PartitionSpec as P

HD = 128
BLK = 64
CAP = 2
EPS = 1e-06
SCALE = HD ** (-0.5)
HIDE = -1e30
VMEM_LIMIT = 16 * 1024 * 1024

vmem = pl.BlockSpec(memory_space=pltpu.VMEM)
smem = pl.BlockSpec(memory_space=pltpu.SMEM)


def silu(x):
    half = x * 0.5
    return half + half * jnp.tanh(half)


def kernel_call(body, out_shape, in_specs, scratch_shapes=(), flops=0, moved=0):
    return pl.pallas_call(
        body,
        out_shape=out_shape,
        in_specs=in_specs,
        out_specs=jax.tree.map(lambda _: vmem, out_shape),
        scratch_shapes=scratch_shapes,
        cost_estimate=pl.CostEstimate(flops=flops, bytes_accessed=moved, transcendentals=0),
        compiler_params=pltpu.CompilerParams(vmem_limit_bytes=VMEM_LIMIT),
    )


def normed_rows(rows_ref, gain):
    rows = rows_ref[...].astype(jnp.float32)
    count, cands, width = rows.shape
    rows = rows.reshape(count * cands, width)
    mean_square = jnp.mean(rows * rows, axis=-1, keepdims=True)
    return (rows * lax.rsqrt(mean_square + EPS) * gain).astype(jnp.bfloat16)


def own_slots(sess_ref, req_count):
    me = lax.axis_index("cache")
    base = me * req_count
    sessions = [sess_ref[base + request] for request in range(req_count)]
    slots = []
    for request in range(req_count):
        place = 0
        for earlier in range(request):
            place = place + (sessions[earlier] == sessions[request]).astype(jnp.int32)
        slots.append((sessions[request] ^ me) * CAP + place)
    return slots


def query_kernel(sess_ref, own_ref, other_ref, gain_ref, w_ref, *refs):
    *slot_refs, queries_ref, normed_ref, table_ref = refs
    req_count, half_cands, _ = own_ref.shape
    rows = req_count * half_cands
    gain = gain_ref[...].astype(jnp.float32)
    normed_ref[:rows, :] = normed_rows(own_ref, gain)
    normed_ref[rows:, :] = normed_rows(other_ref, gain)
    table_ref[...] = jnp.zeros_like(table_ref)
    queries = silu(jnp.dot(normed_ref[...], w_ref[0], preferred_element_type=jnp.float32))
    queries_ref[...] = queries.astype(jnp.bfloat16)
    for request, slot in enumerate(own_slots(sess_ref, req_count)):
        low = request * half_cands
        both = jnp.concatenate([queries[low : low + half_cands], queries[rows + low : rows + low + half_cands]], axis=0)
        table_ref[slot] = both.astype(jnp.bfloat16)
    for distance, slot_ref in enumerate(slot_refs):
        slot_ref[...] = table_ref[distance * CAP : (distance + 1) * CAP].reshape(slot_ref.shape)


def self_kernel(sess_ref, len_ref, mask_ref, normed_ref, queries_ref, w_ref, own_ref, gates_ref, hide_rows_ref, hide_cols_ref, marks_ref):
    width = queries_ref.shape[1]
    normed = normed_ref[...]
    me = lax.axis_index("cache")
    keys = silu(jnp.dot(normed, w_ref[1], preferred_element_type=jnp.float32)).astype(jnp.bfloat16)
    products = queries_ref[...].astype(jnp.float32) * keys.astype(jnp.float32)
    values = silu(jnp.dot(normed, w_ref[2], preferred_element_type=jnp.float32)).astype(jnp.bfloat16)
    gates_ref[...] = silu(jnp.dot(normed, w_ref[3], preferred_element_type=jnp.float32)).astype(jnp.bfloat16)
    for low in range(0, width, HD):
        score = jnp.sum(products[:, low : low + HD], axis=-1, keepdims=True) * SCALE
        own_ref[:, low : low + HD] = silu(score) * values[:, low : low + HD].astype(jnp.float32)

    blocks, requests = mask_ref.shape
    owners = len_ref.shape[0]
    per_owner = requests // owners
    sessions = sess_ref[...]
    lane = lax.broadcasted_iota(jnp.int32, (1, requests), 1)
    place = jnp.zeros((1, requests), jnp.int32)
    for back in range(1, per_owner):
        same = (pltpu.roll(sessions, back, 1) == sessions) & (lane % per_owner >= back)
        place = place + same.astype(jnp.int32)
    slot_of = jnp.where(sessions == me, ((lane // per_owner) ^ me) * CAP + place, -1)
    slots = owners * CAP
    at_slot = lax.broadcasted_iota(jnp.int32, (slots, requests), 0)
    chosen = (at_slot == slot_of).astype(jnp.float32).astype(jnp.bfloat16)
    marks_ref[...] = jnp.zeros_like(marks_ref)
    marks_ref[:blocks, :] = mask_ref[...].astype(jnp.float32).astype(jnp.bfloat16)
    seen = lax.dot_general(chosen, marks_ref[...], (((1,), (1,)), ((), ())), preferred_element_type=jnp.float32)
    at_lane = lax.broadcasted_iota(jnp.int32, (slots, HD), 1)
    hidden = jnp.where(at_lane < blocks, (1.0 - seen) * HIDE, jnp.where(at_lane == blocks, HIDE, 0.0))
    per_slot = hide_rows_ref.shape[0] // slots
    hide_rows_ref[...] = (
        jnp.broadcast_to(hidden[:, None, :], (slots, per_slot, HD)).reshape(slots * per_slot, HD).astype(jnp.bfloat16)
    )
    hist_rows = hide_cols_ref.shape[0]
    at_row = lax.broadcasted_iota(jnp.int32, (hist_rows, HD), 0)
    at_lane = lax.broadcasted_iota(jnp.int32, (hist_rows, HD), 1)
    hide_cols_ref[...] = jnp.where(
        (at_lane == at_row // BLK) | ((at_lane == blocks) & (at_row >= len_ref[me])), 1.0, 0.0
    ).astype(jnp.bfloat16)


def history_kernel(owners, hide_rows_ref, hide_cols_ref, keys_ref, values_ref, *refs):
    slot_refs, out_refs = refs[:owners], refs[owners:]
    per_owner, width = slot_refs[0].shape
    hist_rows = keys_ref.shape[0]
    span = min(256, hist_rows)
    per_step = max(1, min(owners, 256 // per_owner))
    for first in range(0, owners, per_step):
        group = range(first, min(first + per_step, owners))
        queries = jnp.concatenate([slot_refs[at][...] for at in group], axis=0)
        hide_rows = hide_rows_ref[first * per_owner : first * per_owner + queries.shape[0], :]
        for low in range(0, width, HD):
            lhs = jnp.concatenate([queries[:, low : low + HD], hide_rows], axis=1)
            total = None
            for start in range(0, hist_rows, span):
                rhs = jnp.concatenate(
                    [keys_ref[start : start + span, low : low + HD], hide_cols_ref[start : start + span, :]], axis=1
                )
                scores = lax.dot_general(lhs, rhs, (((1,), (1,)), ((), ())), preferred_element_type=jnp.float32)
                weights = silu(scores * SCALE).astype(jnp.bfloat16)
                term = jnp.dot(
                    weights, values_ref[start : start + span, low : low + HD], preferred_element_type=jnp.float32
                )
                total = term if total is None else total + term
            total = total.astype(jnp.bfloat16)
            for place, at in enumerate(group):
                out_refs[at][:, low : low + HD] = total[place * per_owner : (place + 1) * per_owner]


def mix_kernel(owners, req_count, sess_ref, own_ref, gates_ref, *refs):
    back_refs, (keep_ref, send_ref, table_ref) = refs[:owners], refs[owners:]
    rows, width = keep_ref.shape
    half_cands = rows // req_count
    for distance, back_ref in enumerate(back_refs):
        table_ref[distance * CAP : (distance + 1) * CAP] = back_ref[...].reshape((CAP,) + table_ref.shape[1:])
    picked = [table_ref[slot].astype(jnp.float32) for slot in own_slots(sess_ref, req_count)]
    for side, out_ref in enumerate((keep_ref, send_ref)):
        history = jnp.concatenate([both[side * half_cands : (side + 1) * half_cands] for both in picked], axis=0)
        attended = history + own_ref[side * rows : (side + 1) * rows, :]
        gates = gates_ref[side * rows : (side + 1) * rows, :].astype(jnp.float32)
        for low in range(0, width, HD):
            head = attended[:, low : low + HD]
            level = lax.rsqrt(jnp.mean(head * head, axis=-1, keepdims=True) + EPS)
            out_ref[:, low : low + HD] = (head * level * gates[:, low : low + HD]).astype(jnp.bfloat16)


def output_kernel(own_ref, keep_ref, got_ref, w_own_ref, w_other_ref, out_ref):
    req_count, half_cands, model_width = own_ref.shape
    total = own_ref[...].astype(jnp.float32).reshape(req_count * half_cands, model_width)
    total = total + jnp.dot(keep_ref[...], w_own_ref[...], preferred_element_type=jnp.float32)
    total = total + jnp.dot(got_ref[...], w_other_ref[...], preferred_element_type=jnp.float32)
    out_ref[...] = total.reshape(req_count, half_cands, model_width).astype(jnp.bfloat16)


def exchange(pieces):
    count = len(pieces)
    return [pieces[0]] + [
        lax.ppermute(pieces[distance], "cache", [(place, place ^ distance) for place in range(count)])
        for distance in range(1, count)
    ]


def body(candidates, input_gain, w_in, w_out, hist_keys, hist_values, request_session, hist_len, block_mask):
    owners = lax.axis_size("cache")
    req_count, half_cands, model_width = candidates.shape
    width = w_in.shape[2]
    cand_count = 2 * half_cands
    rows = req_count * half_cands
    hist_rows = hist_keys.shape[1]
    blocks = block_mask.shape[1]
    swap = [(0, 1), (1, 0)]
    bf16 = functools.partial(jax.ShapeDtypeStruct, dtype=jnp.bfloat16)
    sessions = request_session.reshape(-1)
    piece = bf16((CAP * cand_count, width))
    table = pltpu.VMEM((owners * CAP, cand_count, width), jnp.bfloat16)

    other = lax.ppermute(candidates, "serve", swap)
    weights = jnp.transpose(w_in, (1, 0, 2))
    *pieces, queries, normed = kernel_call(
        query_kernel,
        [piece] * owners + [bf16((2 * rows, width)), bf16((2 * rows, model_width))],
        [smem, vmem, vmem, vmem, vmem],
        [table],
        flops=4 * rows * model_width * width,
        moved=2 * model_width * width,
    )(sessions, candidates, other, input_gain.reshape(1, -1), weights)
    slots = exchange(pieces)
    slot_rows = owners * CAP * cand_count
    own_term, gates, hide_rows, hide_cols = kernel_call(
        self_kernel,
        [
            jax.ShapeDtypeStruct((2 * rows, width), jnp.float32),
            bf16((2 * rows, width)),
            bf16((slot_rows, HD)),
            bf16((hist_rows, HD)),
        ],
        [vmem, smem, vmem, vmem, vmem, vmem],
        [pltpu.VMEM((HD, owners * req_count), jnp.bfloat16)],
        flops=12 * rows * model_width * width,
        moved=6 * model_width * width,
    )(request_session.reshape(1, -1), hist_len, block_mask.T, normed, queries, weights)
    w_other = lax.ppermute(w_out, "serve", swap)
    backs = exchange(
        kernel_call(
            functools.partial(history_kernel, owners),
            [piece] * owners,
            [vmem] * (4 + owners),
            flops=8 * slot_rows * hist_rows * width,
            moved=4 * hist_rows * width,
        )(hide_rows, hide_cols, hist_keys.reshape(hist_rows, width), hist_values.reshape(hist_rows, width), *slots)
    )
    keep, send = kernel_call(
        functools.partial(mix_kernel, owners, req_count),
        [bf16((rows, width))] * 2,
        [smem] + [vmem] * (2 + owners),
        [table],
    )(sessions, own_term, gates, *backs)
    got = lax.ppermute(send, "serve", swap)
    return kernel_call(
        output_kernel,
        bf16((req_count, half_cands, model_width)),
        [vmem] * 5,
        flops=8 * rows * model_width * width,
        moved=4 * model_width * width,
    )(candidates, keep, got, w_out, w_other)


def solution(mesh):
    placed = (
        P(("groups", "cache"), "serve", None),
        P(),
        P(None, None, "serve"),
        P("serve", None),
        P(("groups", "cache"), None, "serve"),
        P(("groups", "cache"), None, "serve"),
        P("groups", None),
        P("groups"),
        P("groups", None),
    )
    return jax.shard_map(
        body,
        mesh=mesh,
        in_specs=placed,
        out_specs=P(("groups", "cache"), "serve", None),
        check_vma=False,
    )
```

```python
import functools

import jax
import jax.numpy as jnp
from jax import lax
from jax.experimental import pallas as pl
from jax.experimental.pallas import tpu as pltpu
from jax.sharding import PartitionSpec as P

HD = 128
BLK = 64
CAP = 2
EPS = 1e-06
SCALE = HD ** (-0.5)
HIDE = -1e30
VMEM_LIMIT = 16 * 1024 * 1024

vmem = pl.BlockSpec(memory_space=pltpu.VMEM)
smem = pl.BlockSpec(memory_space=pltpu.SMEM)


def silu(x):
    half = x * 0.5
    return half + half * jnp.tanh(half)


def kernel_call(body, out_shape, in_specs, scratch_shapes=(), flops=0, moved=0):
    return pl.pallas_call(
        body,
        out_shape=out_shape,
        in_specs=in_specs,
        out_specs=jax.tree.map(lambda _: vmem, out_shape),
        scratch_shapes=scratch_shapes,
        cost_estimate=pl.CostEstimate(flops=flops, bytes_accessed=moved, transcendentals=0),
        compiler_params=pltpu.CompilerParams(vmem_limit_bytes=VMEM_LIMIT),
    )


def normed_rows(rows_ref, gain):
    rows = rows_ref[...].astype(jnp.float32)
    count, cands, width = rows.shape
    rows = rows.reshape(count * cands, width)
    mean_square = jnp.mean(rows * rows, axis=-1, keepdims=True)
    return (rows * lax.rsqrt(mean_square + EPS) * gain).astype(jnp.bfloat16)


def own_slots(sess_ref, req_count):
    base = lax.axis_index("cache") * req_count
    sessions = [sess_ref[base + request] for request in range(req_count)]
    slots = []
    for request in range(req_count):
        place = 0
        for earlier in range(request):
            place = place + (sessions[earlier] == sessions[request]).astype(jnp.int32)
        slots.append(sessions[request] * CAP + place)
    return slots


def query_kernel(sess_ref, own_ref, other_ref, gain_ref, w_ref, table_ref, queries_ref, normed_ref):
    req_count, half_cands, _ = own_ref.shape
    rows = req_count * half_cands
    gain = gain_ref[...].astype(jnp.float32)
    normed_ref[:rows, :] = normed_rows(own_ref, gain)
    normed_ref[rows:, :] = normed_rows(other_ref, gain)
    table_ref[...] = jnp.zeros_like(table_ref)
    queries = silu(jnp.dot(normed_ref[...], w_ref[:, 0, :], preferred_element_type=jnp.float32))
    queries_ref[...] = queries.astype(jnp.bfloat16)
    for request, slot in enumerate(own_slots(sess_ref, req_count)):
        low = request * half_cands
        both = jnp.concatenate([queries[low : low + half_cands], queries[rows + low : rows + low + half_cands]], axis=0)
        table_ref[slot] = both.astype(jnp.bfloat16)


def self_kernel(sess_ref, len_ref, mask_ref, normed_ref, queries_ref, w_ref, own_ref, gates_ref, hide_rows_ref, hide_cols_ref, marks_ref):
    width = queries_ref.shape[1]
    normed = normed_ref[...]
    me = lax.axis_index("cache")
    keys = silu(jnp.dot(normed, w_ref[:, 1, :], preferred_element_type=jnp.float32)).astype(jnp.bfloat16)
    products = queries_ref[...].astype(jnp.float32) * keys.astype(jnp.float32)
    values = silu(jnp.dot(normed, w_ref[:, 2, :], preferred_element_type=jnp.float32)).astype(jnp.bfloat16)
    gates_ref[...] = silu(jnp.dot(normed, w_ref[:, 3, :], preferred_element_type=jnp.float32)).astype(jnp.bfloat16)
    for low in range(0, width, HD):
        score = jnp.sum(products[:, low : low + HD], axis=-1, keepdims=True) * SCALE
        own_ref[:, low : low + HD] = silu(score) * values[:, low : low + HD].astype(jnp.float32)

    blocks, requests = mask_ref.shape
    owners = len_ref.shape[0]
    per_owner = requests // owners
    sessions = sess_ref[...]
    lane = lax.broadcasted_iota(jnp.int32, (1, requests), 1)
    place = jnp.zeros((1, requests), jnp.int32)
    for back in range(1, per_owner):
        same = (pltpu.roll(sessions, back, 1) == sessions) & (lane % per_owner >= back)
        place = place + same.astype(jnp.int32)
    slot_of = jnp.where(sessions == me, (lane // per_owner) * CAP + place, -1)
    slots = owners * CAP
    at_slot = lax.broadcasted_iota(jnp.int32, (slots, requests), 0)
    chosen = (at_slot == slot_of).astype(jnp.float32).astype(jnp.bfloat16)
    marks_ref[...] = jnp.zeros_like(marks_ref)
    marks_ref[:blocks, :] = mask_ref[...].astype(jnp.float32).astype(jnp.bfloat16)
    seen = lax.dot_general(chosen, marks_ref[...], (((1,), (1,)), ((), ())), preferred_element_type=jnp.float32)
    at_lane = lax.broadcasted_iota(jnp.int32, (slots, HD), 1)
    hidden = jnp.where(at_lane < blocks, (1.0 - seen) * HIDE, jnp.where(at_lane == blocks, HIDE, 0.0))
    per_slot = hide_rows_ref.shape[0] // slots
    hide_rows_ref[...] = (
        jnp.broadcast_to(hidden[:, None, :], (slots, per_slot, HD)).reshape(slots * per_slot, HD).astype(jnp.bfloat16)
    )
    hist_rows = hide_cols_ref.shape[0]
    at_row = lax.broadcasted_iota(jnp.int32, (hist_rows, HD), 0)
    at_lane = lax.broadcasted_iota(jnp.int32, (hist_rows, HD), 1)
    hide_cols_ref[...] = jnp.where(
        (at_lane == at_row // BLK) | ((at_lane == blocks) & (at_row >= len_ref[me])), 1.0, 0.0
    ).astype(jnp.bfloat16)


def history_kernel(slots_ref, hide_rows_ref, hide_cols_ref, keys_ref, values_ref, out_ref):
    slot_rows, width = slots_ref.shape
    hist_rows = keys_ref.shape[0]
    span = min(256, hist_rows)
    per_step = min(slot_rows, 256)
    for first in range(0, slot_rows, per_step):
        queries = slots_ref[first : first + per_step, :]
        hide_rows = hide_rows_ref[first : first + per_step, :]
        for low in range(0, width, HD):
            lhs = jnp.concatenate([queries[:, low : low + HD], hide_rows], axis=1)
            total = None
            for start in range(0, hist_rows, span):
                rhs = jnp.concatenate(
                    [keys_ref[start : start + span, low : low + HD], hide_cols_ref[start : start + span, :]], axis=1
                )
                scores = lax.dot_general(lhs, rhs, (((1,), (1,)), ((), ())), preferred_element_type=jnp.float32)
                weights = silu(scores * SCALE).astype(jnp.bfloat16)
                term = jnp.dot(
                    weights, values_ref[start : start + span, low : low + HD], preferred_element_type=jnp.float32
                )
                total = term if total is None else total + term
            out_ref[first : first + per_step, low : low + HD] = total.astype(jnp.bfloat16)


def mix_kernel(req_count, sess_ref, own_ref, gates_ref, table_ref, keep_ref, send_ref):
    rows, width = keep_ref.shape
    half_cands = rows // req_count
    picked = [table_ref[slot].astype(jnp.float32) for slot in own_slots(sess_ref, req_count)]
    for side, out_ref in enumerate((keep_ref, send_ref)):
        history = jnp.concatenate([both[side * half_cands : (side + 1) * half_cands] for both in picked], axis=0)
        attended = history + own_ref[side * rows : (side + 1) * rows, :]
        gates = gates_ref[side * rows : (side + 1) * rows, :].astype(jnp.float32)
        for low in range(0, width, HD):
            head = attended[:, low : low + HD]
            level = lax.rsqrt(jnp.mean(head * head, axis=-1, keepdims=True) + EPS)
            out_ref[:, low : low + HD] = (head * level * gates[:, low : low + HD]).astype(jnp.bfloat16)


def output_kernel(own_ref, keep_ref, got_ref, w_own_ref, w_other_ref, out_ref):
    req_count, half_cands, model_width = own_ref.shape
    total = own_ref[...].astype(jnp.float32).reshape(req_count * half_cands, model_width)
    total = total + jnp.dot(keep_ref[...], w_own_ref[...], preferred_element_type=jnp.float32)
    total = total + jnp.dot(got_ref[...], w_other_ref[...], preferred_element_type=jnp.float32)
    out_ref[...] = total.reshape(req_count, half_cands, model_width).astype(jnp.bfloat16)


def exchange(table, owners):
    rows, width = table.shape
    blocks = table.reshape(owners, rows // owners, width)
    return lax.all_to_all(blocks, "cache", split_axis=0, concat_axis=0, tiled=True).reshape(rows, width)


def body(candidates, input_gain, w_in, w_out, hist_keys, hist_values, request_session, hist_len, block_mask):
    owners = lax.axis_size("cache")
    req_count, half_cands, model_width = candidates.shape
    width = w_in.shape[2]
    cand_count = 2 * half_cands
    rows = req_count * half_cands
    hist_rows = hist_keys.shape[1]
    blocks = block_mask.shape[1]
    swap = [(0, 1), (1, 0)]
    bf16 = functools.partial(jax.ShapeDtypeStruct, dtype=jnp.bfloat16)
    sessions = request_session.reshape(-1)
    slot_rows = owners * CAP * cand_count

    other = lax.ppermute(candidates, "serve", swap)
    table, queries, normed = kernel_call(
        query_kernel,
        [bf16((owners * CAP, cand_count, width)), bf16((2 * rows, width)), bf16((2 * rows, model_width))],
        [smem, vmem, vmem, vmem, vmem],
        flops=4 * rows * model_width * width,
        moved=2 * model_width * width,
    )(sessions, candidates, other, input_gain.reshape(1, -1), w_in)
    slots = exchange(table.reshape(slot_rows, width), owners)
    own_term, gates, hide_rows, hide_cols = kernel_call(
        self_kernel,
        [
            jax.ShapeDtypeStruct((2 * rows, width), jnp.float32),
            bf16((2 * rows, width)),
            bf16((slot_rows, HD)),
            bf16((hist_rows, HD)),
        ],
        [vmem, smem, vmem, vmem, vmem, vmem],
        [pltpu.VMEM((HD, owners * req_count), jnp.bfloat16)],
        flops=12 * rows * model_width * width,
        moved=6 * model_width * width,
    )(request_session.reshape(1, -1), hist_len, block_mask.T, normed, queries, w_in)
    w_other = lax.ppermute(w_out, "serve", swap)
    attended = kernel_call(
        history_kernel,
        bf16((slot_rows, width)),
        [vmem] * 5,
        flops=8 * slot_rows * hist_rows * width,
        moved=4 * hist_rows * width,
    )(slots, hide_rows, hide_cols, hist_keys.reshape(hist_rows, width), hist_values.reshape(hist_rows, width))
    returned = exchange(attended, owners).reshape(owners * CAP, cand_count, width)
    keep, send = kernel_call(
        functools.partial(mix_kernel, req_count),
        [bf16((rows, width))] * 2,
        [smem] + [vmem] * 3,
    )(sessions, own_term, gates, returned)
    got = lax.ppermute(send, "serve", swap)
    return kernel_call(
        output_kernel,
        bf16((req_count, half_cands, model_width)),
        [vmem] * 5,
        flops=8 * rows * model_width * width,
        moved=4 * model_width * width,
    )(candidates, keep, got, w_out, w_other)


def solution(mesh):
    placed = (
        P(("groups", "cache"), "serve", None),
        P(),
        P(None, None, "serve"),
        P("serve", None),
        P(("groups", "cache"), None, "serve"),
        P(("groups", "cache"), None, "serve"),
        P("groups", None),
        P("groups"),
        P("groups", None),
    )
    return jax.shard_map(
        body,
        mesh=mesh,
        in_specs=placed,
        out_specs=P(("groups", "cache"), "serve", None),
        check_vma=False,
    )
```

```python
import functools

import jax
import jax.numpy as jnp
from jax import lax
from jax.experimental import pallas as pl
from jax.experimental.pallas import tpu as pltpu
from jax.sharding import PartitionSpec as P

HD = 128
BLK = 64
CAP = 2
EPS = 1e-06
SCALE = HD ** (-0.5)
HIDE = -1e30
VMEM_LIMIT = 16 * 1024 * 1024

vmem = pl.BlockSpec(memory_space=pltpu.VMEM)
smem = pl.BlockSpec(memory_space=pltpu.SMEM)


def silu(x):
    half = x * 0.5
    return half + half * jnp.tanh(half)


def kernel_call(body, out_shape, in_specs, scratch_shapes=(), flops=0, moved=0):
    return pl.pallas_call(
        body,
        out_shape=out_shape,
        in_specs=in_specs,
        out_specs=jax.tree.map(lambda _: vmem, out_shape),
        scratch_shapes=scratch_shapes,
        cost_estimate=pl.CostEstimate(flops=flops, bytes_accessed=moved, transcendentals=0),
        compiler_params=pltpu.CompilerParams(vmem_limit_bytes=VMEM_LIMIT),
    )


def normed_rows(rows_ref, gain):
    rows = rows_ref[...].astype(jnp.float32)
    count, cands, width = rows.shape
    rows = rows.reshape(count * cands, width)
    mean_square = jnp.mean(rows * rows, axis=-1, keepdims=True)
    return (rows * lax.rsqrt(mean_square + EPS) * gain).astype(jnp.bfloat16)


def own_slots(sess_ref, req_count):
    me = lax.axis_index("cache")
    base = me * req_count
    sessions = [sess_ref[base + request] for request in range(req_count)]
    slots = []
    for request in range(req_count):
        place = 0
        for earlier in range(request):
            place = place + (sessions[earlier] == sessions[request]).astype(jnp.int32)
        slots.append((sessions[request] ^ me) * CAP + place)
    return slots


def query_kernel(sess_ref, own_ref, other_ref, gain_ref, w_ref, *refs):
    *slot_refs, queries_ref, normed_ref, table_ref = refs
    req_count, half_cands, _ = own_ref.shape
    rows = req_count * half_cands
    gain = gain_ref[...].astype(jnp.float32)
    normed_ref[:rows, :] = normed_rows(own_ref, gain)
    normed_ref[rows:, :] = normed_rows(other_ref, gain)
    table_ref[...] = jnp.zeros_like(table_ref)
    queries = silu(jnp.dot(normed_ref[...], w_ref[0], preferred_element_type=jnp.float32))
    queries_ref[...] = queries.astype(jnp.bfloat16)
    for request, slot in enumerate(own_slots(sess_ref, req_count)):
        low = request * half_cands
        both = jnp.concatenate([queries[low : low + half_cands], queries[rows + low : rows + low + half_cands]], axis=0)
        table_ref[slot] = both.astype(jnp.bfloat16)
    at = 0
    for slot_ref in slot_refs:
        slots = slot_ref.shape[0] // table_ref.shape[1]
        slot_ref[...] = table_ref[at : at + slots].reshape(slot_ref.shape)
        at += slots


def self_kernel(sess_ref, len_ref, mask_ref, normed_ref, queries_ref, w_ref, own_ref, gates_ref, hide_rows_ref, hide_cols_ref, marks_ref):
    width = queries_ref.shape[1]
    normed = normed_ref[...]
    me = lax.axis_index("cache")
    keys = silu(jnp.dot(normed, w_ref[1], preferred_element_type=jnp.float32)).astype(jnp.bfloat16)
    products = queries_ref[...].astype(jnp.float32) * keys.astype(jnp.float32)
    values = silu(jnp.dot(normed, w_ref[2], preferred_element_type=jnp.float32)).astype(jnp.bfloat16)
    gates_ref[...] = silu(jnp.dot(normed, w_ref[3], preferred_element_type=jnp.float32)).astype(jnp.bfloat16)
    for low in range(0, width, HD):
        score = jnp.sum(products[:, low : low + HD], axis=-1, keepdims=True) * SCALE
        own_ref[:, low : low + HD] = silu(score) * values[:, low : low + HD].astype(jnp.float32)

    blocks, requests = mask_ref.shape
    owners = len_ref.shape[0]
    per_owner = requests // owners
    sessions = sess_ref[...]
    lane = lax.broadcasted_iota(jnp.int32, (1, requests), 1)
    place = jnp.zeros((1, requests), jnp.int32)
    for back in range(1, per_owner):
        same = (pltpu.roll(sessions, back, 1) == sessions) & (lane % per_owner >= back)
        place = place + same.astype(jnp.int32)
    slot_of = jnp.where(sessions == me, ((lane // per_owner) ^ me) * CAP + place, -1)
    slots = owners * CAP
    at_slot = lax.broadcasted_iota(jnp.int32, (slots, requests), 0)
    chosen = (at_slot == slot_of).astype(jnp.float32).astype(jnp.bfloat16)
    marks_ref[...] = jnp.zeros_like(marks_ref)
    marks_ref[:blocks, :] = mask_ref[...].astype(jnp.float32).astype(jnp.bfloat16)
    seen = lax.dot_general(chosen, marks_ref[...], (((1,), (1,)), ((), ())), preferred_element_type=jnp.float32)
    at_lane = lax.broadcasted_iota(jnp.int32, (slots, HD), 1)
    hidden = jnp.where(at_lane < blocks, (1.0 - seen) * HIDE, jnp.where(at_lane == blocks, HIDE, 0.0))
    per_slot = hide_rows_ref.shape[0] // slots
    hide_rows_ref[...] = (
        jnp.broadcast_to(hidden[:, None, :], (slots, per_slot, HD)).reshape(slots * per_slot, HD).astype(jnp.bfloat16)
    )
    hist_rows = hide_cols_ref.shape[0]
    at_row = lax.broadcasted_iota(jnp.int32, (hist_rows, HD), 0)
    at_lane = lax.broadcasted_iota(jnp.int32, (hist_rows, HD), 1)
    hide_cols_ref[...] = jnp.where(
        (at_lane == at_row // BLK) | ((at_lane == blocks) & (at_row >= len_ref[me])), 1.0, 0.0
    ).astype(jnp.bfloat16)


def history_kernel(owners, hide_rows_ref, hide_cols_ref, keys_ref, values_ref, *refs):
    slot_refs, out_refs = refs[:owners], refs[owners:]
    per_owner, width = slot_refs[0].shape
    hist_rows = keys_ref.shape[0]
    span = min(256, hist_rows)
    per_step = max(1, min(owners, 256 // per_owner))
    places = []
    for out_ref in out_refs:
        places += [(out_ref, low) for low in range(0, out_ref.shape[0], per_owner)]
    for first in range(0, owners, per_step):
        group = range(first, min(first + per_step, owners))
        queries = jnp.concatenate([slot_refs[at][:per_owner, :] for at in group], axis=0)
        hide_rows = hide_rows_ref[first * per_owner : first * per_owner + queries.shape[0], :]
        for low in range(0, width, HD):
            lhs = jnp.concatenate([queries[:, low : low + HD], hide_rows], axis=1)
            total = None
            for start in range(0, hist_rows, span):
                rhs = jnp.concatenate(
                    [keys_ref[start : start + span, low : low + HD], hide_cols_ref[start : start + span, :]], axis=1
                )
                scores = lax.dot_general(lhs, rhs, (((1,), (1,)), ((), ())), preferred_element_type=jnp.float32)
                weights = silu(scores * SCALE).astype(jnp.bfloat16)
                term = jnp.dot(
                    weights, values_ref[start : start + span, low : low + HD], preferred_element_type=jnp.float32
                )
                total = term if total is None else total + term
            total = total.astype(jnp.bfloat16)
            for place, at in enumerate(group):
                out_ref, row = places[at]
                out_ref[row : row + per_owner, low : low + HD] = total[place * per_owner : (place + 1) * per_owner]


def mix_kernel(owners, req_count, sess_ref, own_ref, gates_ref, *refs):
    back_refs, (keep_ref, send_ref, table_ref) = refs[:owners], refs[owners:]
    rows, width = keep_ref.shape
    half_cands = rows // req_count
    for distance, back_ref in enumerate(back_refs):
        rows_here = back_ref[: back_refs[0].shape[0], :]
        table_ref[distance * CAP : (distance + 1) * CAP] = rows_here.reshape((CAP,) + table_ref.shape[1:])
    picked = [table_ref[slot].astype(jnp.float32) for slot in own_slots(sess_ref, req_count)]
    for side, out_ref in enumerate((keep_ref, send_ref)):
        history = jnp.concatenate([both[side * half_cands : (side + 1) * half_cands] for both in picked], axis=0)
        attended = history + own_ref[side * rows : (side + 1) * rows, :]
        gates = gates_ref[side * rows : (side + 1) * rows, :].astype(jnp.float32)
        for low in range(0, width, HD):
            head = attended[:, low : low + HD]
            level = lax.rsqrt(jnp.mean(head * head, axis=-1, keepdims=True) + EPS)
            out_ref[:, low : low + HD] = (head * level * gates[:, low : low + HD]).astype(jnp.bfloat16)


def output_kernel(own_ref, keep_ref, got_ref, w_own_ref, w_other_ref, out_ref):
    req_count, half_cands, model_width = own_ref.shape
    total = own_ref[...].astype(jnp.float32).reshape(req_count * half_cands, model_width)
    total = total + jnp.dot(keep_ref[...], w_own_ref[...], preferred_element_type=jnp.float32)
    total = total + jnp.dot(got_ref[...], w_other_ref[...], preferred_element_type=jnp.float32)
    out_ref[...] = total.reshape(req_count, half_cands, model_width).astype(jnp.bfloat16)


def exchange(owners, local, near, *far):
    half = local.shape[0]

    def send(rows, distance):
        return lax.ppermute(rows, "cache", [(place, place ^ distance) for place in range(owners)])

    came = [send(pair, 2 * (at + 1)) for at, pair in enumerate(far)]
    out = [local, send(near, 1)]
    for pair in came:
        out += [pair, send(pair[half:], 1)]
    return out


def body(candidates, input_gain, w_in, w_out, hist_keys, hist_values, request_session, hist_len, block_mask):
    owners = lax.axis_size("cache")
    req_count, half_cands, model_width = candidates.shape
    width = w_in.shape[2]
    cand_count = 2 * half_cands
    rows = req_count * half_cands
    hist_rows = hist_keys.shape[1]
    blocks = block_mask.shape[1]
    swap = [(0, 1), (1, 0)]
    bf16 = functools.partial(jax.ShapeDtypeStruct, dtype=jnp.bfloat16)
    sessions = request_session.reshape(-1)
    piece, pair = bf16((CAP * cand_count, width)), bf16((2 * CAP * cand_count, width))
    layout = [piece, piece] + [pair] * (owners // 2 - 1)
    table = pltpu.VMEM((owners * CAP, cand_count, width), jnp.bfloat16)

    other = lax.ppermute(candidates, "serve", swap)
    weights = jnp.transpose(w_in, (1, 0, 2))
    *pieces, queries, normed = kernel_call(
        query_kernel,
        layout + [bf16((2 * rows, width)), bf16((2 * rows, model_width))],
        [smem, vmem, vmem, vmem, vmem],
        [table],
        flops=4 * rows * model_width * width,
        moved=2 * model_width * width,
    )(sessions, candidates, other, input_gain.reshape(1, -1), weights)
    slots = exchange(owners, *pieces)
    slot_rows = owners * CAP * cand_count
    own_term, gates, hide_rows, hide_cols = kernel_call(
        self_kernel,
        [
            jax.ShapeDtypeStruct((2 * rows, width), jnp.float32),
            bf16((2 * rows, width)),
            bf16((slot_rows, HD)),
            bf16((hist_rows, HD)),
        ],
        [vmem, smem, vmem, vmem, vmem, vmem],
        [pltpu.VMEM((HD, owners * req_count), jnp.bfloat16)],
        flops=12 * rows * model_width * width,
        moved=6 * model_width * width,
    )(request_session.reshape(1, -1), hist_len, block_mask.T, normed, queries, weights)
    w_other = lax.ppermute(w_out, "serve", swap)
    backs = exchange(
        owners,
        *kernel_call(
            functools.partial(history_kernel, owners),
            layout,
            [vmem] * (4 + owners),
            flops=8 * slot_rows * hist_rows * width,
            moved=4 * hist_rows * width,
        )(hide_rows, hide_cols, hist_keys.reshape(hist_rows, width), hist_values.reshape(hist_rows, width), *slots)
    )
    keep, send = kernel_call(
        functools.partial(mix_kernel, owners, req_count),
        [bf16((rows, width))] * 2,
        [smem] + [vmem] * (2 + owners),
        [table],
    )(sessions, own_term, gates, *backs)
    got = lax.ppermute(send, "serve", swap)
    return kernel_call(
        output_kernel,
        bf16((req_count, half_cands, model_width)),
        [vmem] * 5,
        flops=8 * rows * model_width * width,
        moved=4 * model_width * width,
    )(candidates, keep, got, w_out, w_other)


def solution(mesh):
    placed = (
        P(("groups", "cache"), "serve", None),
        P(),
        P(None, None, "serve"),
        P("serve", None),
        P(("groups", "cache"), None, "serve"),
        P(("groups", "cache"), None, "serve"),
        P("groups", None),
        P("groups"),
        P("groups", None),
    )
    return jax.shard_map(
        body,
        mesh=mesh,
        in_specs=placed,
        out_specs=P(("groups", "cache"), "serve", None),
        check_vma=False,
    )
```

```python
import functools

import jax
import jax.numpy as jnp
from jax import lax
from jax.experimental import pallas as pl
from jax.experimental.pallas import tpu as pltpu
from jax.sharding import PartitionSpec as P

HD = 128
BLK = 64
CAP = 2
EPS = 1e-06
SCALE = HD ** (-0.5)
HIDE = -1e30
VMEM_LIMIT = 16 * 1024 * 1024

vmem = pl.BlockSpec(memory_space=pltpu.VMEM)
smem = pl.BlockSpec(memory_space=pltpu.SMEM)


def silu_of_half(half):
    return half + half * jnp.tanh(half)


def silu(x):
    return silu_of_half(x * 0.5)


def kernel_call(body, out_shape, in_specs, scratch_shapes=(), flops=0, moved=0):
    return pl.pallas_call(
        body,
        out_shape=out_shape,
        in_specs=in_specs,
        out_specs=jax.tree.map(lambda _: vmem, out_shape),
        scratch_shapes=scratch_shapes,
        cost_estimate=pl.CostEstimate(flops=flops, bytes_accessed=moved, transcendentals=0),
        compiler_params=pltpu.CompilerParams(vmem_limit_bytes=VMEM_LIMIT),
    )


def normed_rows(rows_ref, gain):
    rows = rows_ref[...].astype(jnp.float32)
    count, cands, width = rows.shape
    rows = rows.reshape(count * cands, width)
    mean_square = jnp.mean(rows * rows, axis=-1, keepdims=True)
    return (rows * lax.rsqrt(mean_square + EPS) * gain).astype(jnp.bfloat16)


def own_slots(sess_ref, req_count):
    me = lax.axis_index("cache")
    base = me * req_count
    sessions = [sess_ref[base + request] for request in range(req_count)]
    slots = []
    for request in range(req_count):
        place = 0
        for earlier in range(request):
            place = place + (sessions[earlier] == sessions[request]).astype(jnp.int32)
        slots.append((sessions[request] ^ me) * CAP + place)
    return slots


def query_kernel(sess_ref, own_ref, other_ref, gain_ref, w_ref, *refs):
    *slot_refs, queries_ref, normed_ref, table_ref = refs
    req_count, half_cands, _ = own_ref.shape
    rows = req_count * half_cands
    gain = gain_ref[...].astype(jnp.float32)
    normed_ref[:rows, :] = normed_rows(own_ref, gain)
    normed_ref[rows:, :] = normed_rows(other_ref, gain)
    table_ref[...] = jnp.zeros_like(table_ref)
    queries = silu(jnp.dot(normed_ref[...], w_ref[0], preferred_element_type=jnp.float32))
    queries_ref[...] = queries.astype(jnp.bfloat16)
    for request, slot in enumerate(own_slots(sess_ref, req_count)):
        low = request * half_cands
        both = jnp.concatenate([queries[low : low + half_cands], queries[rows + low : rows + low + half_cands]], axis=0)
        table_ref[slot] = both.astype(jnp.bfloat16)
    at = 0
    for slot_ref in slot_refs:
        slots = slot_ref.shape[0] // table_ref.shape[1]
        slot_ref[...] = table_ref[at : at + slots].reshape(slot_ref.shape)
        at += slots


def self_kernel(sess_ref, len_ref, mask_ref, normed_ref, queries_ref, w_ref, own_ref, gates_ref, hide_rows_ref, hide_cols_ref, marks_ref):
    width = queries_ref.shape[1]
    normed = normed_ref[...]
    me = lax.axis_index("cache")
    keys = silu(jnp.dot(normed, w_ref[1], preferred_element_type=jnp.float32)).astype(jnp.bfloat16)
    products = queries_ref[...].astype(jnp.float32) * keys.astype(jnp.float32)
    values = silu(jnp.dot(normed, w_ref[2], preferred_element_type=jnp.float32)).astype(jnp.bfloat16)
    gates_ref[...] = silu(jnp.dot(normed, w_ref[3], preferred_element_type=jnp.float32)).astype(jnp.bfloat16)
    for low in range(0, width, HD):
        score = jnp.sum(products[:, low : low + HD], axis=-1, keepdims=True) * SCALE
        own_ref[:, low : low + HD] = silu(score) * values[:, low : low + HD].astype(jnp.float32)

    blocks, requests = mask_ref.shape
    owners = len_ref.shape[0]
    per_owner = requests // owners
    sessions = sess_ref[...]
    lane = lax.broadcasted_iota(jnp.int32, (1, requests), 1)
    place = jnp.zeros((1, requests), jnp.int32)
    for back in range(1, per_owner):
        same = (pltpu.roll(sessions, back, 1) == sessions) & (lane % per_owner >= back)
        place = place + same.astype(jnp.int32)
    slot_of = jnp.where(sessions == me, ((lane // per_owner) ^ me) * CAP + place, -1)
    slots = owners * CAP
    at_slot = lax.broadcasted_iota(jnp.int32, (slots, requests), 0)
    chosen = (at_slot == slot_of).astype(jnp.float32).astype(jnp.bfloat16)
    marks_ref[...] = jnp.zeros_like(marks_ref)
    marks_ref[:blocks, :] = mask_ref[...].astype(jnp.float32).astype(jnp.bfloat16)
    seen = lax.dot_general(chosen, marks_ref[...], (((1,), (1,)), ((), ())), preferred_element_type=jnp.float32)
    at_lane = lax.broadcasted_iota(jnp.int32, (slots, HD), 1)
    hidden = jnp.where(at_lane < blocks, (1.0 - seen) * HIDE, jnp.where(at_lane == blocks, HIDE, 0.0))
    per_slot = hide_rows_ref.shape[0] // slots
    hide_rows_ref[...] = (
        jnp.broadcast_to(hidden[:, None, :], (slots, per_slot, HD)).reshape(slots * per_slot, HD).astype(jnp.bfloat16)
    )
    hist_rows = hide_cols_ref.shape[0]
    at_row = lax.broadcasted_iota(jnp.int32, (hist_rows, HD), 0)
    at_lane = lax.broadcasted_iota(jnp.int32, (hist_rows, HD), 1)
    hide_cols_ref[...] = jnp.where(
        (at_lane == at_row // BLK) | ((at_lane == blocks) & (at_row >= len_ref[me])), 1.0, 0.0
    ).astype(jnp.bfloat16)


def history_kernel(begin, owners, per_owner, hide_rows_ref, hide_cols_ref, keys_ref, values_ref, *refs):
    slot_refs, out_refs = refs[:owners], refs[owners:]
    width = slot_refs[0].shape[1]
    hist_rows = keys_ref.shape[0]
    span = min(256, hist_rows)
    per_step = max(1, min(owners, 256 // per_owner))
    places = []
    for out_ref in out_refs:
        places += [(out_ref, low) for low in range(0, out_ref.shape[0], per_owner)]
    for first in range(0, owners, per_step):
        group = range(first, min(first + per_step, owners))
        queries = jnp.concatenate([slot_refs[at][:per_owner, :] for at in group], axis=0)
        start_row = (begin + first) * per_owner
        hide_rows = hide_rows_ref[start_row : start_row + queries.shape[0], :]
        for low in range(0, width, HD):
            lhs = jnp.concatenate([queries[:, low : low + HD], hide_rows], axis=1)
            total = None
            for start in range(0, hist_rows, span):
                rhs = jnp.concatenate(
                    [keys_ref[start : start + span, low : low + HD], hide_cols_ref[start : start + span, :]], axis=1
                )
                scores = lax.dot_general(lhs, rhs, (((1,), (1,)), ((), ())), preferred_element_type=jnp.float32)
                weights = silu_of_half(scores * (0.5 * SCALE)).astype(jnp.bfloat16)
                term = jnp.dot(
                    weights, values_ref[start : start + span, low : low + HD], preferred_element_type=jnp.float32
                )
                total = term if total is None else total + term
            total = total.astype(jnp.bfloat16)
            for place, at in enumerate(group):
                out_ref, row = places[at]
                out_ref[row : row + per_owner, low : low + HD] = total[place * per_owner : (place + 1) * per_owner]


def mix_kernel(owners, req_count, sess_ref, own_ref, gates_ref, *refs):
    back_refs, (keep_ref, send_ref, table_ref) = refs[:owners], refs[owners:]
    rows, width = keep_ref.shape
    half_cands = rows // req_count
    for distance, back_ref in enumerate(back_refs):
        rows_here = back_ref[: back_refs[0].shape[0], :]
        table_ref[distance * CAP : (distance + 1) * CAP] = rows_here.reshape((CAP,) + table_ref.shape[1:])
    picked = [table_ref[slot].astype(jnp.float32) for slot in own_slots(sess_ref, req_count)]
    for side, out_ref in enumerate((keep_ref, send_ref)):
        history = jnp.concatenate([both[side * half_cands : (side + 1) * half_cands] for both in picked], axis=0)
        attended = history + own_ref[side * rows : (side + 1) * rows, :]
        gates = gates_ref[side * rows : (side + 1) * rows, :].astype(jnp.float32)
        for low in range(0, width, HD):
            head = attended[:, low : low + HD]
            level = lax.rsqrt(jnp.mean(head * head, axis=-1, keepdims=True) + EPS)
            out_ref[:, low : low + HD] = (head * level * gates[:, low : low + HD]).astype(jnp.bfloat16)


def kept_kernel(own_ref, keep_ref, w_own_ref, out_ref):
    rows, model_width = out_ref.shape
    total = own_ref[...].astype(jnp.float32).reshape(rows, model_width)
    out_ref[...] = total + jnp.dot(keep_ref[...], w_own_ref[...], preferred_element_type=jnp.float32)


def output_kernel(kept_ref, got_ref, w_other_ref, out_ref):
    total = kept_ref[...] + jnp.dot(got_ref[...], w_other_ref[...], preferred_element_type=jnp.float32)
    out_ref[...] = total.reshape(out_ref.shape).astype(jnp.bfloat16)


def send(rows, owners, distance):
    return lax.ppermute(rows, "cache", [(place, place ^ distance) for place in range(owners)])


def send_far(owners, pairs):
    came = {e: send(pairs[e], owners, 2 * e) for e in sorted(pairs, reverse=True)}
    return dict(sorted(came.items()))


def forward(owners, pairs):
    return {e: send(pair[pair.shape[0] // 2 :], owners, 1) for e, pair in pairs.items()}


def body(candidates, input_gain, w_in, w_out, hist_keys, hist_values, request_session, hist_len, block_mask):
    owners = lax.axis_size("cache")
    req_count, half_cands, model_width = candidates.shape
    width = w_in.shape[2]
    cand_count = 2 * half_cands
    rows = req_count * half_cands
    hist_rows = hist_keys.shape[1]
    blocks = block_mask.shape[1]
    swap = [(0, 1), (1, 0)]
    bf16 = functools.partial(jax.ShapeDtypeStruct, dtype=jnp.bfloat16)
    sessions = request_session.reshape(-1)
    piece, pair = bf16((CAP * cand_count, width)), bf16((2 * CAP * cand_count, width))
    layout = [piece, piece] + [pair] * (owners // 2 - 1)
    table = pltpu.VMEM((owners * CAP, cand_count, width), jnp.bfloat16)

    other = lax.ppermute(candidates, "serve", swap)
    weights = jnp.transpose(w_in, (1, 0, 2))
    local, near, *far, queries, normed = kernel_call(
        query_kernel,
        layout + [bf16((2 * rows, width)), bf16((2 * rows, model_width))],
        [smem, vmem, vmem, vmem, vmem],
        [table],
        flops=4 * rows * model_width * width,
        moved=2 * model_width * width,
    )(sessions, candidates, other, input_gain.reshape(1, -1), weights)
    came = send_far(owners, dict(enumerate(far, 1)))
    near = send(near, owners, 1)
    slot_rows = owners * CAP * cand_count
    own = kernel_call(
        self_kernel,
        [
            jax.ShapeDtypeStruct((2 * rows, width), jnp.float32),
            bf16((2 * rows, width)),
            bf16((slot_rows, HD)),
            bf16((hist_rows, HD)),
        ],
        [vmem, smem, vmem, vmem, vmem, vmem],
        [pltpu.VMEM((HD, owners * req_count), jnp.bfloat16)],
        flops=12 * rows * model_width * width,
        moved=6 * model_width * width,
    )(request_session.reshape(1, -1), hist_len, block_mask.T, normed, queries, weights)
    came, (own_term, gates, hide_rows, hide_cols) = lax.optimization_barrier((came, own))
    passed = forward(owners, came)
    slots = [local, near]
    for e in came:
        slots += [came[e], passed[e]]
    w_other = lax.ppermute(w_out, "serve", swap)
    keys, values = hist_keys.reshape(hist_rows, width), hist_values.reshape(hist_rows, width)
    back = []
    middle = owners // 2
    for begin, end, outs in ((0, middle, layout[: 1 + middle // 2]), (middle, owners, layout[1 + middle // 2 :])):
        back += kernel_call(
            functools.partial(history_kernel, begin, end - begin, CAP * cand_count),
            outs,
            [vmem] * (4 + end - begin),
            flops=8 * (slot_rows // 2) * hist_rows * width,
            moved=4 * hist_rows * width,
        )(hide_rows, hide_cols, keys, values, *slots[begin:end])
    local, near, *far = back
    came = send_far(owners, dict(enumerate(far, 1)))
    near = send(near, owners, 1)
    passed = forward(owners, came)
    backs = [local, near]
    for e in came:
        backs += [came[e], passed[e]]
    keep, send_mixed = kernel_call(
        functools.partial(mix_kernel, owners, req_count),
        [bf16((rows, width))] * 2,
        [smem] + [vmem] * (2 + owners),
        [table],
    )(sessions, own_term, gates, *backs)
    got = lax.ppermute(send_mixed, "serve", swap)
    kept = kernel_call(
        kept_kernel,
        jax.ShapeDtypeStruct((rows, model_width), jnp.float32),
        [vmem] * 3,
        flops=4 * rows * model_width * width,
        moved=2 * model_width * width,
    )(candidates, keep, w_out)
    return kernel_call(
        output_kernel,
        bf16((req_count, half_cands, model_width)),
        [vmem] * 3,
        flops=4 * rows * model_width * width,
        moved=2 * model_width * width,
    )(kept, got, w_other)


def solution(mesh):
    placed = (
        P(("groups", "cache"), "serve", None),
        P(),
        P(None, None, "serve"),
        P("serve", None),
        P(("groups", "cache"), None, "serve"),
        P(("groups", "cache"), None, "serve"),
        P("groups", None),
        P("groups"),
        P("groups", None),
    )
    return jax.shard_map(
        body,
        mesh=mesh,
        in_specs=placed,
        out_specs=P(("groups", "cache"), "serve", None),
        check_vma=False,
    )
```

```python
import functools

import jax
import jax.numpy as jnp
from jax import lax
from jax.experimental import pallas as pl
from jax.experimental.pallas import tpu as pltpu
from jax.sharding import PartitionSpec as P

HD = 128
BLK = 64
CAP = 2
EPS = 1e-06
SCALE = HD ** (-0.5)
HIDE = -1e30
VMEM_LIMIT = 16 * 1024 * 1024

vmem = pl.BlockSpec(memory_space=pltpu.VMEM)
smem = pl.BlockSpec(memory_space=pltpu.SMEM)


def silu_of_half(half):
    return half + half * jnp.tanh(half)


def silu(x):
    return silu_of_half(x * 0.5)


def kernel_call(body, out_shape, in_specs, scratch_shapes=(), flops=0, moved=0):
    return pl.pallas_call(
        body,
        out_shape=out_shape,
        in_specs=in_specs,
        out_specs=jax.tree.map(lambda _: vmem, out_shape),
        scratch_shapes=scratch_shapes,
        cost_estimate=pl.CostEstimate(flops=flops, bytes_accessed=moved, transcendentals=0),
        compiler_params=pltpu.CompilerParams(vmem_limit_bytes=VMEM_LIMIT),
    )


def normed_rows(rows_ref, gain):
    rows = rows_ref[...].astype(jnp.float32)
    count, cands, width = rows.shape
    rows = rows.reshape(count * cands, width)
    mean_square = jnp.mean(rows * rows, axis=-1, keepdims=True)
    return (rows * lax.rsqrt(mean_square + EPS) * gain).astype(jnp.bfloat16)


def position(distance, serve, owners):
    return jnp.where(distance % 2 == serve, 0, owners // 2) + distance // 2


def own_slots(sess_ref, req_count):
    me = lax.axis_index("cache")
    base = me * req_count
    sessions = [sess_ref[base + request] for request in range(req_count)]
    slots = []
    for request in range(req_count):
        place = 0
        for earlier in range(request):
            place = place + (sessions[earlier] == sessions[request]).astype(jnp.int32)
        slots.append((sessions[request] ^ me, place))
    return slots


def query_kernel(sess_ref, own_ref, other_ref, gain_ref, w_ref, keep_ref, give_ref, queries_ref, normed_ref, table_ref):
    req_count, half_cands, _ = own_ref.shape
    rows = req_count * half_cands
    serve = lax.axis_index("serve")
    slots = table_ref.shape[0]
    gain = gain_ref[...].astype(jnp.float32)
    normed_ref[:rows, :] = normed_rows(own_ref, gain)
    normed_ref[rows:, :] = normed_rows(other_ref, gain)
    table_ref[...] = jnp.zeros_like(table_ref)
    queries = silu(jnp.dot(normed_ref[...], w_ref[0], preferred_element_type=jnp.float32))
    queries_ref[...] = queries.astype(jnp.bfloat16)
    for request, (distance, place) in enumerate(own_slots(sess_ref, req_count)):
        low = request * half_cands
        both = jnp.concatenate([queries[low : low + half_cands], queries[rows + low : rows + low + half_cands]], axis=0)
        table_ref[position(distance, serve, slots // CAP) * CAP + place] = both.astype(jnp.bfloat16)
    keep_ref[...] = table_ref[: slots // 2].reshape(keep_ref.shape)
    give_ref[...] = table_ref[slots // 2 :].reshape(give_ref.shape)


def self_kernel(sess_ref, len_ref, mask_ref, normed_ref, queries_ref, w_ref, terms_ref, hide_rows_ref, hide_cols_ref, marks_ref):
    width = queries_ref.shape[1]
    normed = normed_ref[...]
    me = lax.axis_index("cache")
    keys = silu(jnp.dot(normed, w_ref[1], preferred_element_type=jnp.float32)).astype(jnp.bfloat16)
    products = queries_ref[...].astype(jnp.float32) * keys.astype(jnp.float32)
    values = silu(jnp.dot(normed, w_ref[2], preferred_element_type=jnp.float32)).astype(jnp.bfloat16)
    terms_ref[1] = silu(jnp.dot(normed, w_ref[3], preferred_element_type=jnp.float32)).astype(jnp.bfloat16)
    for low in range(0, width, HD):
        score = jnp.sum(products[:, low : low + HD], axis=-1, keepdims=True) * SCALE
        own_term = silu(score) * values[:, low : low + HD].astype(jnp.float32)
        terms_ref[0, :, low : low + HD] = own_term.astype(jnp.bfloat16)

    blocks, requests = mask_ref.shape
    owners = len_ref.shape[0]
    per_owner = requests // owners
    sessions = sess_ref[...]
    lane = lax.broadcasted_iota(jnp.int32, (1, requests), 1)
    place = jnp.zeros((1, requests), jnp.int32)
    for back in range(1, per_owner):
        same = (pltpu.roll(sessions, back, 1) == sessions) & (lane % per_owner >= back)
        place = place + same.astype(jnp.int32)
    at = position((lane // per_owner) ^ me, lax.axis_index("serve"), owners)
    slot_of = jnp.where(sessions == me, at * CAP + place, -1)
    slots = owners * CAP
    at_slot = lax.broadcasted_iota(jnp.int32, (slots, requests), 0)
    chosen = (at_slot == slot_of).astype(jnp.float32).astype(jnp.bfloat16)
    marks_ref[...] = jnp.zeros_like(marks_ref)
    marks_ref[:blocks, :] = mask_ref[...].astype(jnp.float32).astype(jnp.bfloat16)
    seen = lax.dot_general(chosen, marks_ref[...], (((1,), (1,)), ((), ())), preferred_element_type=jnp.float32)
    at_lane = lax.broadcasted_iota(jnp.int32, (slots, HD), 1)
    hidden = jnp.where(at_lane < blocks, (1.0 - seen) * HIDE, jnp.where(at_lane == blocks, HIDE, 0.0))
    per_slot = hide_rows_ref.shape[0] // slots
    hide_rows_ref[...] = (
        jnp.broadcast_to(hidden[:, None, :], (slots, per_slot, HD)).reshape(slots * per_slot, HD).astype(jnp.bfloat16)
    )
    hist_rows = hide_cols_ref.shape[0]
    at_row = lax.broadcasted_iota(jnp.int32, (hist_rows, HD), 0)
    at_lane = lax.broadcasted_iota(jnp.int32, (hist_rows, HD), 1)
    hide_cols_ref[...] = jnp.where(
        (at_lane == at_row // BLK) | ((at_lane == blocks) & (at_row >= len_ref[me])), 1.0, 0.0
    ).astype(jnp.bfloat16)


def pack_kernel(keep_ref, got_ref, *out_refs):
    half = out_refs[0].shape[0] // 2
    for at, out_ref in enumerate(out_refs):
        out_ref[:half, :] = keep_ref[at * half : (at + 1) * half, :]
        out_ref[half:, :] = got_ref[at * half : (at + 1) * half, :]


def history_kernel(owners, hide_rows_ref, hide_cols_ref, keys_ref, values_ref, *refs):
    slot_refs, (keep_ref, give_ref) = refs[:owners], refs[owners:]
    rows, width = keep_ref.shape
    per_owner = rows // (owners // 2)
    hist_rows = keys_ref.shape[0]
    span = min(256, hist_rows)
    per_step = max(1, min(owners, 256 // per_owner))
    for first in range(0, owners, per_step):
        group = range(first, min(first + per_step, owners))
        queries = jnp.concatenate([slot_refs[at][:per_owner, :] for at in group], axis=0)
        hide_rows = hide_rows_ref[first * per_owner : first * per_owner + queries.shape[0], :]
        for low in range(0, width, HD):
            lhs = jnp.concatenate([queries[:, low : low + HD], hide_rows], axis=1)
            total = None
            for start in range(0, hist_rows, span):
                rhs = jnp.concatenate(
                    [keys_ref[start : start + span, low : low + HD], hide_cols_ref[start : start + span, :]], axis=1
                )
                scores = lax.dot_general(lhs, rhs, (((1,), (1,)), ((), ())), preferred_element_type=jnp.float32)
                weights = silu_of_half(scores * (0.5 * SCALE)).astype(jnp.bfloat16)
                term = jnp.dot(
                    weights, values_ref[start : start + span, low : low + HD], preferred_element_type=jnp.float32
                )
                total = term if total is None else total + term
            total = total.astype(jnp.bfloat16)
            for place, at in enumerate(group):
                out_ref, row = (keep_ref, at * per_owner) if at < owners // 2 else (give_ref, at * per_owner - rows)
                out_ref[row : row + per_owner, low : low + HD] = total[place * per_owner : (place + 1) * per_owner]


def mix_kernel(messages, req_count, sess_ref, terms_ref, their_terms_ref, *refs):
    back_refs, (keep_ref, give_ref, table_ref) = refs[:messages], refs[messages:]
    rows, model_width = keep_ref.shape
    width = model_width // 2
    half_cands = rows // req_count
    slots = messages * CAP
    for at, back_ref in enumerate(back_refs):
        half = back_ref.shape[0] // 2
        for side in range(2):
            part = back_ref[side * half : (side + 1) * half, :].reshape((CAP,) + table_ref.shape[1:])
            table_ref[side * slots + at * CAP : side * slots + (at + 1) * CAP] = part
    picks = [distance // 2 * CAP + place for distance, place in own_slots(sess_ref, req_count)]
    for side, source_ref in enumerate((terms_ref, their_terms_ref)):
        picked = [table_ref[side * slots + pick].astype(jnp.float32) for pick in picks]
        for part in range(2):
            history = jnp.concatenate([both[part * half_cands : (part + 1) * half_cands] for both in picked], axis=0)
            attended = history + source_ref[0, part * rows : (part + 1) * rows, :].astype(jnp.float32)
            gates = source_ref[1, part * rows : (part + 1) * rows, :].astype(jnp.float32)
            ours = part == side
            out_ref, offset = (keep_ref, side * width) if ours else (give_ref, (1 - side) * width)
            for low in range(0, width, HD):
                head = attended[:, low : low + HD]
                level = lax.rsqrt(jnp.mean(head * head, axis=-1, keepdims=True) + EPS)
                mixed = head * level * gates[:, low : low + HD]
                out_ref[:, offset + low : offset + low + HD] = mixed.astype(jnp.bfloat16)


def output_kernel(sess_ref, own_ref, keep_ref, got_ref, w_own_ref, w_other_ref, out_ref):
    req_count, half_cands, model_width = own_ref.shape
    width = model_width // 2
    serve = lax.axis_index("serve")
    keep, got = keep_ref[...].astype(jnp.float32), got_ref[...].astype(jnp.float32)
    picked = []
    for request, (distance, _) in enumerate(own_slots(sess_ref, req_count)):
        low = request * half_cands
        picked.append(jnp.where(distance % 2 == serve, keep[low : low + half_cands], got[low : low + half_cands]))
    mixed = jnp.concatenate(picked, axis=0).astype(jnp.bfloat16)
    total = own_ref[...].astype(jnp.float32).reshape(req_count * half_cands, model_width)
    total = total + jnp.dot(mixed[:, :width], w_own_ref[...], preferred_element_type=jnp.float32)
    total = total + jnp.dot(mixed[:, width:], w_other_ref[...], preferred_element_type=jnp.float32)
    out_ref[...] = total.reshape(req_count, half_cands, model_width).astype(jnp.bfloat16)


def swap(rows):
    return lax.ppermute(rows, "serve", [(0, 1), (1, 0)])


def cross(owners, messages):
    came = {}
    for at in reversed(range(len(messages))):
        pairs = [
            (place * 2 + core, (place ^ (2 * at + core)) * 2 + core) for place in range(owners) for core in range(2)
        ]
        came[at] = lax.ppermute(messages[at], ("cache", "serve"), pairs)
    return [came[at] for at in range(len(messages))]


def body(candidates, input_gain, w_in, w_out, hist_keys, hist_values, request_session, hist_len, block_mask):
    owners = lax.axis_size("cache")
    req_count, half_cands, model_width = candidates.shape
    width = w_in.shape[2]
    cand_count = 2 * half_cands
    rows = req_count * half_cands
    hist_rows = hist_keys.shape[1]
    bf16 = functools.partial(jax.ShapeDtypeStruct, dtype=jnp.bfloat16)
    sessions = request_session.reshape(-1)
    messages = owners // 2
    piece = CAP * cand_count
    half_table = bf16((messages * piece, width))
    table = pltpu.VMEM((owners * CAP, cand_count, width), jnp.bfloat16)

    def pack(keep, got):
        return kernel_call(pack_kernel, [bf16((2 * piece, width))] * messages, [vmem] * 2)(keep, got)

    other = swap(candidates)
    weights = jnp.transpose(w_in, (1, 0, 2))
    keep, give, queries, normed = kernel_call(
        query_kernel,
        [half_table, half_table, bf16((2 * rows, width)), bf16((2 * rows, model_width))],
        [smem, vmem, vmem, vmem, vmem],
        [table],
        flops=4 * rows * model_width * width,
        moved=2 * model_width * width,
    )(sessions, candidates, other, input_gain.reshape(1, -1), weights)
    got = swap(give)
    own = kernel_call(
        self_kernel,
        [bf16((2, 2 * rows, width)), bf16((owners * piece, HD)), bf16((hist_rows, HD))],
        [vmem, smem, vmem, vmem, vmem, vmem],
        [pltpu.VMEM((HD, owners * req_count), jnp.bfloat16)],
        flops=12 * rows * model_width * width,
        moved=6 * model_width * width,
    )(request_session.reshape(1, -1), hist_len, block_mask.T, normed, queries, weights)
    got, (terms, hide_rows, hide_cols) = lax.optimization_barrier((got, own))
    came = cross(owners, pack(keep, got))
    slots = came + [swap(rows_of[piece:]) for rows_of in came]
    their_terms = swap(terms)
    w_other = swap(w_out)
    keep, give = kernel_call(
        functools.partial(history_kernel, owners),
        [half_table] * 2,
        [vmem] * (4 + owners),
        flops=8 * owners * piece * hist_rows * width,
        moved=4 * hist_rows * width,
    )(hide_rows, hide_cols, hist_keys.reshape(hist_rows, width), hist_values.reshape(hist_rows, width), *slots)
    backs = cross(owners, pack(keep, swap(give)))
    keep, give = kernel_call(
        functools.partial(mix_kernel, messages, req_count),
        [bf16((rows, model_width))] * 2,
        [smem] + [vmem] * (2 + messages),
        [table],
    )(sessions, terms, their_terms, *backs)
    return kernel_call(
        output_kernel,
        bf16((req_count, half_cands, model_width)),
        [smem] + [vmem] * 5,
        flops=8 * rows * model_width * width,
        moved=4 * model_width * width,
    )(sessions, candidates, keep, swap(give), w_out, w_other)


def solution(mesh):
    placed = (
        P(("groups", "cache"), "serve", None),
        P(),
        P(None, None, "serve"),
        P("serve", None),
        P(("groups", "cache"), None, "serve"),
        P(("groups", "cache"), None, "serve"),
        P("groups", None),
        P("groups"),
        P("groups", None),
    )
    return jax.shard_map(
        body,
        mesh=mesh,
        in_specs=placed,
        out_specs=P(("groups", "cache"), "serve", None),
        check_vma=False,
    )
```

```python
import functools

import jax
import jax.numpy as jnp
from jax import lax
from jax.experimental import pallas as pl
from jax.experimental.pallas import tpu as pltpu
from jax.sharding import PartitionSpec as P

HD = 128
BLK = 64
CAP = 2
EPS = 1e-06
SCALE = HD ** (-0.5)
HIDE = -1e30
VMEM_LIMIT = 16 * 1024 * 1024

vmem = pl.BlockSpec(memory_space=pltpu.VMEM)
smem = pl.BlockSpec(memory_space=pltpu.SMEM)


def silu_of_half(half):
    return half + half * jnp.tanh(half)


def silu(x):
    return silu_of_half(x * 0.5)


def kernel_call(body, out_shape, in_specs, scratch_shapes=(), flops=0, moved=0):
    return pl.pallas_call(
        body,
        out_shape=out_shape,
        in_specs=in_specs,
        out_specs=jax.tree.map(lambda _: vmem, out_shape),
        scratch_shapes=scratch_shapes,
        cost_estimate=pl.CostEstimate(flops=flops, bytes_accessed=moved, transcendentals=0),
        compiler_params=pltpu.CompilerParams(vmem_limit_bytes=VMEM_LIMIT),
    )


def normed_rows(rows_ref, gain):
    rows = rows_ref[...].astype(jnp.float32)
    count, cands, width = rows.shape
    rows = rows.reshape(count * cands, width)
    mean_square = jnp.mean(rows * rows, axis=-1, keepdims=True)
    return (rows * lax.rsqrt(mean_square + EPS) * gain).astype(jnp.bfloat16)


def position(distance, serve, owners):
    return jnp.where(distance % 2 == serve, 0, owners // 2) + distance // 2


def own_slots(sess_ref, req_count):
    me = lax.axis_index("cache")
    base = me * req_count
    sessions = [sess_ref[base + request] for request in range(req_count)]
    slots = []
    for request in range(req_count):
        place = 0
        for earlier in range(request):
            place = place + (sessions[earlier] == sessions[request]).astype(jnp.int32)
        slots.append((sessions[request] ^ me, place))
    return slots


def query_kernel(sess_ref, own_ref, other_ref, gain_ref, w_ref, keep_ref, give_ref, queries_ref, normed_ref, table_ref):
    req_count, half_cands, _ = own_ref.shape
    rows = req_count * half_cands
    serve = lax.axis_index("serve")
    slots = table_ref.shape[0]
    gain = gain_ref[...].astype(jnp.float32)
    normed_ref[:rows, :] = normed_rows(own_ref, gain)
    normed_ref[rows:, :] = normed_rows(other_ref, gain)
    table_ref[...] = jnp.zeros_like(table_ref)
    queries = silu(jnp.dot(normed_ref[...], w_ref[0], preferred_element_type=jnp.float32))
    queries_ref[...] = queries.astype(jnp.bfloat16)
    for request, (distance, place) in enumerate(own_slots(sess_ref, req_count)):
        low = request * half_cands
        both = jnp.concatenate([queries[low : low + half_cands], queries[rows + low : rows + low + half_cands]], axis=0)
        table_ref[position(distance, serve, slots // CAP) * CAP + place] = both.astype(jnp.bfloat16)
    keep_ref[...] = table_ref[: slots // 2].reshape(keep_ref.shape)
    give_ref[...] = table_ref[slots // 2 :].reshape(give_ref.shape)


def self_kernel(sess_ref, len_ref, mask_ref, normed_ref, queries_ref, w_ref, terms_ref, hide_rows_ref, hide_cols_ref, marks_ref):
    width = queries_ref.shape[1]
    normed = normed_ref[...]
    me = lax.axis_index("cache")
    keys = silu(jnp.dot(normed, w_ref[1], preferred_element_type=jnp.float32)).astype(jnp.bfloat16)
    products = queries_ref[...].astype(jnp.float32) * keys.astype(jnp.float32)
    values = silu(jnp.dot(normed, w_ref[2], preferred_element_type=jnp.float32)).astype(jnp.bfloat16)
    terms_ref[1] = silu(jnp.dot(normed, w_ref[3], preferred_element_type=jnp.float32)).astype(jnp.bfloat16)
    for low in range(0, width, HD):
        score = jnp.sum(products[:, low : low + HD], axis=-1, keepdims=True) * SCALE
        own_term = silu(score) * values[:, low : low + HD].astype(jnp.float32)
        terms_ref[0, :, low : low + HD] = own_term.astype(jnp.bfloat16)

    blocks, requests = mask_ref.shape
    owners = len_ref.shape[0]
    per_owner = requests // owners
    sessions = sess_ref[...]
    lane = lax.broadcasted_iota(jnp.int32, (1, requests), 1)
    place = jnp.zeros((1, requests), jnp.int32)
    for back in range(1, per_owner):
        same = (pltpu.roll(sessions, back, 1) == sessions) & (lane % per_owner >= back)
        place = place + same.astype(jnp.int32)
    at = position((lane // per_owner) ^ me, lax.axis_index("serve"), owners)
    slot_of = jnp.where(sessions == me, at * CAP + place, -1)
    slots = owners * CAP
    at_slot = lax.broadcasted_iota(jnp.int32, (slots, requests), 0)
    chosen = (at_slot == slot_of).astype(jnp.float32).astype(jnp.bfloat16)
    marks_ref[...] = jnp.zeros_like(marks_ref)
    marks_ref[:blocks, :] = mask_ref[...].astype(jnp.float32).astype(jnp.bfloat16)
    seen = lax.dot_general(chosen, marks_ref[...], (((1,), (1,)), ((), ())), preferred_element_type=jnp.float32)
    at_lane = lax.broadcasted_iota(jnp.int32, (slots, HD), 1)
    hidden = jnp.where(at_lane < blocks, (1.0 - seen) * HIDE, jnp.where(at_lane == blocks, HIDE, 0.0))
    per_slot = hide_rows_ref.shape[0] // slots
    hide_rows_ref[...] = (
        jnp.broadcast_to(hidden[:, None, :], (slots, per_slot, HD)).reshape(slots * per_slot, HD).astype(jnp.bfloat16)
    )
    hist_rows = hide_cols_ref.shape[0]
    at_row = lax.broadcasted_iota(jnp.int32, (hist_rows, HD), 0)
    at_lane = lax.broadcasted_iota(jnp.int32, (hist_rows, HD), 1)
    hide_cols_ref[...] = jnp.where(
        (at_lane == at_row // BLK) | ((at_lane == blocks) & (at_row >= len_ref[me])), 1.0, 0.0
    ).astype(jnp.bfloat16)


def pack_kernel(keep_ref, got_ref, *out_refs):
    half = out_refs[0].shape[0] // 2
    for at, out_ref in enumerate(out_refs):
        out_ref[:half, :] = keep_ref[at * half : (at + 1) * half, :]
        out_ref[half:, :] = got_ref[at * half : (at + 1) * half, :]


def history_kernel(owners, hide_rows_ref, hide_cols_ref, keys_ref, values_ref, *refs):
    keep_ref, give_ref = refs[owners:]
    slot_refs = [None] * owners
    for at, order in enumerate(far_first(owners // 2)):
        slot_refs[order], slot_refs[owners // 2 + order] = refs[2 * at : 2 * at + 2]
    rows, width = keep_ref.shape
    per_owner = rows // (owners // 2)
    hist_rows = keys_ref.shape[0]
    span = min(256, hist_rows)
    per_step = max(1, min(owners, 256 // per_owner))
    for first in range(0, owners, per_step):
        group = range(first, min(first + per_step, owners))
        queries = jnp.concatenate([slot_refs[at][:per_owner, :] for at in group], axis=0)
        hide_rows = hide_rows_ref[first * per_owner : first * per_owner + queries.shape[0], :]
        for low in range(0, width, HD):
            lhs = jnp.concatenate([queries[:, low : low + HD], hide_rows], axis=1)
            total = None
            for start in range(0, hist_rows, span):
                rhs = jnp.concatenate(
                    [keys_ref[start : start + span, low : low + HD], hide_cols_ref[start : start + span, :]], axis=1
                )
                scores = lax.dot_general(lhs, rhs, (((1,), (1,)), ((), ())), preferred_element_type=jnp.float32)
                weights = silu_of_half(scores * (0.5 * SCALE)).astype(jnp.bfloat16)
                term = jnp.dot(
                    weights, values_ref[start : start + span, low : low + HD], preferred_element_type=jnp.float32
                )
                total = term if total is None else total + term
            total = total.astype(jnp.bfloat16)
            for place, at in enumerate(group):
                out_ref, row = (keep_ref, at * per_owner) if at < owners // 2 else (give_ref, at * per_owner - rows)
                out_ref[row : row + per_owner, low : low + HD] = total[place * per_owner : (place + 1) * per_owner]


def mix_kernel(messages, req_count, sess_ref, terms_ref, their_terms_ref, *refs):
    back_refs, (keep_ref, give_ref, table_ref) = refs[:messages], refs[messages:]
    rows, model_width = keep_ref.shape
    width = model_width // 2
    half_cands = rows // req_count
    slots = messages * CAP
    for at, back_ref in zip(far_first(messages), back_refs):
        half = back_ref.shape[0] // 2
        for side in range(2):
            part = back_ref[side * half : (side + 1) * half, :].reshape((CAP,) + table_ref.shape[1:])
            table_ref[side * slots + at * CAP : side * slots + (at + 1) * CAP] = part
    serve = lax.axis_index("serve")
    own = own_slots(sess_ref, req_count)
    picks = [distance // 2 * CAP + place for distance, place in own]
    live = jnp.concatenate(
        [jnp.full((half_cands, HD), distance % 2 == serve, jnp.int32) for distance, _ in own], axis=0
    ) == 1
    for side, source_ref in enumerate((terms_ref, their_terms_ref)):
        picked = [table_ref[side * slots + pick].astype(jnp.float32) for pick in picks]
        for part in range(2):
            history = jnp.concatenate([both[part * half_cands : (part + 1) * half_cands] for both in picked], axis=0)
            attended = history + source_ref[0, part * rows : (part + 1) * rows, :].astype(jnp.float32)
            gates = source_ref[1, part * rows : (part + 1) * rows, :].astype(jnp.float32)
            ours = part == side
            out_ref, offset = (keep_ref, side * width) if ours else (give_ref, (1 - side) * width)
            for low in range(0, width, HD):
                head = attended[:, low : low + HD]
                level = lax.rsqrt(jnp.mean(head * head, axis=-1, keepdims=True) + EPS)
                mixed = head * level * gates[:, low : low + HD]
                out_ref[:, offset + low : offset + low + HD] = jnp.where(live, mixed, 0.0).astype(jnp.bfloat16)


def project(mixed_ref, w_own_ref, w_other_ref):
    width = w_own_ref.shape[0]
    return jnp.dot(mixed_ref[:, :width], w_own_ref[...], preferred_element_type=jnp.float32) + jnp.dot(
        mixed_ref[:, width:], w_other_ref[...], preferred_element_type=jnp.float32
    )


def kept_kernel(own_ref, keep_ref, w_own_ref, w_other_ref, out_ref):
    own = own_ref[...].astype(jnp.float32).reshape(out_ref.shape)
    out_ref[...] = own + project(keep_ref, w_own_ref, w_other_ref)


def output_kernel(kept_ref, got_ref, w_own_ref, w_other_ref, out_ref):
    total = kept_ref[...] + project(got_ref, w_own_ref, w_other_ref)
    out_ref[...] = total.reshape(out_ref.shape).astype(jnp.bfloat16)


def far_first(count):
    return list(reversed(range(count)))


def swap(rows):
    return lax.ppermute(rows, "serve", [(0, 1), (1, 0)])


def cross(owners, messages):
    came = []
    for at in far_first(len(messages)):
        pairs = [
            (place * 2 + core, (place ^ (2 * at + core)) * 2 + core) for place in range(owners) for core in range(2)
        ]
        came.append(lax.ppermute(messages[at], ("cache", "serve"), pairs))
    return came


def body(candidates, input_gain, w_in, w_out, hist_keys, hist_values, request_session, hist_len, block_mask):
    owners = lax.axis_size("cache")
    req_count, half_cands, model_width = candidates.shape
    width = w_in.shape[2]
    cand_count = 2 * half_cands
    rows = req_count * half_cands
    hist_rows = hist_keys.shape[1]
    bf16 = functools.partial(jax.ShapeDtypeStruct, dtype=jnp.bfloat16)
    sessions = request_session.reshape(-1)
    messages = owners // 2
    piece = CAP * cand_count
    half_table = bf16((messages * piece, width))
    table = pltpu.VMEM((owners * CAP, cand_count, width), jnp.bfloat16)

    def pack(keep, got):
        return kernel_call(pack_kernel, [bf16((2 * piece, width))] * messages, [vmem] * 2)(keep, got)

    other = swap(candidates)
    weights = jnp.transpose(w_in, (1, 0, 2))
    keep, give, queries, normed = kernel_call(
        query_kernel,
        [half_table, half_table, bf16((2 * rows, width)), bf16((2 * rows, model_width))],
        [smem, vmem, vmem, vmem, vmem],
        [table],
        flops=4 * rows * model_width * width,
        moved=2 * model_width * width,
    )(sessions, candidates, other, input_gain.reshape(1, -1), weights)
    got = swap(give)
    own = kernel_call(
        self_kernel,
        [bf16((2, 2 * rows, width)), bf16((owners * piece, HD)), bf16((hist_rows, HD))],
        [vmem, smem, vmem, vmem, vmem, vmem],
        [pltpu.VMEM((HD, owners * req_count), jnp.bfloat16)],
        flops=12 * rows * model_width * width,
        moved=6 * model_width * width,
    )(request_session.reshape(1, -1), hist_len, block_mask.T, normed, queries, weights)
    got, (terms, hide_rows, hide_cols) = lax.optimization_barrier((got, own))
    came = cross(owners, pack(keep, got))
    swapped = [swap(rows_of[piece:]) for rows_of in came]
    slots = [rows_of for both in zip(came, swapped) for rows_of in both]
    their_terms = swap(terms)
    w_other = swap(w_out)
    keep, give = kernel_call(
        functools.partial(history_kernel, owners),
        [half_table] * 2,
        [vmem] * (4 + owners),
        flops=8 * owners * piece * hist_rows * width,
        moved=4 * hist_rows * width,
    )(hide_rows, hide_cols, hist_keys.reshape(hist_rows, width), hist_values.reshape(hist_rows, width), *slots)
    backs = cross(owners, pack(keep, swap(give)))
    keep, give = kernel_call(
        functools.partial(mix_kernel, messages, req_count),
        [bf16((rows, model_width))] * 2,
        [smem] + [vmem] * (2 + messages),
        [table],
    )(sessions, terms, their_terms, *backs)
    got = swap(give)
    kept = kernel_call(
        kept_kernel,
        jax.ShapeDtypeStruct((rows, model_width), jnp.float32),
        [vmem] * 4,
        flops=8 * rows * model_width * width,
        moved=4 * model_width * width,
    )(candidates, keep, w_out, w_other)
    return kernel_call(
        output_kernel,
        bf16((req_count, half_cands, model_width)),
        [vmem] * 4,
        flops=8 * rows * model_width * width,
        moved=4 * model_width * width,
    )(kept, got, w_out, w_other)


def solution(mesh):
    placed = (
        P(("groups", "cache"), "serve", None),
        P(),
        P(None, None, "serve"),
        P("serve", None),
        P(("groups", "cache"), None, "serve"),
        P(("groups", "cache"), None, "serve"),
        P("groups", None),
        P("groups"),
        P("groups", None),
    )
    return jax.shard_map(
        body,
        mesh=mesh,
        in_specs=placed,
        out_specs=P(("groups", "cache"), "serve", None),
        check_vma=False,
    )
```

```python
import functools

import jax
import jax.numpy as jnp
from jax import lax
from jax.experimental import pallas as pl
from jax.experimental.pallas import tpu as pltpu
from jax.sharding import PartitionSpec as P

HD = 128
BLK = 64
CAP = 2
EPS = 1e-06
SCALE = HD ** (-0.5)
HIDE = -1e30
VMEM_LIMIT = 16 * 1024 * 1024

vmem = pl.BlockSpec(memory_space=pltpu.VMEM)
smem = pl.BlockSpec(memory_space=pltpu.SMEM)


def silu_of_half(half):
    return half + half * jnp.tanh(half)


def silu(x):
    return silu_of_half(x * 0.5)


def kernel_call(body, out_shape, in_specs, scratch_shapes=(), flops=0, moved=0):
    return pl.pallas_call(
        body,
        out_shape=out_shape,
        in_specs=in_specs,
        out_specs=jax.tree.map(lambda _: vmem, out_shape),
        scratch_shapes=scratch_shapes,
        cost_estimate=pl.CostEstimate(flops=flops, bytes_accessed=moved, transcendentals=0),
        compiler_params=pltpu.CompilerParams(vmem_limit_bytes=VMEM_LIMIT),
    )


def normed_rows(rows_ref, gain):
    rows = rows_ref[...].astype(jnp.float32)
    rows = rows.reshape(-1, rows.shape[-1])
    mean_square = jnp.mean(rows * rows, axis=-1, keepdims=True)
    return (rows * lax.rsqrt(mean_square + EPS) * gain).astype(jnp.bfloat16)


def position(distance, serve, owners):
    return jnp.where(distance % 2 == serve, 0, owners // 2) + distance // 2


def own_slots(sess_ref, req_count):
    me = lax.axis_index("cache")
    base = me * req_count
    sessions = [sess_ref[base + request] for request in range(req_count)]
    slots = []
    for request in range(req_count):
        place = 0
        for earlier in range(request):
            place = place + (sessions[earlier] == sessions[request]).astype(jnp.int32)
        slots.append((sessions[request] ^ me, place))
    return slots


def message_kernel(sess_ref, own_ref, other_ref, *refs):
    *out_refs, table_ref = refs
    req_count, half_cands, _ = own_ref.shape
    serve = lax.axis_index("serve")
    messages = len(out_refs)
    unused = 2 * messages * CAP
    for at in range(2 * messages * CAP):
        table_ref[at] = jnp.zeros_like(table_ref[at])
    for request, (distance, place) in enumerate(own_slots(sess_ref, req_count)):
        ours = distance % 2 == serve
        for side, rows_ref in enumerate((own_ref, other_ref)):
            at = (distance // 2 * 2 + side) * CAP + place
            table_ref[jnp.where(ours, at, unused + side)] = rows_ref[request].astype(jnp.float32)
    for at, out_ref in enumerate(out_refs):
        rows = table_ref[2 * CAP * at : 2 * CAP * (at + 1)]
        out_ref[...] = rows.reshape(out_ref.shape).astype(jnp.bfloat16)


def visible_kernel(sess_ref, len_ref, mask_ref, hide_rows_ref, hide_cols_ref, marks_ref):
    me = lax.axis_index("cache")
    blocks, requests = mask_ref.shape
    owners = len_ref.shape[0]
    per_owner = requests // owners
    sessions = sess_ref[...]
    lane = lax.broadcasted_iota(jnp.int32, (1, requests), 1)
    place = jnp.zeros((1, requests), jnp.int32)
    for back in range(1, per_owner):
        same = (pltpu.roll(sessions, back, 1) == sessions) & (lane % per_owner >= back)
        place = place + same.astype(jnp.int32)
    at = position((lane // per_owner) ^ me, lax.axis_index("serve"), owners)
    slot_of = jnp.where(sessions == me, at * CAP + place, -1)
    slots = owners * CAP
    at_slot = lax.broadcasted_iota(jnp.int32, (slots, requests), 0)
    chosen = (at_slot == slot_of).astype(jnp.float32).astype(jnp.bfloat16)
    marks_ref[...] = jnp.zeros_like(marks_ref)
    marks_ref[:blocks, :] = mask_ref[...].astype(jnp.float32).astype(jnp.bfloat16)
    seen = lax.dot_general(chosen, marks_ref[...], (((1,), (1,)), ((), ())), preferred_element_type=jnp.float32)
    at_lane = lax.broadcasted_iota(jnp.int32, (slots, HD), 1)
    hidden = jnp.where(at_lane < blocks, (1.0 - seen) * HIDE, jnp.where(at_lane == blocks, HIDE, 0.0))
    half = hide_rows_ref.shape[0] // slots // 2
    spread = jnp.broadcast_to(hidden.reshape(owners, 1, CAP, 1, HD), (owners, 2, CAP, half, HD))
    hide_rows_ref[...] = spread.reshape(hide_rows_ref.shape).astype(jnp.bfloat16)
    hist_rows = hide_cols_ref.shape[0]
    at_row = lax.broadcasted_iota(jnp.int32, (hist_rows, HD), 0)
    at_lane = lax.broadcasted_iota(jnp.int32, (hist_rows, HD), 1)
    hide_cols_ref[...] = jnp.where(
        (at_lane == at_row // BLK) | ((at_lane == blocks) & (at_row >= len_ref[me])), 1.0, 0.0
    ).astype(jnp.bfloat16)


def self_kernel(own_ref, other_ref, gain_ref, w_ref, keep_ref, give_ref, normed_ref):
    rows, width = keep_ref.shape[1:]
    gain = gain_ref[...].astype(jnp.float32)
    normed_ref[:rows, :] = normed_rows(own_ref, gain)
    normed_ref[rows:, :] = normed_rows(other_ref, gain)
    normed = normed_ref[...]

    def activated(part):
        return silu(jnp.dot(normed, w_ref[part], preferred_element_type=jnp.float32)).astype(jnp.bfloat16)

    products = activated(0).astype(jnp.float32) * activated(1).astype(jnp.float32)
    values, gates = activated(2), activated(3)
    for low in range(0, width, HD):
        score = jnp.sum(products[:, low : low + HD], axis=-1, keepdims=True) * SCALE
        term = (silu(score) * values[:, low : low + HD].astype(jnp.float32)).astype(jnp.bfloat16)
        keep_ref[0, :, low : low + HD] = term[:rows]
        give_ref[0, :, low : low + HD] = term[rows:]
    keep_ref[1] = gates[:rows]
    give_ref[1] = gates[rows:]


def pack_kernel(keep_ref, got_ref, *out_refs):
    part = out_refs[0].shape[0] // 4
    for at, out_ref in enumerate(out_refs):
        for side in range(2):
            low = (2 * at + side) * part
            out_ref[2 * side * part : (2 * side + 1) * part, :] = keep_ref[low : low + part, :]
            out_ref[(2 * side + 1) * part : (2 * side + 2) * part, :] = got_ref[low : low + part, :]


def history_kernel(owners, gain_ref, w_ref, hide_rows_ref, hide_cols_ref, keys_ref, values_ref, *refs):
    keep_ref, give_ref = refs[owners:]
    slot_refs = [None] * owners
    for at, order in enumerate(far_first(owners // 2)):
        slot_refs[order], slot_refs[owners // 2 + order] = refs[2 * at : 2 * at + 2]
    rows, width = keep_ref.shape
    per_owner = rows // (owners // 2)
    hist_rows = keys_ref.shape[0]
    span = min(256, hist_rows)
    per_step = max(1, min(owners, 256 // per_owner))
    gain = gain_ref[...].astype(jnp.float32)
    for first in range(0, owners, per_step):
        group = range(first, min(first + per_step, owners))
        normed = jnp.concatenate([normed_rows(slot_refs[at], gain) for at in group], axis=0)
        queries = silu(jnp.dot(normed, w_ref[0], preferred_element_type=jnp.float32)).astype(jnp.bfloat16)
        hide_rows = hide_rows_ref[first * per_owner : first * per_owner + queries.shape[0], :]
        for low in range(0, width, HD):
            lhs = jnp.concatenate([queries[:, low : low + HD], hide_rows], axis=1)
            total = None
            for start in range(0, hist_rows, span):
                rhs = jnp.concatenate(
                    [keys_ref[start : start + span, low : low + HD], hide_cols_ref[start : start + span, :]], axis=1
                )
                scores = lax.dot_general(lhs, rhs, (((1,), (1,)), ((), ())), preferred_element_type=jnp.float32)
                weights = silu_of_half(scores * (0.5 * SCALE)).astype(jnp.bfloat16)
                term = jnp.dot(
                    weights, values_ref[start : start + span, low : low + HD], preferred_element_type=jnp.float32
                )
                total = term if total is None else total + term
            total = total.astype(jnp.bfloat16)
            for place, at in enumerate(group):
                out_ref, row = (keep_ref, at * per_owner) if at < owners // 2 else (give_ref, at * per_owner - rows)
                out_ref[row : row + per_owner, low : low + HD] = total[place * per_owner : (place + 1) * per_owner]


def output_kernel(messages, sess_ref, own_ref, keep_ref, got_ref, w_own_ref, w_other_ref, *refs):
    back_refs, (out_ref, table_ref) = refs[: 2 * messages], refs[2 * messages :]
    req_count, half_cands, model_width = own_ref.shape
    rows = req_count * half_cands
    width = model_width // 2
    serve = lax.axis_index("serve")
    part = CAP * half_cands
    for order, at in enumerate(far_first(messages)):
        for side in range(2):
            block = back_refs[2 * order + side][: 2 * part, :].astype(jnp.float32).reshape(2, CAP, half_cands, width)
            for heads in range(2):
                low = ((side * messages + at) * 2 + heads) * CAP
                table_ref[low : low + CAP] = block[heads if side == 0 else 1 - heads]
    own = own_slots(sess_ref, req_count)
    total = own_ref[...].astype(jnp.float32).reshape(rows, model_width)
    for heads, (terms_ref, w_ref) in enumerate(((keep_ref, w_own_ref), (got_ref, w_other_ref))):
        history = []
        for distance, place in own:
            side = jnp.where(distance % 2 == serve, 0, messages)
            history.append(table_ref[((side + distance // 2) * 2 + heads) * CAP + place])
        attended = jnp.concatenate(history, axis=0) + terms_ref[0].astype(jnp.float32)
        gates = terms_ref[1].astype(jnp.float32)
        mixed = []
        for low in range(0, width, HD):
            head = attended[:, low : low + HD]
            level = lax.rsqrt(jnp.mean(head * head, axis=-1, keepdims=True) + EPS)
            mixed.append((head * level * gates[:, low : low + HD]).astype(jnp.bfloat16))
        total = total + jnp.dot(jnp.concatenate(mixed, axis=1), w_ref[...], preferred_element_type=jnp.float32)
    out_ref[...] = total.reshape(out_ref.shape).astype(jnp.bfloat16)


def far_first(count):
    return list(reversed(range(count)))


def swap(rows):
    return lax.ppermute(rows, "serve", [(0, 1), (1, 0)])


def cross(owners, messages):
    came = []
    for at in far_first(len(messages)):
        pairs = [
            (place * 2 + core, (place ^ (2 * at + core)) * 2 + core) for place in range(owners) for core in range(2)
        ]
        came.append(lax.ppermute(messages[at], ("cache", "serve"), pairs))
    return came


def body(candidates, input_gain, w_in, w_out, hist_keys, hist_values, request_session, hist_len, block_mask):
    owners = lax.axis_size("cache")
    req_count, half_cands, model_width = candidates.shape
    width = w_in.shape[2]
    rows = req_count * half_cands
    hist_rows = hist_keys.shape[1]
    bf16 = functools.partial(jax.ShapeDtypeStruct, dtype=jnp.bfloat16)
    sessions = request_session.reshape(-1)
    gain = input_gain.reshape(1, -1)
    messages = owners // 2
    piece = 2 * CAP * half_cands
    half_table = bf16((messages * piece, width))

    other, w_out = lax.optimization_barrier((swap(candidates), w_out))
    w_other = swap(w_out)
    out = kernel_call(
        message_kernel,
        [bf16((piece, model_width))] * messages,
        [smem, vmem, vmem],
        [pltpu.VMEM((2 * messages * CAP + 2, half_cands, model_width), jnp.float32)],
    )(sessions, candidates, other)
    out, w_in = lax.optimization_barrier((out, w_in))
    weights = jnp.transpose(w_in, (1, 0, 2))
    came = cross(owners, out)
    visible = kernel_call(
        visible_kernel,
        [bf16((owners * piece, HD)), bf16((hist_rows, HD))],
        [vmem, smem, vmem],
        [pltpu.VMEM((HD, owners * req_count), jnp.bfloat16)],
    )(request_session.reshape(1, -1), hist_len, block_mask.T)
    came, weights, (hide_rows, hide_cols) = lax.optimization_barrier((came, weights, visible))
    swapped = [swap(message) for message in came]
    keep, give = kernel_call(
        functools.partial(history_kernel, owners),
        [half_table] * 2,
        [vmem] * (6 + owners),
        flops=8 * owners * piece * hist_rows * width,
        moved=4 * hist_rows * width,
    )(
        gain,
        weights,
        hide_rows,
        hide_cols,
        hist_keys.reshape(hist_rows, width),
        hist_values.reshape(hist_rows, width),
        *[rows_of for both in zip(came, swapped) for rows_of in both],
    )
    out = kernel_call(pack_kernel, [bf16((2 * piece, width))] * messages, [vmem] * 2)(keep, swap(give))
    out, other = lax.optimization_barrier((out, other))
    backs = cross(owners, out)
    keep, give = kernel_call(
        self_kernel,
        [bf16((2, rows, width))] * 2,
        [vmem] * 4,
        [pltpu.VMEM((2 * rows, model_width), jnp.bfloat16)],
        flops=16 * rows * model_width * width,
        moved=8 * model_width * width,
    )(candidates, other, gain, weights)
    backs, keep, give = lax.optimization_barrier((backs, keep, give))
    got = swap(give)
    returned = [(back, swap(back[piece:])) for back in backs]
    return kernel_call(
        functools.partial(output_kernel, messages),
        bf16((req_count, half_cands, model_width)),
        [smem] + [vmem] * (5 + 2 * messages),
        [pltpu.VMEM((4 * messages * CAP, half_cands, width), jnp.float32)],
        flops=8 * rows * model_width * width,
        moved=4 * model_width * width,
    )(sessions, candidates, keep, got, w_out, w_other, *[rows_of for both in returned for rows_of in both])


def solution(mesh):
    placed = (
        P(("groups", "cache"), "serve", None),
        P(),
        P(None, None, "serve"),
        P("serve", None),
        P(("groups", "cache"), None, "serve"),
        P(("groups", "cache"), None, "serve"),
        P("groups", None),
        P("groups"),
        P("groups", None),
    )
    return jax.shard_map(
        body,
        mesh=mesh,
        in_specs=placed,
        out_specs=P(("groups", "cache"), "serve", None),
        check_vma=False,
    )
```

```python
import functools

import jax
import jax.numpy as jnp
from jax import lax
from jax.experimental import pallas as pl
from jax.experimental.pallas import tpu as pltpu
from jax.sharding import PartitionSpec as P

HD = 128
BLK = 64
CAP = 2
EPS = 1e-06
SCALE = HD ** (-0.5)
HIDE = -1e30
VMEM_LIMIT = 16 * 1024 * 1024

vmem = pl.BlockSpec(memory_space=pltpu.VMEM)
smem = pl.BlockSpec(memory_space=pltpu.SMEM)


def silu_of_half(half):
    return half + half * jnp.tanh(half)


def silu(x):
    return silu_of_half(x * 0.5)


def kernel_call(body, out_shape, in_specs, scratch_shapes=(), flops=0, moved=0):
    return pl.pallas_call(
        body,
        out_shape=out_shape,
        in_specs=in_specs,
        out_specs=jax.tree.map(lambda _: vmem, out_shape),
        scratch_shapes=scratch_shapes,
        cost_estimate=pl.CostEstimate(flops=flops, bytes_accessed=moved, transcendentals=0),
        compiler_params=pltpu.CompilerParams(vmem_limit_bytes=VMEM_LIMIT),
    )


def normed_rows(rows_ref, gain):
    rows = rows_ref[...].astype(jnp.float32)
    rows = rows.reshape(-1, rows.shape[-1])
    mean_square = jnp.mean(rows * rows, axis=-1, keepdims=True)
    return (rows * lax.rsqrt(mean_square + EPS) * gain).astype(jnp.bfloat16)


def position(distance, serve, owners):
    return jnp.where(distance % 2 == serve, 0, owners // 2) + distance // 2


def own_slots(sess_ref, req_count):
    me = lax.axis_index("cache")
    base = me * req_count
    sessions = [sess_ref[base + request] for request in range(req_count)]
    slots = []
    for request in range(req_count):
        place = 0
        for earlier in range(request):
            place = place + (sessions[earlier] == sessions[request]).astype(jnp.int32)
        slots.append((sessions[request] ^ me, place))
    return slots


def message_kernel(sess_ref, own_ref, other_ref, *refs):
    *out_refs, table_ref = refs
    req_count, half_cands, _ = own_ref.shape
    serve = lax.axis_index("serve")
    messages = len(out_refs)
    unused = 2 * messages * CAP
    for at in range(2 * messages * CAP):
        table_ref[at] = jnp.zeros_like(table_ref[at])
    for request, (distance, place) in enumerate(own_slots(sess_ref, req_count)):
        ours = distance % 2 == serve
        for side, rows_ref in enumerate((own_ref, other_ref)):
            at = (distance // 2 * 2 + side) * CAP + place
            table_ref[jnp.where(ours, at, unused + side)] = rows_ref[request].astype(jnp.float32)
    for at, out_ref in enumerate(out_refs):
        rows = table_ref[2 * CAP * at : 2 * CAP * (at + 1)]
        out_ref[...] = rows.reshape(out_ref.shape).astype(jnp.bfloat16)


def visible_kernel(sess_ref, len_ref, mask_ref, hide_rows_ref, hide_cols_ref, marks_ref):
    me = lax.axis_index("cache")
    blocks, requests = mask_ref.shape
    owners = len_ref.shape[0]
    per_owner = requests // owners
    sessions = sess_ref[...]
    lane = lax.broadcasted_iota(jnp.int32, (1, requests), 1)
    place = jnp.zeros((1, requests), jnp.int32)
    for back in range(1, per_owner):
        same = (pltpu.roll(sessions, back, 1) == sessions) & (lane % per_owner >= back)
        place = place + same.astype(jnp.int32)
    at = position((lane // per_owner) ^ me, lax.axis_index("serve"), owners)
    slot_of = jnp.where(sessions == me, at * CAP + place, -1)
    slots = owners * CAP
    at_slot = lax.broadcasted_iota(jnp.int32, (slots, requests), 0)
    chosen = (at_slot == slot_of).astype(jnp.float32).astype(jnp.bfloat16)
    marks_ref[...] = jnp.zeros_like(marks_ref)
    marks_ref[:blocks, :] = mask_ref[...].astype(jnp.float32).astype(jnp.bfloat16)
    seen = lax.dot_general(chosen, marks_ref[...], (((1,), (1,)), ((), ())), preferred_element_type=jnp.float32)
    at_lane = lax.broadcasted_iota(jnp.int32, (slots, HD), 1)
    hidden = jnp.where(at_lane < blocks, (1.0 - seen) * HIDE, jnp.where(at_lane == blocks, HIDE, 0.0))
    half = hide_rows_ref.shape[0] // slots // 2
    spread = jnp.broadcast_to(hidden.reshape(owners, 1, CAP, 1, HD), (owners, 2, CAP, half, HD))
    hide_rows_ref[...] = spread.reshape(hide_rows_ref.shape).astype(jnp.bfloat16)
    hist_rows = hide_cols_ref.shape[0]
    at_row = lax.broadcasted_iota(jnp.int32, (hist_rows, HD), 0)
    at_lane = lax.broadcasted_iota(jnp.int32, (hist_rows, HD), 1)
    hide_cols_ref[...] = jnp.where(
        (at_lane == at_row // BLK) | ((at_lane == blocks) & (at_row >= len_ref[me])), 1.0, 0.0
    ).astype(jnp.bfloat16)


def self_kernel(own_ref, other_ref, gain_ref, w_ref, keep_ref, give_ref, normed_ref):
    rows, width = keep_ref.shape[1:]
    gain = gain_ref[...].astype(jnp.float32)
    normed_ref[:rows, :] = normed_rows(own_ref, gain)
    normed_ref[rows:, :] = normed_rows(other_ref, gain)
    normed = normed_ref[...]

    def activated(part):
        return silu(jnp.dot(normed, w_ref[part], preferred_element_type=jnp.float32)).astype(jnp.bfloat16)

    products = activated(0).astype(jnp.float32) * activated(1).astype(jnp.float32)
    values, gates = activated(2), activated(3)
    for low in range(0, width, HD):
        score = jnp.sum(products[:, low : low + HD], axis=-1, keepdims=True) * SCALE
        term = (silu(score) * values[:, low : low + HD].astype(jnp.float32)).astype(jnp.bfloat16)
        keep_ref[0, :, low : low + HD] = term[:rows]
        give_ref[0, :, low : low + HD] = term[rows:]
    keep_ref[1] = gates[:rows]
    give_ref[1] = gates[rows:]


def pack_kernel(keep_ref, got_ref, *out_refs):
    part = out_refs[0].shape[0] // 4
    for at, out_ref in enumerate(out_refs):
        for side in range(2):
            low = (2 * at + side) * part
            out_ref[2 * side * part : (2 * side + 1) * part, :] = keep_ref[low : low + part, :]
            out_ref[(2 * side + 1) * part : (2 * side + 2) * part, :] = got_ref[low : low + part, :]


def history_kernel(owners, gain_ref, w_ref, hide_rows_ref, hide_cols_ref, keys_ref, values_ref, *refs):
    keep_ref, give_ref = refs[owners:]
    slot_refs = [None] * owners
    for at, order in enumerate(far_first(owners // 2)):
        slot_refs[order], slot_refs[owners // 2 + order] = refs[2 * at : 2 * at + 2]
    rows, width = keep_ref.shape
    per_owner = rows // (owners // 2)
    hist_rows = keys_ref.shape[0]
    span = min(256, hist_rows)
    per_step = max(1, min(owners, 256 // per_owner))
    gain = gain_ref[...].astype(jnp.float32)
    for first in range(0, owners, per_step):
        group = range(first, min(first + per_step, owners))
        normed = jnp.concatenate([normed_rows(slot_refs[at], gain) for at in group], axis=0)
        queries = silu(jnp.dot(normed, w_ref[0], preferred_element_type=jnp.float32)).astype(jnp.bfloat16)
        hide_rows = hide_rows_ref[first * per_owner : first * per_owner + queries.shape[0], :]
        for low in range(0, width, HD):
            lhs = jnp.concatenate([queries[:, low : low + HD], hide_rows], axis=1)
            total = None
            for start in range(0, hist_rows, span):
                rhs = jnp.concatenate(
                    [keys_ref[start : start + span, low : low + HD], hide_cols_ref[start : start + span, :]], axis=1
                )
                scores = lax.dot_general(lhs, rhs, (((1,), (1,)), ((), ())), preferred_element_type=jnp.float32)
                weights = silu_of_half(scores * (0.5 * SCALE)).astype(jnp.bfloat16)
                term = jnp.dot(
                    weights, values_ref[start : start + span, low : low + HD], preferred_element_type=jnp.float32
                )
                total = term if total is None else total + term
            total = total.astype(jnp.bfloat16)
            for place, at in enumerate(group):
                out_ref, row = (keep_ref, at * per_owner) if at < owners // 2 else (give_ref, at * per_owner - rows)
                out_ref[row : row + per_owner, low : low + HD] = total[place * per_owner : (place + 1) * per_owner]


def output_kernel(messages, sess_ref, own_ref, keep_ref, got_ref, w_own_ref, w_other_ref, *refs):
    back_refs, (out_ref, table_ref) = refs[: 2 * messages], refs[2 * messages :]
    req_count, half_cands, model_width = own_ref.shape
    rows = req_count * half_cands
    width = model_width // 2
    serve = lax.axis_index("serve")
    part = CAP * half_cands
    for order, at in enumerate(far_first(messages)):
        for side in range(2):
            block = back_refs[2 * order + side][: 2 * part, :].astype(jnp.float32).reshape(2, CAP, half_cands, width)
            for heads in range(2):
                low = ((side * messages + at) * 2 + heads) * CAP
                table_ref[low : low + CAP] = block[heads if side == 0 else 1 - heads]
    own = own_slots(sess_ref, req_count)
    total = own_ref[...].astype(jnp.float32).reshape(rows, model_width)
    for heads, (terms_ref, w_ref) in enumerate(((keep_ref, w_own_ref), (got_ref, w_other_ref))):
        history = []
        for distance, place in own:
            side = jnp.where(distance % 2 == serve, 0, messages)
            history.append(table_ref[((side + distance // 2) * 2 + heads) * CAP + place])
        attended = jnp.concatenate(history, axis=0) + terms_ref[0].astype(jnp.float32)
        gates = terms_ref[1].astype(jnp.float32)
        mixed = []
        for low in range(0, width, HD):
            head = attended[:, low : low + HD]
            level = lax.rsqrt(jnp.mean(head * head, axis=-1, keepdims=True) + EPS)
            mixed.append((head * level * gates[:, low : low + HD]).astype(jnp.bfloat16))
        total = total + jnp.dot(jnp.concatenate(mixed, axis=1), w_ref[...], preferred_element_type=jnp.float32)
    out_ref[...] = total.reshape(out_ref.shape).astype(jnp.bfloat16)


def far_first(count):
    return list(reversed(range(count)))


def swap(rows):
    return lax.ppermute(rows, "serve", [(0, 1), (1, 0)])


def cross(owners, at, message):
    pairs = [(place * 2 + core, (place ^ (2 * at + core)) * 2 + core) for place in range(owners) for core in range(2)]
    return lax.ppermute(message, ("cache", "serve"), pairs)


def cross_beside(owners, messages, work, take):
    order = far_first(len(messages))
    first, (second, *rest) = messages[order[0]], [messages[at] for at in order[1:]]
    came = [cross(owners, order[0], first)]
    second, done = lax.optimization_barrier((second, work(first)))
    came.append(cross(owners, order[1], second))
    came[0], rest = lax.optimization_barrier((came[0], rest))
    came += [cross(owners, at, message) for at, message in zip(order[2:], rest)]
    return [rows_of for message in came for rows_of in (message, swap(message[take:]))], done


def body(candidates, input_gain, w_in, w_out, hist_keys, hist_values, request_session, hist_len, block_mask):
    owners = lax.axis_size("cache")
    req_count, half_cands, model_width = candidates.shape
    width = w_in.shape[2]
    rows = req_count * half_cands
    hist_rows = hist_keys.shape[1]
    bf16 = functools.partial(jax.ShapeDtypeStruct, dtype=jnp.bfloat16)
    sessions = request_session.reshape(-1)
    gain = input_gain.reshape(1, -1)
    messages = owners // 2
    piece = 2 * CAP * half_cands
    half_table = bf16((messages * piece, width))

    visible = kernel_call(
        visible_kernel,
        [bf16((owners * piece, HD)), bf16((hist_rows, HD))],
        [vmem, smem, vmem],
        [pltpu.VMEM((HD, owners * req_count), jnp.bfloat16)],
    )(request_session.reshape(1, -1), hist_len, block_mask.T)
    other, w_out, (hide_rows, hide_cols) = lax.optimization_barrier((swap(candidates), w_out, visible))
    w_other = swap(w_out)
    out = kernel_call(
        message_kernel,
        [bf16((piece, model_width))] * messages,
        [smem, vmem, vmem],
        [pltpu.VMEM((2 * messages * CAP + 2, half_cands, model_width), jnp.float32)],
    )(sessions, candidates, other)

    def relayout(after):
        return jnp.transpose(lax.optimization_barrier((w_in, after))[0], (1, 0, 2))

    came, weights = cross_beside(owners, out, relayout, 0)
    keep, give = kernel_call(
        functools.partial(history_kernel, owners),
        [half_table] * 2,
        [vmem] * (6 + owners),
        flops=8 * owners * piece * hist_rows * width,
        moved=4 * hist_rows * width,
    )(
        gain,
        weights,
        hide_rows,
        hide_cols,
        hist_keys.reshape(hist_rows, width),
        hist_values.reshape(hist_rows, width),
        *came,
    )
    keep, give, w_other = lax.optimization_barrier((keep, give, w_other))
    out = kernel_call(pack_kernel, [bf16((2 * piece, width))] * messages, [vmem] * 2)(keep, swap(give))

    def own_terms(after):
        return kernel_call(
            self_kernel,
            [bf16((2, rows, width))] * 2,
            [vmem] * 4,
            [pltpu.VMEM((2 * rows, model_width), jnp.bfloat16)],
            flops=16 * rows * model_width * width,
            moved=8 * model_width * width,
        )(candidates, lax.optimization_barrier((other, after))[0], gain, weights)

    backs, (keep, give) = cross_beside(owners, out, own_terms, piece)
    return kernel_call(
        functools.partial(output_kernel, messages),
        bf16((req_count, half_cands, model_width)),
        [smem] + [vmem] * (5 + 2 * messages),
        [pltpu.VMEM((4 * messages * CAP, half_cands, width), jnp.float32)],
        flops=8 * rows * model_width * width,
        moved=4 * model_width * width,
    )(sessions, candidates, keep, swap(give), w_out, w_other, *backs)


def solution(mesh):
    placed = (
        P(("groups", "cache"), "serve", None),
        P(),
        P(None, None, "serve"),
        P("serve", None),
        P(("groups", "cache"), None, "serve"),
        P(("groups", "cache"), None, "serve"),
        P("groups", None),
        P("groups"),
        P("groups", None),
    )
    return jax.shard_map(
        body,
        mesh=mesh,
        in_specs=placed,
        out_specs=P(("groups", "cache"), "serve", None),
        check_vma=False,
    )
```

```python
import functools

import jax
import jax.numpy as jnp
from jax import lax
from jax.experimental import pallas as pl
from jax.experimental.pallas import tpu as pltpu
from jax.sharding import PartitionSpec as P

HD = 128
BLK = 64
CAP = 2
EPS = 1e-06
SCALE = HD ** (-0.5)
HIDE = -1e30
VMEM_LIMIT = 16 * 1024 * 1024

vmem = pl.BlockSpec(memory_space=pltpu.VMEM)
smem = pl.BlockSpec(memory_space=pltpu.SMEM)


def silu_of_half(half):
    return half + half * jnp.tanh(half)


def silu(x):
    return silu_of_half(x * 0.5)


def kernel_call(body, out_shape, in_specs, scratch_shapes=(), flops=0, moved=0):
    return pl.pallas_call(
        body,
        out_shape=out_shape,
        in_specs=in_specs,
        out_specs=jax.tree.map(lambda _: vmem, out_shape),
        scratch_shapes=scratch_shapes,
        cost_estimate=pl.CostEstimate(flops=flops, bytes_accessed=moved, transcendentals=0),
        compiler_params=pltpu.CompilerParams(vmem_limit_bytes=VMEM_LIMIT),
    )


def normed_rows(rows_ref, gain):
    rows = rows_ref[...].astype(jnp.float32)
    rows = rows.reshape(-1, rows.shape[-1])
    mean_square = jnp.mean(rows * rows, axis=-1, keepdims=True)
    return (rows * lax.rsqrt(mean_square + EPS) * gain).astype(jnp.bfloat16)


def core_of(distance):
    parity = distance
    for shift in (16, 8, 4, 2, 1):
        parity = parity ^ (parity >> shift)
    return parity & 1


def position(distance, serve, owners):
    return jnp.where(core_of(distance) == serve, 0, owners // 2) + distance // 2


def own_slots(sess_ref, req_count):
    me = lax.axis_index("cache")
    base = me * req_count
    sessions = [sess_ref[base + request] for request in range(req_count)]
    slots = []
    for request in range(req_count):
        place = 0
        for earlier in range(request):
            place = place + (sessions[earlier] == sessions[request]).astype(jnp.int32)
        slots.append((sessions[request] ^ me, place))
    return slots


def front_kernel(
    sess_hbm, len_hbm, mask_hbm, cand_hbm,
    hide_rows_ref, hide_cols_ref, chosen_ref, own_ref,
    sess_ref, len_ref, mask_ref, marks_ref, sems,
):
    copies = [
        pltpu.make_async_copy(source, target, sems.at[at])
        for at, (source, target) in enumerate(
            ((sess_hbm, sess_ref), (len_hbm, len_ref), (mask_hbm, mask_ref), (cand_hbm, own_ref))
        )
    ]
    for copy in copies:
        copy.start()
    me, serve = lax.axis_index("cache"), lax.axis_index("serve")
    blocks, requests = mask_ref.shape
    owners = len_ref.shape[1]
    per_owner = requests // owners
    half_cands = own_ref.shape[1]
    rows = per_owner * half_cands
    hist_rows = hide_cols_ref.shape[0]
    at_row = lax.broadcasted_iota(jnp.int32, (hist_rows, HD), 0)
    at_lane = lax.broadcasted_iota(jnp.int32, (hist_rows, HD), 1)
    in_block = at_lane == at_row // BLK
    marks_ref[...] = jnp.zeros_like(marks_ref)
    for copy in copies[:3]:
        copy.wait()

    sessions = sess_ref[...]
    lane = lax.broadcasted_iota(jnp.int32, (1, requests), 1)
    place = jnp.zeros((1, requests), jnp.int32)
    for back in range(1, per_owner):
        same = (pltpu.roll(sessions, back, 1) == sessions) & (lane % per_owner >= back)
        place = place + same.astype(jnp.int32)

    distance = sessions ^ me
    code = jnp.where(core_of(distance) == serve, (distance // 2) * (2 * CAP) + place, owners * CAP)
    request = lax.broadcasted_iota(jnp.int32, (requests, 2 * rows), 0)
    column = lax.broadcasted_iota(jnp.int32, (requests, 2 * rows), 1)
    spread = (request == me * per_owner + (column % rows) // half_cands).astype(jnp.float32).astype(jnp.bfloat16)
    codes = jnp.broadcast_to(code, (8, requests)).astype(jnp.float32).astype(jnp.bfloat16)
    target = jnp.dot(codes, spread, preferred_element_type=jnp.float32)[:1].astype(jnp.int32)
    at = lax.broadcasted_iota(jnp.int32, chosen_ref.shape, 0)
    column = lax.broadcasted_iota(jnp.int32, chosen_ref.shape, 1)
    hit = (at // half_cands == target + (column // rows) * CAP) & (at % half_cands == column % half_cands)
    chosen_ref[...] = hit.astype(jnp.float32).astype(jnp.bfloat16)

    at = position((lane // per_owner) ^ me, serve, owners)
    slot_of = jnp.where(sessions == me, at * CAP + place, -1)
    slots = owners * CAP
    at_slot = lax.broadcasted_iota(jnp.int32, (slots, requests), 0)
    taken = (at_slot == slot_of).astype(jnp.float32).astype(jnp.bfloat16)
    marks_ref[:blocks, :] = mask_ref[...].astype(jnp.float32).astype(jnp.bfloat16)
    seen = lax.dot_general(taken, marks_ref[...], (((1,), (1,)), ((), ())), preferred_element_type=jnp.float32)
    slot_lane = lax.broadcasted_iota(jnp.int32, (slots, HD), 1)
    hidden = jnp.where(slot_lane < blocks, (1.0 - seen) * HIDE, jnp.where(slot_lane == blocks, HIDE, 0.0))
    wide = jnp.broadcast_to(hidden.reshape(owners, 1, CAP, 1, HD), (owners, 2, CAP, half_cands, HD))
    hide_rows_ref[...] = wide.reshape(hide_rows_ref.shape).astype(jnp.bfloat16)
    owner_lane = lax.broadcasted_iota(jnp.int32, (1, owners), 1)
    length = jnp.sum(jnp.where(owner_lane == me, len_ref[...], 0), axis=1, keepdims=True)
    hide_cols_ref[...] = jnp.where(in_block | ((at_lane == blocks) & (at_row >= length)), 1.0, 0.0).astype(jnp.bfloat16)
    copies[3].wait()


def message_kernel(chosen_ref, own_ref, other_ref, *out_refs):
    model_width = own_ref.shape[2]
    source = jnp.concatenate(
        [ref[...].astype(jnp.float32).reshape(-1, model_width) for ref in (own_ref, other_ref)], axis=0
    ).astype(jnp.bfloat16)
    rows = jnp.dot(chosen_ref[...], source, preferred_element_type=jnp.float32)
    piece = out_refs[0].shape[0]
    for at, out_ref in enumerate(out_refs):
        out_ref[...] = rows[at * piece : (at + 1) * piece].astype(jnp.bfloat16)


def self_kernel(own_ref, other_ref, gain_ref, w_ref, keep_ref, give_ref, normed_ref):
    rows, width = keep_ref.shape[1:]
    gain = gain_ref[...].astype(jnp.float32)
    normed_ref[:rows, :] = normed_rows(own_ref, gain)
    normed_ref[rows:, :] = normed_rows(other_ref, gain)
    normed = normed_ref[...]

    def activated(part):
        return silu(jnp.dot(normed, w_ref[part], preferred_element_type=jnp.float32)).astype(jnp.bfloat16)

    products = activated(0).astype(jnp.float32) * activated(1).astype(jnp.float32)
    values, gates = activated(2), activated(3)
    for low in range(0, width, HD):
        score = jnp.sum(products[:, low : low + HD], axis=-1, keepdims=True) * SCALE
        term = (silu(score) * values[:, low : low + HD].astype(jnp.float32)).astype(jnp.bfloat16)
        keep_ref[0, :, low : low + HD] = term[:rows]
        give_ref[0, :, low : low + HD] = term[rows:]
    keep_ref[1] = gates[:rows]
    give_ref[1] = gates[rows:]


def pack_kernel(keep_ref, got_ref, *out_refs):
    part = out_refs[0].shape[0] // 4
    for at, out_ref in enumerate(out_refs):
        for side in range(2):
            low = (2 * at + side) * part
            out_ref[2 * side * part : (2 * side + 1) * part, :] = keep_ref[low : low + part, :]
            out_ref[(2 * side + 1) * part : (2 * side + 2) * part, :] = got_ref[low : low + part, :]


def history_kernel(owners, gain_ref, w_ref, hide_rows_ref, hide_cols_ref, keys_ref, values_ref, *refs):
    keep_ref, give_ref = refs[owners:]
    slot_refs = [None] * owners
    for at, order in enumerate(far_first(owners // 2)):
        slot_refs[order], slot_refs[owners // 2 + order] = refs[2 * at : 2 * at + 2]
    rows, width = keep_ref.shape
    per_owner = rows // (owners // 2)
    hist_rows = keys_ref.shape[0]
    span = min(256, hist_rows)
    per_step = max(1, min(owners, 256 // per_owner))
    gain = gain_ref[...].astype(jnp.float32)
    for first in range(0, owners, per_step):
        group = range(first, min(first + per_step, owners))
        normed = jnp.concatenate([normed_rows(slot_refs[at], gain) for at in group], axis=0)
        queries = silu(jnp.dot(normed, w_ref[0], preferred_element_type=jnp.float32)).astype(jnp.bfloat16)
        hide_rows = hide_rows_ref[first * per_owner : first * per_owner + queries.shape[0], :]
        for low in range(0, width, HD):
            lhs = jnp.concatenate([queries[:, low : low + HD], hide_rows], axis=1)
            total = None
            for start in range(0, hist_rows, span):
                rhs = jnp.concatenate(
                    [keys_ref[start : start + span, low : low + HD], hide_cols_ref[start : start + span, :]], axis=1
                )
                scores = lax.dot_general(lhs, rhs, (((1,), (1,)), ((), ())), preferred_element_type=jnp.float32)
                weights = silu_of_half(scores * (0.5 * SCALE)).astype(jnp.bfloat16)
                term = jnp.dot(
                    weights, values_ref[start : start + span, low : low + HD], preferred_element_type=jnp.float32
                )
                total = term if total is None else total + term
            total = total.astype(jnp.bfloat16)
            for place, at in enumerate(group):
                out_ref, row = (keep_ref, at * per_owner) if at < owners // 2 else (give_ref, at * per_owner - rows)
                out_ref[row : row + per_owner, low : low + HD] = total[place * per_owner : (place + 1) * per_owner]


def output_kernel(messages, sess_ref, own_ref, keep_ref, got_ref, w_own_ref, w_other_ref, *refs):
    back_refs, (out_ref, table_ref) = refs[: 2 * messages], refs[2 * messages :]
    req_count, half_cands, model_width = own_ref.shape
    rows = req_count * half_cands
    width = model_width // 2
    serve = lax.axis_index("serve")
    part = CAP * half_cands
    for order, at in enumerate(far_first(messages)):
        for side in range(2):
            block = back_refs[2 * order + side][: 2 * part, :].astype(jnp.float32).reshape(2, CAP, half_cands, width)
            for heads in range(2):
                low = ((side * messages + at) * 2 + heads) * CAP
                table_ref[low : low + CAP] = block[heads if side == 0 else 1 - heads]
    own = own_slots(sess_ref, req_count)
    total = own_ref[...].astype(jnp.float32).reshape(rows, model_width)
    for heads, (terms_ref, w_ref) in enumerate(((keep_ref, w_own_ref), (got_ref, w_other_ref))):
        history = []
        for distance, place in own:
            side = jnp.where(core_of(distance) == serve, 0, messages)
            history.append(table_ref[((side + distance // 2) * 2 + heads) * CAP + place])
        attended = jnp.concatenate(history, axis=0) + terms_ref[0].astype(jnp.float32)
        gates = terms_ref[1].astype(jnp.float32)
        mixed = []
        for low in range(0, width, HD):
            head = attended[:, low : low + HD]
            level = lax.rsqrt(jnp.mean(head * head, axis=-1, keepdims=True) + EPS)
            mixed.append((head * level * gates[:, low : low + HD]).astype(jnp.bfloat16))
        total = total + jnp.dot(jnp.concatenate(mixed, axis=1), w_ref[...], preferred_element_type=jnp.float32)
    out_ref[...] = total.reshape(out_ref.shape).astype(jnp.bfloat16)


def far_first(count):
    return list(reversed(range(count)))


def swap(rows):
    return lax.ppermute(rows, "serve", [(0, 1), (1, 0)])


def cross(owners, messages):
    came = []
    for at in far_first(len(messages)):
        steps = [2 * at + side for side in range(2)]
        pairs = [(place * 2 + core_of(step), (place ^ step) * 2 + core_of(step)) for place in range(owners) for step in steps]
        came.append(lax.ppermute(messages[at], ("cache", "serve"), pairs))
    return came


def body(candidates, input_gain, w_in, w_out, hist_keys, hist_values, request_session, hist_len, block_mask):
    owners = lax.axis_size("cache")
    req_count, half_cands, model_width = candidates.shape
    width = w_in.shape[2]
    rows = req_count * half_cands
    hist_rows = hist_keys.shape[1]
    bf16 = functools.partial(jax.ShapeDtypeStruct, dtype=jnp.bfloat16)
    sessions = request_session.reshape(-1)
    gain = input_gain.reshape(1, -1)
    messages = owners // 2
    piece = 2 * CAP * half_cands
    half_table = bf16((messages * piece, width))

    hbm = pl.BlockSpec(memory_space=pltpu.HBM)
    hide_rows, hide_cols, chosen, own = kernel_call(
        front_kernel,
        [
            bf16((owners * piece, HD)),
            bf16((hist_rows, HD)),
            bf16((messages * piece, 2 * rows)),
            bf16(candidates.shape),
        ],
        [hbm] * 4,
        [
            pltpu.VMEM((1, owners * req_count), jnp.int32),
            pltpu.VMEM((1, owners), jnp.int32),
            pltpu.VMEM(block_mask.shape[::-1], jnp.int32),
            pltpu.VMEM((HD, owners * req_count), jnp.bfloat16),
            pltpu.SemaphoreType.DMA((4,)),
        ],
    )(request_session.reshape(1, -1), hist_len.reshape(1, -1), block_mask.T, candidates)
    other, w_out, own = lax.optimization_barrier((swap(candidates), w_out, own))
    w_other = swap(w_out)
    out = kernel_call(message_kernel, [bf16((piece, model_width))] * messages, [vmem] * 3)(chosen, own, other)
    out, w_in = lax.optimization_barrier((out, w_in))
    weights = jnp.transpose(w_in, (1, 0, 2))
    came = cross(owners, out)
    terms = kernel_call(
        self_kernel,
        [bf16((2, rows, width))] * 2,
        [vmem] * 4,
        [pltpu.VMEM((2 * rows, model_width), jnp.bfloat16)],
        flops=16 * rows * model_width * width,
        moved=8 * model_width * width,
    )(own, other, gain, weights)
    came, weights, (keep_terms, give_terms) = lax.optimization_barrier((came, weights, terms))
    swapped = [swap(message) for message in came]
    got_terms = swap(give_terms)
    keep, give = kernel_call(
        functools.partial(history_kernel, owners),
        [half_table] * 2,
        [vmem] * (6 + owners),
        flops=8 * owners * piece * hist_rows * width,
        moved=4 * hist_rows * width,
    )(
        gain,
        weights,
        hide_rows,
        hide_cols,
        hist_keys.reshape(hist_rows, width),
        hist_values.reshape(hist_rows, width),
        *[rows_of for both in zip(came, swapped) for rows_of in both],
    )
    keep, give, got_terms, w_other = lax.optimization_barrier((keep, give, got_terms, w_other))
    backs = cross(owners, kernel_call(pack_kernel, [bf16((2 * piece, width))] * messages, [vmem] * 2)(keep, swap(give)))
    returned = [rows_of for back in backs for rows_of in (back, swap(back[piece:]))]
    return kernel_call(
        functools.partial(output_kernel, messages),
        bf16((req_count, half_cands, model_width)),
        [smem] + [vmem] * (5 + 2 * messages),
        [pltpu.VMEM((4 * messages * CAP, half_cands, width), jnp.float32)],
        flops=8 * rows * model_width * width,
        moved=4 * model_width * width,
    )(sessions, own, keep_terms, got_terms, w_out, w_other, *returned)


def solution(mesh):
    placed = (
        P(("groups", "cache"), "serve", None),
        P(),
        P(None, None, "serve"),
        P("serve", None),
        P(("groups", "cache"), None, "serve"),
        P(("groups", "cache"), None, "serve"),
        P("groups", None),
        P("groups"),
        P("groups", None),
    )
    return jax.shard_map(
        body,
        mesh=mesh,
        in_specs=placed,
        out_specs=P(("groups", "cache"), "serve", None),
        check_vma=False,
    )
```

```python
import functools

import jax
import jax.numpy as jnp
from jax import lax
from jax.experimental import pallas as pl
from jax.experimental.pallas import tpu as pltpu
from jax.sharding import PartitionSpec as P

HD = 128
BLK = 64
CAP = 2
EPS = 1e-06
SCALE = HD ** (-0.5)
HIDE = -1e30
VMEM_LIMIT = 16 * 1024 * 1024

vmem = pl.BlockSpec(memory_space=pltpu.VMEM)
smem = pl.BlockSpec(memory_space=pltpu.SMEM)


def silu_of_half(half):
    return half + half * jnp.tanh(half)


def silu(x):
    return silu_of_half(x * 0.5)


def kernel_call(body, out_shape, in_specs, scratch_shapes=(), flops=0, moved=0):
    return pl.pallas_call(
        body,
        out_shape=out_shape,
        in_specs=in_specs,
        out_specs=jax.tree.map(lambda _: vmem, out_shape),
        scratch_shapes=scratch_shapes,
        cost_estimate=pl.CostEstimate(flops=flops, bytes_accessed=moved, transcendentals=0),
        compiler_params=pltpu.CompilerParams(vmem_limit_bytes=VMEM_LIMIT),
    )


def gain_row(gain_ref):
    gain = gain_ref[...].astype(jnp.float32)
    return jnp.concatenate([gain[at : at + 1] for at in range(gain.shape[0])], axis=1)


def normed_rows(rows_ref, gain):
    rows = rows_ref[...].astype(jnp.float32)
    rows = rows.reshape(-1, rows.shape[-1])
    mean_square = jnp.mean(rows * rows, axis=-1, keepdims=True)
    return (rows * lax.rsqrt(mean_square + EPS) * gain).astype(jnp.bfloat16)


def core_of(distance):
    parity = distance
    for shift in (16, 8, 4, 2, 1):
        parity = parity ^ (parity >> shift)
    return parity & 1


def position(distance, serve, owners):
    return jnp.where(core_of(distance) == serve, 0, owners // 2) + distance // 2


def own_slots(sess_ref, req_count):
    me = lax.axis_index("cache")
    base = me * req_count
    sessions = [sess_ref[base + request] for request in range(req_count)]
    slots = []
    for request in range(req_count):
        place = 0
        for earlier in range(request):
            place = place + (sessions[earlier] == sessions[request]).astype(jnp.int32)
        slots.append((sessions[request] ^ me, place))
    return slots


def front_kernel(owners, half_cands, facts_ref, hide_rows_ref, hide_cols_ref, chosen_ref, marks_ref):
    me, serve = lax.axis_index("cache"), lax.axis_index("serve")
    blocks, requests = facts_ref.shape[0] - 2, facts_ref.shape[1]
    per_owner = requests // owners
    rows = per_owner * half_cands
    hist_rows = hide_cols_ref.shape[0]
    at_row = lax.broadcasted_iota(jnp.int32, (hist_rows, HD), 0)
    at_lane = lax.broadcasted_iota(jnp.int32, (hist_rows, HD), 1)
    in_block = at_lane == at_row // BLK
    marks_ref[...] = jnp.zeros_like(marks_ref)

    sessions = facts_ref[blocks : blocks + 1, :]
    lane = lax.broadcasted_iota(jnp.int32, (1, requests), 1)
    place = jnp.zeros((1, requests), jnp.int32)
    for back in range(1, per_owner):
        same = (pltpu.roll(sessions, back, 1) == sessions) & (lane % per_owner >= back)
        place = place + same.astype(jnp.int32)

    distance = sessions ^ me
    code = jnp.where(core_of(distance) == serve, (distance // 2) * (2 * CAP) + place, owners * CAP)
    request = lax.broadcasted_iota(jnp.int32, (requests, 2 * rows), 0)
    column = lax.broadcasted_iota(jnp.int32, (requests, 2 * rows), 1)
    spread = (request == me * per_owner + (column % rows) // half_cands).astype(jnp.float32).astype(jnp.bfloat16)
    codes = jnp.broadcast_to(code, (8, requests)).astype(jnp.float32).astype(jnp.bfloat16)
    target = jnp.dot(codes, spread, preferred_element_type=jnp.float32)[:1].astype(jnp.int32)
    at = lax.broadcasted_iota(jnp.int32, chosen_ref.shape, 0)
    column = lax.broadcasted_iota(jnp.int32, chosen_ref.shape, 1)
    hit = (at // half_cands == target + (column // rows) * CAP) & (at % half_cands == column % half_cands)
    chosen_ref[...] = hit.astype(jnp.float32).astype(jnp.bfloat16)

    at = position((lane // per_owner) ^ me, serve, owners)
    slot_of = jnp.where(sessions == me, at * CAP + place, -1)
    slots = owners * CAP
    at_slot = lax.broadcasted_iota(jnp.int32, (slots, requests), 0)
    taken = (at_slot == slot_of).astype(jnp.float32).astype(jnp.bfloat16)
    marks_ref[:blocks, :] = facts_ref[:blocks, :].astype(jnp.float32).astype(jnp.bfloat16)
    seen = lax.dot_general(taken, marks_ref[...], (((1,), (1,)), ((), ())), preferred_element_type=jnp.float32)
    slot_lane = lax.broadcasted_iota(jnp.int32, (slots, HD), 1)
    hidden = jnp.where(slot_lane < blocks, (1.0 - seen) * HIDE, jnp.where(slot_lane == blocks, HIDE, 0.0))
    wide = jnp.broadcast_to(hidden.reshape(owners, 1, CAP, 1, HD), (owners, 2, CAP, half_cands, HD))
    hide_rows_ref[...] = wide.reshape(hide_rows_ref.shape).astype(jnp.bfloat16)
    lengths = facts_ref[blocks + 1 : blocks + 2, :]
    length = jnp.sum(jnp.where(lane == me, lengths, 0), axis=1, keepdims=True)
    hide_cols_ref[...] = jnp.where(in_block | ((at_lane == blocks) & (at_row >= length)), 1.0, 0.0).astype(jnp.bfloat16)


def message_kernel(chosen_ref, own_ref, other_ref, *out_refs):
    model_width = own_ref.shape[2]
    source = jnp.concatenate(
        [ref[...].astype(jnp.float32).reshape(-1, model_width) for ref in (own_ref, other_ref)], axis=0
    ).astype(jnp.bfloat16)
    rows = jnp.dot(chosen_ref[...], source, preferred_element_type=jnp.float32)
    piece = out_refs[0].shape[0]
    for at, out_ref in enumerate(out_refs):
        out_ref[...] = rows[at * piece : (at + 1) * piece].astype(jnp.bfloat16)


def self_kernel(own_ref, other_ref, gain_ref, w_ref, keep_ref, give_ref, normed_ref):
    rows, width = keep_ref.shape[1:]
    gain = gain_row(gain_ref)
    normed_ref[:rows, :] = normed_rows(own_ref, gain)
    normed_ref[rows:, :] = normed_rows(other_ref, gain)
    normed = normed_ref[...]

    def activated(part):
        return silu(jnp.dot(normed, w_ref[part], preferred_element_type=jnp.float32)).astype(jnp.bfloat16)

    products = activated(0).astype(jnp.float32) * activated(1).astype(jnp.float32)
    values, gates = activated(2), activated(3)
    for low in range(0, width, HD):
        score = jnp.sum(products[:, low : low + HD], axis=-1, keepdims=True) * SCALE
        term = (silu(score) * values[:, low : low + HD].astype(jnp.float32)).astype(jnp.bfloat16)
        keep_ref[0, :, low : low + HD] = term[:rows]
        give_ref[0, :, low : low + HD] = term[rows:]
    keep_ref[1] = gates[:rows]
    give_ref[1] = gates[rows:]


def pack_kernel(keep_ref, got_ref, *out_refs):
    part = out_refs[0].shape[0] // 4
    for at, out_ref in enumerate(out_refs):
        for side in range(2):
            low = (2 * at + side) * part
            out_ref[2 * side * part : (2 * side + 1) * part, :] = keep_ref[low : low + part, :]
            out_ref[(2 * side + 1) * part : (2 * side + 2) * part, :] = got_ref[low : low + part, :]


def history_kernel(owners, gain_ref, w_ref, hide_rows_ref, hide_cols_ref, keys_ref, values_ref, *refs):
    keep_ref, give_ref = refs[owners:]
    slot_refs = [None] * owners
    for at, order in enumerate(far_first(owners // 2)):
        slot_refs[order], slot_refs[owners // 2 + order] = refs[2 * at : 2 * at + 2]
    rows, width = keep_ref.shape
    per_owner = rows // (owners // 2)
    hist_rows = keys_ref.shape[0]
    span = min(256, hist_rows)
    per_step = max(1, min(owners, 256 // per_owner))
    gain = gain_row(gain_ref)
    for first in range(0, owners, per_step):
        group = range(first, min(first + per_step, owners))
        normed = jnp.concatenate([normed_rows(slot_refs[at], gain) for at in group], axis=0)
        queries = silu(jnp.dot(normed, w_ref[0], preferred_element_type=jnp.float32)).astype(jnp.bfloat16)
        hide_rows = hide_rows_ref[first * per_owner : first * per_owner + queries.shape[0], :]
        for low in range(0, width, HD):
            lhs = jnp.concatenate([queries[:, low : low + HD], hide_rows], axis=1)
            total = None
            for start in range(0, hist_rows, span):
                rhs = jnp.concatenate(
                    [keys_ref[start : start + span, low : low + HD], hide_cols_ref[start : start + span, :]], axis=1
                )
                scores = lax.dot_general(lhs, rhs, (((1,), (1,)), ((), ())), preferred_element_type=jnp.float32)
                weights = silu_of_half(scores * (0.5 * SCALE)).astype(jnp.bfloat16)
                term = jnp.dot(
                    weights, values_ref[start : start + span, low : low + HD], preferred_element_type=jnp.float32
                )
                total = term if total is None else total + term
            total = total.astype(jnp.bfloat16)
            for place, at in enumerate(group):
                out_ref, row = (keep_ref, at * per_owner) if at < owners // 2 else (give_ref, at * per_owner - rows)
                out_ref[row : row + per_owner, low : low + HD] = total[place * per_owner : (place + 1) * per_owner]


def output_kernel(messages, sess_ref, own_ref, keep_ref, got_ref, w_own_ref, w_other_ref, *refs):
    back_refs, (out_ref, table_ref) = refs[: 2 * messages], refs[2 * messages :]
    req_count, half_cands, model_width = own_ref.shape
    rows = req_count * half_cands
    width = model_width // 2
    serve = lax.axis_index("serve")
    part = CAP * half_cands
    for order, at in enumerate(far_first(messages)):
        for side in range(2):
            block = back_refs[2 * order + side][: 2 * part, :].astype(jnp.float32).reshape(2, CAP, half_cands, width)
            for heads in range(2):
                low = ((side * messages + at) * 2 + heads) * CAP
                table_ref[low : low + CAP] = block[heads if side == 0 else 1 - heads]
    own = own_slots(sess_ref, req_count)
    total = own_ref[...].astype(jnp.float32).reshape(rows, model_width)
    for heads, (terms_ref, w_ref) in enumerate(((keep_ref, w_own_ref), (got_ref, w_other_ref))):
        history = []
        for distance, place in own:
            side = jnp.where(core_of(distance) == serve, 0, messages)
            history.append(table_ref[((side + distance // 2) * 2 + heads) * CAP + place])
        attended = jnp.concatenate(history, axis=0) + terms_ref[0].astype(jnp.float32)
        gates = terms_ref[1].astype(jnp.float32)
        mixed = []
        for low in range(0, width, HD):
            head = attended[:, low : low + HD]
            level = lax.rsqrt(jnp.mean(head * head, axis=-1, keepdims=True) + EPS)
            mixed.append((head * level * gates[:, low : low + HD]).astype(jnp.bfloat16))
        total = total + jnp.dot(jnp.concatenate(mixed, axis=1), w_ref[...], preferred_element_type=jnp.float32)
    out_ref[...] = total.reshape(out_ref.shape).astype(jnp.bfloat16)


def far_first(count):
    return list(reversed(range(count)))


def swap(rows):
    return lax.ppermute(rows, "serve", [(0, 1), (1, 0)])


def cross(owners, messages):
    came = []
    for at in far_first(len(messages)):
        steps = [2 * at + side for side in range(2)]
        pairs = [(place * 2 + core_of(step), (place ^ step) * 2 + core_of(step)) for place in range(owners) for step in steps]
        came.append(lax.ppermute(messages[at], ("cache", "serve"), pairs))
    return came


def body(candidates, input_gain, w_in, w_out, hist_keys, hist_values, request_session, hist_len, block_mask):
    owners = lax.axis_size("cache")
    req_count, half_cands, model_width = candidates.shape
    width = w_in.shape[2]
    rows = req_count * half_cands
    hist_rows = hist_keys.shape[1]
    bf16 = functools.partial(jax.ShapeDtypeStruct, dtype=jnp.bfloat16)
    sessions = request_session.reshape(-1)
    gain = input_gain.reshape(-1, HD)
    messages = owners // 2
    piece = 2 * CAP * half_cands
    half_table = bf16((messages * piece, width))

    facts = jnp.concatenate(
        [
            block_mask.T,
            request_session.reshape(1, -1),
            jnp.pad(hist_len, (0, owners * (req_count - 1))).reshape(1, -1),
        ],
        axis=0,
    )
    hide_rows, hide_cols, chosen = kernel_call(
        functools.partial(front_kernel, owners, half_cands),
        [bf16((owners * piece, HD)), bf16((hist_rows, HD)), bf16((messages * piece, 2 * rows))],
        [vmem],
        [pltpu.VMEM((HD, owners * req_count), jnp.bfloat16)],
        flops=8 * messages * piece * model_width * width,
        moved=2 * hist_rows * HD,
    )(facts)
    other, w_out, chosen = lax.optimization_barrier((swap(candidates), w_out, chosen))
    w_other = swap(w_out)
    out = kernel_call(message_kernel, [bf16((piece, model_width))] * messages, [vmem] * 3)(chosen, candidates, other)
    out, w_in = lax.optimization_barrier((out, w_in))
    weights = jnp.transpose(w_in, (1, 0, 2))
    came = cross(owners, out)
    came, weights = lax.optimization_barrier((came, weights))
    swapped = [swap(message) for message in came]
    keep, give = kernel_call(
        functools.partial(history_kernel, owners),
        [half_table] * 2,
        [vmem] * (6 + owners),
        flops=8 * owners * piece * hist_rows * width,
        moved=4 * hist_rows * width,
    )(
        gain,
        weights,
        hide_rows,
        hide_cols,
        hist_keys.reshape(hist_rows, width),
        hist_values.reshape(hist_rows, width),
        *[rows_of for both in zip(came, swapped) for rows_of in both],
    )
    keep, give, w_other = lax.optimization_barrier((keep, give, w_other))
    out = kernel_call(pack_kernel, [bf16((2 * piece, width))] * messages, [vmem] * 2)(keep, swap(give))
    out, other = lax.optimization_barrier((out, other))
    backs = cross(owners, out)
    terms = kernel_call(
        self_kernel,
        [bf16((2, rows, width))] * 2,
        [vmem] * 4,
        [pltpu.VMEM((2 * rows, model_width), jnp.bfloat16)],
        flops=16 * rows * model_width * width,
        moved=8 * model_width * width,
    )(candidates, other, gain, weights)
    backs[0], (keep_terms, give_terms) = lax.optimization_barrier((backs[0], terms))
    returned = [rows_of for back in backs for rows_of in (back, swap(back[piece:]))]
    return kernel_call(
        functools.partial(output_kernel, messages),
        bf16((req_count, half_cands, model_width)),
        [smem] + [vmem] * (5 + 2 * messages),
        [pltpu.VMEM((4 * messages * CAP, half_cands, width), jnp.float32)],
        flops=8 * rows * model_width * width,
        moved=4 * model_width * width,
    )(sessions, candidates, keep_terms, swap(give_terms), w_out, w_other, *returned)


def solution(mesh):
    placed = (
        P(("groups", "cache"), "serve", None),
        P(),
        P(None, None, "serve"),
        P("serve", None),
        P(("groups", "cache"), None, "serve"),
        P(("groups", "cache"), None, "serve"),
        P("groups", None),
        P("groups"),
        P("groups", None),
    )
    return jax.shard_map(
        body,
        mesh=mesh,
        in_specs=placed,
        out_specs=P(("groups", "cache"), "serve", None),
        check_vma=False,
    )
```

```python
import functools

import jax
import jax.numpy as jnp
from jax import lax
from jax.experimental import pallas as pl
from jax.experimental.pallas import tpu as pltpu
from jax.sharding import PartitionSpec as P

HD = 128
BLK = 64
CAP = 2
EPS = 1e-06
SCALE = HD ** (-0.5)
HIDE = -1e30
VMEM_LIMIT = 16 * 1024 * 1024

vmem = pl.BlockSpec(memory_space=pltpu.VMEM)
smem = pl.BlockSpec(memory_space=pltpu.SMEM)


def silu_of_half(half):
    return half + half * jnp.tanh(half)


def silu(x):
    return silu_of_half(x * 0.5)


def kernel_call(body, out_shape, in_specs, scratch_shapes=(), flops=0, moved=0):
    return pl.pallas_call(
        body,
        out_shape=out_shape,
        in_specs=in_specs,
        out_specs=jax.tree.map(lambda _: vmem, out_shape),
        scratch_shapes=scratch_shapes,
        cost_estimate=pl.CostEstimate(flops=flops, bytes_accessed=moved, transcendentals=0),
        compiler_params=pltpu.CompilerParams(vmem_limit_bytes=VMEM_LIMIT),
    )


def gain_row(gain_ref):
    gain = gain_ref[...].astype(jnp.float32)
    return jnp.concatenate([gain[at : at + 1] for at in range(gain.shape[0])], axis=1)


def normed_rows(rows_ref, gain):
    rows = rows_ref[...].astype(jnp.float32)
    rows = rows.reshape(-1, rows.shape[-1])
    mean_square = jnp.mean(rows * rows, axis=-1, keepdims=True)
    return (rows * lax.rsqrt(mean_square + EPS) * gain).astype(jnp.bfloat16)


def core_of(distance):
    parity = distance
    for shift in (16, 8, 4, 2, 1):
        parity = parity ^ (parity >> shift)
    return parity & 1


def position(distance, serve, owners):
    return jnp.where(core_of(distance) == serve, 0, owners // 2) + distance // 2


def own_slots(sess_ref, req_count):
    me = lax.axis_index("cache")
    base = me * req_count
    sessions = [sess_ref[base + request] for request in range(req_count)]
    slots = []
    for request in range(req_count):
        place = 0
        for earlier in range(request):
            place = place + (sessions[earlier] == sessions[request]).astype(jnp.int32)
        slots.append((sessions[request] ^ me, place))
    return slots


def front_kernel(owners, half_cands, facts_ref, hide_rows_ref, hide_cols_ref, chosen_ref, marks_ref):
    me, serve = lax.axis_index("cache"), lax.axis_index("serve")
    blocks, requests = facts_ref.shape[0] - 2, facts_ref.shape[1]
    per_owner = requests // owners
    rows = per_owner * half_cands
    hist_rows = hide_cols_ref.shape[0]
    at_row = lax.broadcasted_iota(jnp.int32, (hist_rows, HD), 0)
    at_lane = lax.broadcasted_iota(jnp.int32, (hist_rows, HD), 1)
    in_block = at_lane == at_row // BLK
    marks_ref[...] = jnp.zeros_like(marks_ref)

    sessions = facts_ref[blocks : blocks + 1, :]
    lane = lax.broadcasted_iota(jnp.int32, (1, requests), 1)
    place = jnp.zeros((1, requests), jnp.int32)
    for back in range(1, per_owner):
        same = (pltpu.roll(sessions, back, 1) == sessions) & (lane % per_owner >= back)
        place = place + same.astype(jnp.int32)

    distance = sessions ^ me
    code = jnp.where(core_of(distance) == serve, (distance // 2) * (2 * CAP) + place, owners * CAP)
    request = lax.broadcasted_iota(jnp.int32, (requests, 2 * rows), 0)
    column = lax.broadcasted_iota(jnp.int32, (requests, 2 * rows), 1)
    spread = (request == me * per_owner + (column % rows) // half_cands).astype(jnp.float32).astype(jnp.bfloat16)
    codes = jnp.broadcast_to(code, (8, requests)).astype(jnp.float32).astype(jnp.bfloat16)
    target = jnp.dot(codes, spread, preferred_element_type=jnp.float32)[:1].astype(jnp.int32)
    at = lax.broadcasted_iota(jnp.int32, chosen_ref.shape, 0)
    column = lax.broadcasted_iota(jnp.int32, chosen_ref.shape, 1)
    hit = (at // half_cands == target + (column // rows) * CAP) & (at % half_cands == column % half_cands)
    chosen_ref[...] = hit.astype(jnp.float32).astype(jnp.bfloat16)

    at = position((lane // per_owner) ^ me, serve, owners)
    slot_of = jnp.where(sessions == me, at * CAP + place, -1)
    slots = owners * CAP
    at_slot = lax.broadcasted_iota(jnp.int32, (slots, requests), 0)
    taken = (at_slot == slot_of).astype(jnp.float32).astype(jnp.bfloat16)
    marks_ref[:blocks, :] = facts_ref[:blocks, :].astype(jnp.float32).astype(jnp.bfloat16)
    seen = lax.dot_general(taken, marks_ref[...], (((1,), (1,)), ((), ())), preferred_element_type=jnp.float32)
    slot_lane = lax.broadcasted_iota(jnp.int32, (slots, HD), 1)
    hidden = jnp.where(slot_lane < blocks, (1.0 - seen) * HIDE, jnp.where(slot_lane == blocks, HIDE, 0.0))
    wide = jnp.broadcast_to(hidden.reshape(owners, 1, CAP, 1, HD), (owners, 2, CAP, half_cands, HD))
    hide_rows_ref[...] = wide.reshape(hide_rows_ref.shape).astype(jnp.bfloat16)
    lengths = facts_ref[blocks + 1 : blocks + 2, :]
    length = jnp.sum(jnp.where(lane == me, lengths, 0), axis=1, keepdims=True)
    hide_cols_ref[...] = jnp.where(in_block | ((at_lane == blocks) & (at_row >= length)), 1.0, 0.0).astype(jnp.bfloat16)


def message_kernel(chosen_ref, own_ref, other_ref, *out_refs):
    model_width = own_ref.shape[2]
    source = jnp.concatenate(
        [ref[...].astype(jnp.float32).reshape(-1, model_width) for ref in (own_ref, other_ref)], axis=0
    ).astype(jnp.bfloat16)
    rows = jnp.dot(chosen_ref[...], source, preferred_element_type=jnp.float32)
    piece = out_refs[0].shape[0]
    for at, out_ref in enumerate(out_refs):
        out_ref[...] = rows[at * piece : (at + 1) * piece].astype(jnp.bfloat16)


def self_kernel(own_ref, other_ref, gain_ref, w_ref, keep_ref, give_ref, normed_ref):
    rows, width = keep_ref.shape[1:]
    gain = gain_row(gain_ref)
    normed_ref[:rows, :] = normed_rows(own_ref, gain)
    normed_ref[rows:, :] = normed_rows(other_ref, gain)
    normed = normed_ref[...]

    def activated(part):
        return silu(jnp.dot(normed, w_ref[part], preferred_element_type=jnp.float32)).astype(jnp.bfloat16)

    products = activated(0).astype(jnp.float32) * activated(1).astype(jnp.float32)
    values, gates = activated(2), activated(3)
    for low in range(0, width, HD):
        score = jnp.sum(products[:, low : low + HD], axis=-1, keepdims=True) * SCALE
        term = (silu(score) * values[:, low : low + HD].astype(jnp.float32)).astype(jnp.bfloat16)
        keep_ref[0, :, low : low + HD] = term[:rows]
        give_ref[0, :, low : low + HD] = term[rows:]
    keep_ref[1] = gates[:rows]
    give_ref[1] = gates[rows:]


def pack_kernel(keep_ref, got_ref, *out_refs):
    part = out_refs[0].shape[0] // 4
    for at, out_ref in enumerate(out_refs):
        for side in range(2):
            low = (2 * at + side) * part
            out_ref[2 * side * part : (2 * side + 1) * part, :] = keep_ref[low : low + part, :]
            out_ref[(2 * side + 1) * part : (2 * side + 2) * part, :] = got_ref[low : low + part, :]


def history_kernel(owners, gain_ref, w_ref, hide_rows_ref, hide_cols_ref, keys_ref, values_ref, *refs):
    keep_ref, give_ref = refs[owners:]
    slot_refs = [None] * owners
    for at, order in enumerate(far_first(owners // 2)):
        slot_refs[order], slot_refs[owners // 2 + order] = refs[2 * at : 2 * at + 2]
    rows, width = keep_ref.shape
    per_owner = rows // (owners // 2)
    hist_rows = keys_ref.shape[0]
    span = min(256, hist_rows)
    per_step = max(1, min(owners, 256 // per_owner))
    gain = gain_row(gain_ref)
    for first in range(0, owners, per_step):
        group = range(first, min(first + per_step, owners))
        normed = jnp.concatenate([normed_rows(slot_refs[at], gain) for at in group], axis=0)
        queries = silu(jnp.dot(normed, w_ref[0], preferred_element_type=jnp.float32)).astype(jnp.bfloat16)
        hide_rows = hide_rows_ref[first * per_owner : first * per_owner + queries.shape[0], :]
        for low in range(0, width, HD):
            lhs = jnp.concatenate([queries[:, low : low + HD], hide_rows], axis=1)
            total = None
            for start in range(0, hist_rows, span):
                rhs = jnp.concatenate(
                    [keys_ref[start : start + span, low : low + HD], hide_cols_ref[start : start + span, :]], axis=1
                )
                scores = lax.dot_general(lhs, rhs, (((1,), (1,)), ((), ())), preferred_element_type=jnp.float32)
                weights = silu_of_half(scores * (0.5 * SCALE)).astype(jnp.bfloat16)
                term = jnp.dot(
                    weights, values_ref[start : start + span, low : low + HD], preferred_element_type=jnp.float32
                )
                total = term if total is None else total + term
            total = total.astype(jnp.bfloat16)
            for place, at in enumerate(group):
                out_ref, row = (keep_ref, at * per_owner) if at < owners // 2 else (give_ref, at * per_owner - rows)
                out_ref[row : row + per_owner, low : low + HD] = total[place * per_owner : (place + 1) * per_owner]


def output_kernel(messages, sess_ref, own_ref, keep_ref, got_ref, w_own_ref, w_other_ref, *refs):
    back_refs, (out_ref, table_ref) = refs[: 2 * messages], refs[2 * messages :]
    req_count, half_cands, model_width = own_ref.shape
    rows = req_count * half_cands
    width = model_width // 2
    serve = lax.axis_index("serve")
    part = CAP * half_cands
    for order, at in enumerate(far_first(messages)):
        for side in range(2):
            block = back_refs[2 * order + side][: 2 * part, :].astype(jnp.float32).reshape(2, CAP, half_cands, width)
            for heads in range(2):
                low = ((side * messages + at) * 2 + heads) * CAP
                table_ref[low : low + CAP] = block[heads if side == 0 else 1 - heads]
    own = own_slots(sess_ref, req_count)
    total = own_ref[...].astype(jnp.float32).reshape(rows, model_width)
    for heads, (terms_ref, w_ref) in enumerate(((keep_ref, w_own_ref), (got_ref, w_other_ref))):
        history = []
        for distance, place in own:
            side = jnp.where(core_of(distance) == serve, 0, messages)
            history.append(table_ref[((side + distance // 2) * 2 + heads) * CAP + place])
        attended = jnp.concatenate(history, axis=0) + terms_ref[0].astype(jnp.float32)
        gates = terms_ref[1].astype(jnp.float32)
        mixed = []
        for low in range(0, width, HD):
            head = attended[:, low : low + HD]
            level = lax.rsqrt(jnp.mean(head * head, axis=-1, keepdims=True) + EPS)
            mixed.append((head * level * gates[:, low : low + HD]).astype(jnp.bfloat16))
        total = total + jnp.dot(jnp.concatenate(mixed, axis=1), w_ref[...], preferred_element_type=jnp.float32)
    out_ref[...] = total.reshape(out_ref.shape).astype(jnp.bfloat16)


def far_first(count):
    return list(reversed(range(count)))


def swap(rows):
    return lax.ppermute(rows, "serve", [(0, 1), (1, 0)])


def cross(owners, messages):
    came = []
    for at in far_first(len(messages)):
        steps = [2 * at + side for side in range(2)]
        pairs = [(place * 2 + core_of(step), (place ^ step) * 2 + core_of(step)) for place in range(owners) for step in steps]
        came.append(lax.ppermute(messages[at], ("cache", "serve"), pairs))
    return came


def body(candidates, input_gain, w_in, w_out, hist_keys, hist_values, request_session, hist_len, block_mask):
    owners = lax.axis_size("cache")
    req_count, half_cands, model_width = candidates.shape
    width = w_in.shape[2]
    rows = req_count * half_cands
    hist_rows = hist_keys.shape[1]
    bf16 = functools.partial(jax.ShapeDtypeStruct, dtype=jnp.bfloat16)
    sessions = request_session.reshape(-1)
    gain = input_gain.reshape(-1, HD)
    messages = owners // 2
    piece = 2 * CAP * half_cands
    half_table = bf16((messages * piece, width))

    facts = jnp.concatenate(
        [
            block_mask.T,
            request_session.reshape(1, -1),
            jnp.pad(hist_len, (0, owners * (req_count - 1))).reshape(1, -1),
        ],
        axis=0,
    )
    hide_rows, hide_cols, chosen = kernel_call(
        functools.partial(front_kernel, owners, half_cands),
        [bf16((owners * piece, HD)), bf16((hist_rows, HD)), bf16((messages * piece, 2 * rows))],
        [vmem],
        [pltpu.VMEM((HD, owners * req_count), jnp.bfloat16)],
        flops=8 * messages * piece * model_width * width,
        moved=2 * hist_rows * HD,
    )(facts)
    other, w_out, chosen = lax.optimization_barrier((swap(candidates), w_out, chosen))
    w_other = swap(w_out)
    out = kernel_call(message_kernel, [bf16((piece, model_width))] * messages, [vmem] * 3)(chosen, candidates, other)
    out, w_in = lax.optimization_barrier((out, w_in))
    weights = jnp.transpose(w_in, (1, 0, 2))
    came = cross(owners, out)
    came, weights = lax.optimization_barrier((came, weights))
    swapped = [swap(message) for message in came]
    keep, give = kernel_call(
        functools.partial(history_kernel, owners),
        [half_table] * 2,
        [vmem] * (6 + owners),
        flops=8 * owners * piece * hist_rows * width,
        moved=4 * hist_rows * width,
    )(
        gain,
        weights,
        hide_rows,
        hide_cols,
        hist_keys.reshape(hist_rows, width),
        hist_values.reshape(hist_rows, width),
        *[rows_of for both in zip(came, swapped) for rows_of in both],
    )
    keep, give, w_other = lax.optimization_barrier((keep, give, w_other))
    got = swap(give)
    terms = kernel_call(
        self_kernel,
        [bf16((2, rows, width))] * 2,
        [vmem] * 4,
        [pltpu.VMEM((2 * rows, model_width), jnp.bfloat16)],
        flops=16 * rows * model_width * width,
        moved=8 * model_width * width,
    )(candidates, lax.optimization_barrier((other, give))[0], gain, weights)
    got, (keep_terms, give_terms) = lax.optimization_barrier((got, terms))
    backs = cross(owners, kernel_call(pack_kernel, [bf16((2 * piece, width))] * messages, [vmem] * 2)(keep, got))
    returned = [rows_of for back in backs for rows_of in (back, swap(back[piece:]))]
    return kernel_call(
        functools.partial(output_kernel, messages),
        bf16((req_count, half_cands, model_width)),
        [smem] + [vmem] * (5 + 2 * messages),
        [pltpu.VMEM((4 * messages * CAP, half_cands, width), jnp.float32)],
        flops=8 * rows * model_width * width,
        moved=4 * model_width * width,
    )(sessions, candidates, keep_terms, swap(give_terms), w_out, w_other, *returned)


def solution(mesh):
    placed = (
        P(("groups", "cache"), "serve", None),
        P(),
        P(None, None, "serve"),
        P("serve", None),
        P(("groups", "cache"), None, "serve"),
        P(("groups", "cache"), None, "serve"),
        P("groups", None),
        P("groups"),
        P("groups", None),
    )
    return jax.shard_map(
        body,
        mesh=mesh,
        in_specs=placed,
        out_specs=P(("groups", "cache"), "serve", None),
        check_vma=False,
    )
```

```python
import functools

import jax
import jax.numpy as jnp
from jax import lax
from jax.experimental import pallas as pl
from jax.experimental.pallas import tpu as pltpu
from jax.sharding import PartitionSpec as P

HD = 128
BLK = 64
CAP = 2
EPS = 1e-06
SCALE = HD ** (-0.5)
HIDE = -1e30
VMEM_LIMIT = 16 * 1024 * 1024

vmem = pl.BlockSpec(memory_space=pltpu.VMEM)
smem = pl.BlockSpec(memory_space=pltpu.SMEM)


def silu_of_half(half):
    return half + half * jnp.tanh(half)


def silu(x):
    return silu_of_half(x * 0.5)


def kernel_call(body, out_shape, in_specs, scratch_shapes=(), flops=0, moved=0):
    return pl.pallas_call(
        body,
        out_shape=out_shape,
        in_specs=in_specs,
        out_specs=jax.tree.map(lambda _: vmem, out_shape),
        scratch_shapes=scratch_shapes,
        cost_estimate=pl.CostEstimate(flops=flops, bytes_accessed=moved, transcendentals=0),
        compiler_params=pltpu.CompilerParams(vmem_limit_bytes=VMEM_LIMIT),
    )


def gain_row(gain_ref):
    gain = gain_ref[...].astype(jnp.float32)
    return jnp.concatenate([gain[at : at + 1] for at in range(gain.shape[0])], axis=1)


def normed_rows(rows_ref, gain):
    rows = rows_ref[...].astype(jnp.float32)
    rows = rows.reshape(-1, rows.shape[-1])
    mean_square = jnp.mean(rows * rows, axis=-1, keepdims=True)
    return (rows * lax.rsqrt(mean_square + EPS) * gain).astype(jnp.bfloat16)


def core_of(distance):
    parity = distance
    for shift in (16, 8, 4, 2, 1):
        parity = parity ^ (parity >> shift)
    return parity & 1


def position(distance, serve, owners):
    return jnp.where(core_of(distance) == serve, 0, owners // 2) + distance // 2


def own_slots(sess_ref, req_count):
    me = lax.axis_index("cache")
    base = me * req_count
    sessions = [sess_ref[base + request] for request in range(req_count)]
    slots = []
    for request in range(req_count):
        place = 0
        for earlier in range(request):
            place = place + (sessions[earlier] == sessions[request]).astype(jnp.int32)
        slots.append((sessions[request] ^ me, place))
    return slots


def places(sessions, per_owner):
    lane = lax.broadcasted_iota(jnp.int32, sessions.shape, 1)
    place = jnp.zeros_like(sessions)
    for back in range(1, per_owner):
        same = (pltpu.roll(sessions, back, 1) == sessions) & (lane % per_owner >= back)
        place = place + same.astype(jnp.int32)
    return place


def front_kernel(owners, half_cands, sess_ref, chosen_ref):
    me, serve = lax.axis_index("cache"), lax.axis_index("serve")
    sessions = sess_ref[...]
    requests = sessions.shape[1]
    per_owner = requests // owners
    rows = per_owner * half_cands
    distance = sessions ^ me
    first = distance // 2 * (2 * CAP)
    code = jnp.where(core_of(distance) == serve, first + places(sessions, per_owner), owners * CAP)
    request = lax.broadcasted_iota(jnp.int32, (requests, 2 * rows), 0)
    column = lax.broadcasted_iota(jnp.int32, (requests, 2 * rows), 1)
    spread = (request == me * per_owner + (column % rows) // half_cands).astype(jnp.float32).astype(jnp.bfloat16)
    codes = jnp.broadcast_to(code, (8, requests)).astype(jnp.float32).astype(jnp.bfloat16)
    target = jnp.dot(codes, spread, preferred_element_type=jnp.float32)[:1].astype(jnp.int32)
    at = lax.broadcasted_iota(jnp.int32, chosen_ref.shape, 0)
    column = lax.broadcasted_iota(jnp.int32, chosen_ref.shape, 1)
    hit = (at // half_cands == target + (column // rows) * CAP) & (at % half_cands == column % half_cands)
    chosen_ref[...] = hit.astype(jnp.float32).astype(jnp.bfloat16)


def visible_kernel(sess_ref, len_ref, mask_ref, hide_rows_ref, hide_cols_ref, marks_ref):
    me, serve = lax.axis_index("cache"), lax.axis_index("serve")
    blocks, requests = mask_ref.shape
    owners = len_ref.shape[1]
    per_owner = requests // owners
    sessions = sess_ref[...]
    lane = lax.broadcasted_iota(jnp.int32, (1, requests), 1)
    at = position((lane // per_owner) ^ me, serve, owners)
    slot_of = jnp.where(sessions == me, at * CAP + places(sessions, per_owner), -1)
    slots = owners * CAP
    at_slot = lax.broadcasted_iota(jnp.int32, (slots, requests), 0)
    taken = (at_slot == slot_of).astype(jnp.float32).astype(jnp.bfloat16)
    marks_ref[...] = jnp.zeros_like(marks_ref)
    marks_ref[:blocks, :] = mask_ref[...].astype(jnp.float32).astype(jnp.bfloat16)
    seen = lax.dot_general(taken, marks_ref[...], (((1,), (1,)), ((), ())), preferred_element_type=jnp.float32)
    slot_lane = lax.broadcasted_iota(jnp.int32, (slots, HD), 1)
    hidden = jnp.where(slot_lane < blocks, (1.0 - seen) * HIDE, jnp.where(slot_lane == blocks, HIDE, 0.0))
    half = hide_rows_ref.shape[0] // slots // 2
    wide = jnp.broadcast_to(hidden.reshape(owners, 1, CAP, 1, HD), (owners, 2, CAP, half, HD))
    hide_rows_ref[...] = wide.reshape(hide_rows_ref.shape).astype(jnp.bfloat16)
    hist_rows = hide_cols_ref.shape[0]
    owner_lane = lax.broadcasted_iota(jnp.int32, (1, owners), 1)
    length = jnp.sum(jnp.where(owner_lane == me, len_ref[...], 0), axis=1, keepdims=True)
    at_row = lax.broadcasted_iota(jnp.int32, (hist_rows, HD), 0)
    at_lane = lax.broadcasted_iota(jnp.int32, (hist_rows, HD), 1)
    hide_cols_ref[...] = jnp.where(
        (at_lane == at_row // BLK) | ((at_lane == blocks) & (at_row >= length)), 1.0, 0.0
    ).astype(jnp.bfloat16)


def message_kernel(chosen_ref, own_ref, other_ref, *out_refs):
    model_width = own_ref.shape[2]
    source = jnp.concatenate(
        [ref[...].astype(jnp.float32).reshape(-1, model_width) for ref in (own_ref, other_ref)], axis=0
    ).astype(jnp.bfloat16)
    rows = jnp.dot(chosen_ref[...], source, preferred_element_type=jnp.float32)
    piece = out_refs[0].shape[0]
    for at, out_ref in enumerate(out_refs):
        out_ref[...] = rows[at * piece : (at + 1) * piece].astype(jnp.bfloat16)


def self_kernel(own_ref, other_ref, gain_ref, w_ref, keep_ref, give_ref, normed_ref):
    rows, width = keep_ref.shape[1:]
    gain = gain_row(gain_ref)
    normed_ref[:rows, :] = normed_rows(own_ref, gain)
    normed_ref[rows:, :] = normed_rows(other_ref, gain)
    normed = normed_ref[...]

    def activated(part):
        return silu(jnp.dot(normed, w_ref[part], preferred_element_type=jnp.float32)).astype(jnp.bfloat16)

    products = activated(0).astype(jnp.float32) * activated(1).astype(jnp.float32)
    values, gates = activated(2), activated(3)
    for low in range(0, width, HD):
        score = jnp.sum(products[:, low : low + HD], axis=-1, keepdims=True) * SCALE
        term = (silu(score) * values[:, low : low + HD].astype(jnp.float32)).astype(jnp.bfloat16)
        keep_ref[0, :, low : low + HD] = term[:rows]
        give_ref[0, :, low : low + HD] = term[rows:]
    keep_ref[1] = gates[:rows]
    give_ref[1] = gates[rows:]


def pack_kernel(keep_ref, got_ref, *out_refs):
    part = out_refs[0].shape[0] // 4
    for at, out_ref in enumerate(out_refs):
        for side in range(2):
            low = (2 * at + side) * part
            out_ref[2 * side * part : (2 * side + 1) * part, :] = keep_ref[low : low + part, :]
            out_ref[(2 * side + 1) * part : (2 * side + 2) * part, :] = got_ref[low : low + part, :]


def history_kernel(owners, gain_ref, w_ref, hide_rows_ref, hide_cols_ref, keys_ref, values_ref, *refs):
    keep_ref, give_ref = refs[owners:]
    slot_refs = [None] * owners
    for at, order in enumerate(far_first(owners // 2)):
        slot_refs[order], slot_refs[owners // 2 + order] = refs[2 * at : 2 * at + 2]
    rows, width = keep_ref.shape
    per_owner = rows // (owners // 2)
    hist_rows = keys_ref.shape[0]
    span = min(256, hist_rows)
    per_step = max(1, min(owners, 256 // per_owner))
    gain = gain_row(gain_ref)
    for first in range(0, owners, per_step):
        group = range(first, min(first + per_step, owners))
        normed = jnp.concatenate([normed_rows(slot_refs[at], gain) for at in group], axis=0)
        queries = silu(jnp.dot(normed, w_ref[0], preferred_element_type=jnp.float32)).astype(jnp.bfloat16)
        hide_rows = hide_rows_ref[first * per_owner : first * per_owner + queries.shape[0], :]
        for low in range(0, width, HD):
            lhs = jnp.concatenate([queries[:, low : low + HD], hide_rows], axis=1)
            total = None
            for start in range(0, hist_rows, span):
                rhs = jnp.concatenate(
                    [keys_ref[start : start + span, low : low + HD], hide_cols_ref[start : start + span, :]], axis=1
                )
                scores = lax.dot_general(lhs, rhs, (((1,), (1,)), ((), ())), preferred_element_type=jnp.float32)
                weights = silu_of_half(scores * (0.5 * SCALE)).astype(jnp.bfloat16)
                term = jnp.dot(
                    weights, values_ref[start : start + span, low : low + HD], preferred_element_type=jnp.float32
                )
                total = term if total is None else total + term
            total = total.astype(jnp.bfloat16)
            for place, at in enumerate(group):
                out_ref, row = (keep_ref, at * per_owner) if at < owners // 2 else (give_ref, at * per_owner - rows)
                out_ref[row : row + per_owner, low : low + HD] = total[place * per_owner : (place + 1) * per_owner]


def output_kernel(messages, sess_ref, own_ref, keep_ref, got_ref, w_own_ref, w_other_ref, *refs):
    back_refs, (out_ref, table_ref) = refs[: 2 * messages], refs[2 * messages :]
    req_count, half_cands, model_width = own_ref.shape
    rows = req_count * half_cands
    width = model_width // 2
    serve = lax.axis_index("serve")
    part = CAP * half_cands
    for order, at in enumerate(far_first(messages)):
        for side in range(2):
            block = back_refs[2 * order + side][: 2 * part, :].astype(jnp.float32).reshape(2, CAP, half_cands, width)
            for heads in range(2):
                low = ((side * messages + at) * 2 + heads) * CAP
                table_ref[low : low + CAP] = block[heads if side == 0 else 1 - heads]
    own = own_slots(sess_ref, req_count)
    total = own_ref[...].astype(jnp.float32).reshape(rows, model_width)
    for heads, (terms_ref, w_ref) in enumerate(((keep_ref, w_own_ref), (got_ref, w_other_ref))):
        history = []
        for distance, place in own:
            side = jnp.where(core_of(distance) == serve, 0, messages)
            history.append(table_ref[((side + distance // 2) * 2 + heads) * CAP + place])
        attended = jnp.concatenate(history, axis=0) + terms_ref[0].astype(jnp.float32)
        gates = terms_ref[1].astype(jnp.float32)
        mixed = []
        for low in range(0, width, HD):
            head = attended[:, low : low + HD]
            level = lax.rsqrt(jnp.mean(head * head, axis=-1, keepdims=True) + EPS)
            mixed.append((head * level * gates[:, low : low + HD]).astype(jnp.bfloat16))
        total = total + jnp.dot(jnp.concatenate(mixed, axis=1), w_ref[...], preferred_element_type=jnp.float32)
    out_ref[...] = total.reshape(out_ref.shape).astype(jnp.bfloat16)


def far_first(count):
    return list(reversed(range(count)))


def swap(rows):
    return lax.ppermute(rows, "serve", [(0, 1), (1, 0)])


def cross(owners, messages):
    came = []
    for at in far_first(len(messages)):
        steps = [2 * at + side for side in range(2)]
        pairs = [(place * 2 + core_of(step), (place ^ step) * 2 + core_of(step)) for place in range(owners) for step in steps]
        came.append(lax.ppermute(messages[at], ("cache", "serve"), pairs))
    return came


def body(candidates, input_gain, w_in, w_out, hist_keys, hist_values, request_session, hist_len, block_mask):
    owners = lax.axis_size("cache")
    req_count, half_cands, model_width = candidates.shape
    width = w_in.shape[2]
    rows = req_count * half_cands
    hist_rows = hist_keys.shape[1]
    bf16 = functools.partial(jax.ShapeDtypeStruct, dtype=jnp.bfloat16)
    sessions = request_session.reshape(-1)
    gain = input_gain.reshape(-1, HD)
    messages = owners // 2
    piece = 2 * CAP * half_cands
    half_table = bf16((messages * piece, width))

    session_row = request_session.reshape(1, -1)
    chosen = kernel_call(
        functools.partial(front_kernel, owners, half_cands),
        bf16((messages * piece, 2 * rows)),
        [vmem],
    )(session_row)
    other, w_out, chosen = lax.optimization_barrier((swap(candidates), w_out, chosen))
    w_other = swap(w_out)
    out = kernel_call(message_kernel, [bf16((piece, model_width))] * messages, [vmem] * 3)(chosen, candidates, other)
    out, w_in = lax.optimization_barrier((out, w_in))
    weights = jnp.transpose(w_in, (1, 0, 2))
    came = cross(owners, out)
    visible = kernel_call(
        visible_kernel,
        [bf16((owners * piece, HD)), bf16((hist_rows, HD))],
        [vmem] * 3,
        [pltpu.VMEM((HD, owners * req_count), jnp.bfloat16)],
    )(session_row, hist_len.reshape(1, -1), lax.optimization_barrier((block_mask.T, out))[0])
    came, weights, (hide_rows, hide_cols) = lax.optimization_barrier((came, weights, visible))
    swapped = [swap(message) for message in came]
    keep, give = kernel_call(
        functools.partial(history_kernel, owners),
        [half_table] * 2,
        [vmem] * (6 + owners),
        flops=8 * owners * piece * hist_rows * width,
        moved=4 * hist_rows * width,
    )(
        gain,
        weights,
        hide_rows,
        hide_cols,
        hist_keys.reshape(hist_rows, width),
        hist_values.reshape(hist_rows, width),
        *[rows_of for both in zip(came, swapped) for rows_of in both],
    )
    keep, give, w_other = lax.optimization_barrier((keep, give, w_other))
    got = swap(give)
    terms = kernel_call(
        self_kernel,
        [bf16((2, rows, width))] * 2,
        [vmem] * 4,
        [pltpu.VMEM((2 * rows, model_width), jnp.bfloat16)],
        flops=16 * rows * model_width * width,
        moved=8 * model_width * width,
    )(candidates, lax.optimization_barrier((other, give))[0], gain, weights)
    got, (keep_terms, give_terms) = lax.optimization_barrier((got, terms))
    backs = cross(owners, kernel_call(pack_kernel, [bf16((2 * piece, width))] * messages, [vmem] * 2)(keep, got))
    returned = [rows_of for back in backs for rows_of in (back, swap(back[piece:]))]
    return kernel_call(
        functools.partial(output_kernel, messages),
        bf16((req_count, half_cands, model_width)),
        [smem] + [vmem] * (5 + 2 * messages),
        [pltpu.VMEM((4 * messages * CAP, half_cands, width), jnp.float32)],
        flops=8 * rows * model_width * width,
        moved=4 * model_width * width,
    )(sessions, candidates, keep_terms, swap(give_terms), w_out, w_other, *returned)


def solution(mesh):
    placed = (
        P(("groups", "cache"), "serve", None),
        P(),
        P(None, None, "serve"),
        P("serve", None),
        P(("groups", "cache"), None, "serve"),
        P(("groups", "cache"), None, "serve"),
        P("groups", None),
        P("groups"),
        P("groups", None),
    )
    return jax.shard_map(
        body,
        mesh=mesh,
        in_specs=placed,
        out_specs=P(("groups", "cache"), "serve", None),
        check_vma=False,
    )
```

```python
import functools

import jax
import jax.numpy as jnp
from jax import lax
from jax.experimental import pallas as pl
from jax.experimental.pallas import tpu as pltpu
from jax.sharding import PartitionSpec as P

HD = 128
BLK = 64
CAP = 2
EPS = 1e-06
SCALE = HD ** (-0.5)
HIDE = -1e30
VMEM_LIMIT = 16 * 1024 * 1024

vmem = pl.BlockSpec(memory_space=pltpu.VMEM)
smem = pl.BlockSpec(memory_space=pltpu.SMEM)


def silu_of_half(half):
    return half + half * jnp.tanh(half)


def silu(x):
    return silu_of_half(x * 0.5)


def kernel_call(body, out_shape, in_specs, scratch_shapes=(), flops=0, moved=0):
    return pl.pallas_call(
        body,
        out_shape=out_shape,
        in_specs=in_specs,
        out_specs=jax.tree.map(lambda _: vmem, out_shape),
        scratch_shapes=scratch_shapes,
        cost_estimate=pl.CostEstimate(flops=flops, bytes_accessed=moved, transcendentals=0),
        compiler_params=pltpu.CompilerParams(vmem_limit_bytes=VMEM_LIMIT),
    )


def gain_row(gain_ref):
    gain = gain_ref[...].astype(jnp.float32)
    return jnp.concatenate([gain[at : at + 1] for at in range(gain.shape[0])], axis=1)


def normed_rows(rows_ref, gain):
    rows = rows_ref[...].astype(jnp.float32)
    rows = rows.reshape(-1, rows.shape[-1])
    mean_square = jnp.mean(rows * rows, axis=-1, keepdims=True)
    return (rows * lax.rsqrt(mean_square + EPS) * gain).astype(jnp.bfloat16)


def core_of(distance):
    parity = distance
    for shift in (16, 8, 4, 2, 1):
        parity = parity ^ (parity >> shift)
    return parity & 1


def position(distance, serve, owners):
    far = jnp.where(core_of(distance) == serve, 0, owners // 2 - 1) + distance // 2 + 1
    return jnp.where(distance < 2, distance, far)


def own_slots(sess_ref, req_count):
    me = lax.axis_index("cache")
    base = me * req_count
    sessions = [sess_ref[base + request] for request in range(req_count)]
    slots = []
    for request in range(req_count):
        place = 0
        for earlier in range(request):
            place = place + (sessions[earlier] == sessions[request]).astype(jnp.int32)
        slots.append((sessions[request] ^ me, place))
    return slots


def places(sessions, per_owner):
    lane = lax.broadcasted_iota(jnp.int32, sessions.shape, 1)
    place = jnp.zeros_like(sessions)
    for back in range(1, per_owner):
        same = (pltpu.roll(sessions, back, 1) == sessions) & (lane % per_owner >= back)
        place = place + same.astype(jnp.int32)
    return place


def front_kernel(owners, half_cands, sess_ref, chosen_ref):
    me, serve = lax.axis_index("cache"), lax.axis_index("serve")
    sessions = sess_ref[...]
    requests = sessions.shape[1]
    per_owner = requests // owners
    rows = per_owner * half_cands
    distance = sessions ^ me
    at = position(distance, serve, owners)
    sent = at <= owners // 2
    code = jnp.where(sent, at * (2 * CAP) + places(sessions, per_owner), owners * (2 * CAP))
    request = lax.broadcasted_iota(jnp.int32, (requests, 2 * rows), 0)
    column = lax.broadcasted_iota(jnp.int32, (requests, 2 * rows), 1)
    spread = (request == me * per_owner + (column % rows) // half_cands).astype(jnp.float32).astype(jnp.bfloat16)
    codes = jnp.broadcast_to(code, (8, requests)).astype(jnp.float32).astype(jnp.bfloat16)
    target = jnp.dot(codes, spread, preferred_element_type=jnp.float32)[:1].astype(jnp.int32)
    at = lax.broadcasted_iota(jnp.int32, chosen_ref.shape, 0)
    column = lax.broadcasted_iota(jnp.int32, chosen_ref.shape, 1)
    hit = (at // half_cands == target + (column // rows) * CAP) & (at % half_cands == column % half_cands)
    chosen_ref[...] = hit.astype(jnp.float32).astype(jnp.bfloat16)


def visible_kernel(sess_ref, len_ref, mask_ref, hide_rows_ref, hide_cols_ref, marks_ref):
    me, serve = lax.axis_index("cache"), lax.axis_index("serve")
    blocks, requests = mask_ref.shape
    owners = len_ref.shape[1]
    per_owner = requests // owners
    sessions = sess_ref[...]
    lane = lax.broadcasted_iota(jnp.int32, (1, requests), 1)
    at = position((lane // per_owner) ^ me, serve, owners)
    slot_of = jnp.where(sessions == me, at * CAP + places(sessions, per_owner), -1)
    slots = owners * CAP
    at_slot = lax.broadcasted_iota(jnp.int32, (slots, requests), 0)
    taken = (at_slot == slot_of).astype(jnp.float32).astype(jnp.bfloat16)
    marks_ref[...] = jnp.zeros_like(marks_ref)
    marks_ref[:blocks, :] = mask_ref[...].astype(jnp.float32).astype(jnp.bfloat16)
    seen = lax.dot_general(taken, marks_ref[...], (((1,), (1,)), ((), ())), preferred_element_type=jnp.float32)
    slot_lane = lax.broadcasted_iota(jnp.int32, (slots, HD), 1)
    hidden = jnp.where(slot_lane < blocks, (1.0 - seen) * HIDE, jnp.where(slot_lane == blocks, HIDE, 0.0))
    half = hide_rows_ref.shape[0] // slots // 2
    wide = jnp.broadcast_to(hidden.reshape(owners, 1, CAP, 1, HD), (owners, 2, CAP, half, HD))
    hide_rows_ref[...] = wide.reshape(hide_rows_ref.shape).astype(jnp.bfloat16)
    hist_rows = hide_cols_ref.shape[0]
    owner_lane = lax.broadcasted_iota(jnp.int32, (1, owners), 1)
    length = jnp.sum(jnp.where(owner_lane == me, len_ref[...], 0), axis=1, keepdims=True)
    at_row = lax.broadcasted_iota(jnp.int32, (hist_rows, HD), 0)
    at_lane = lax.broadcasted_iota(jnp.int32, (hist_rows, HD), 1)
    hide_cols_ref[...] = jnp.where(
        (at_lane == at_row // BLK) | ((at_lane == blocks) & (at_row >= length)), 1.0, 0.0
    ).astype(jnp.bfloat16)


def message_kernel(chosen_ref, own_ref, other_ref, *out_refs):
    model_width = own_ref.shape[2]
    source = jnp.concatenate(
        [ref[...].astype(jnp.float32).reshape(-1, model_width) for ref in (own_ref, other_ref)], axis=0
    ).astype(jnp.bfloat16)
    rows = jnp.dot(chosen_ref[...], source, preferred_element_type=jnp.float32)
    piece = out_refs[0].shape[0]
    for at, out_ref in enumerate(out_refs):
        out_ref[...] = rows[at * piece : (at + 1) * piece].astype(jnp.bfloat16)


def self_kernel(own_ref, other_ref, gain_ref, w_ref, keep_ref, give_ref, normed_ref):
    rows, width = keep_ref.shape[1:]
    gain = gain_row(gain_ref)
    normed_ref[:rows, :] = normed_rows(own_ref, gain)
    normed_ref[rows:, :] = normed_rows(other_ref, gain)
    normed = normed_ref[...]

    def activated(part):
        return silu(jnp.dot(normed, w_ref[part], preferred_element_type=jnp.float32)).astype(jnp.bfloat16)

    products = activated(0).astype(jnp.float32) * activated(1).astype(jnp.float32)
    values, gates = activated(2), activated(3)
    for low in range(0, width, HD):
        score = jnp.sum(products[:, low : low + HD], axis=-1, keepdims=True) * SCALE
        term = (silu(score) * values[:, low : low + HD].astype(jnp.float32)).astype(jnp.bfloat16)
        keep_ref[0, :, low : low + HD] = term[:rows]
        give_ref[0, :, low : low + HD] = term[rows:]
    keep_ref[1] = gates[:rows]
    give_ref[1] = gates[rows:]


def pack_kernel(keep_ref, got_ref, *out_refs):
    part = out_refs[0].shape[0] // 4
    for at, out_ref in enumerate(out_refs):
        for side in range(2):
            low = (2 * at + side) * part
            out_ref[2 * side * part : (2 * side + 1) * part, :] = keep_ref[low : low + part, :]
            out_ref[(2 * side + 1) * part : (2 * side + 2) * part, :] = got_ref[low : low + part, :]


def history_kernel(owners, gain_ref, w_ref, hide_rows_ref, hide_cols_ref, keys_ref, values_ref, *refs):
    slot_refs, (local_ref, near_ref, keep_ref, give_ref) = refs[:owners], refs[owners:]
    width = near_ref.shape[1]
    per_owner = near_ref.shape[0]
    half = per_owner // 2
    far = [(ref, at * per_owner, 0, per_owner) for ref in (keep_ref, give_ref) for at in range(owners // 2 - 1)]
    local = [(local_ref, 0, 0, half), (give_ref, (owners // 2 - 1) * per_owner, half, half)]
    targets = [local, [(near_ref, 0, 0, per_owner)]] + [[target] for target in far]
    hist_rows = keys_ref.shape[0]
    span = min(256, hist_rows)
    per_step = max(1, min(owners, 256 // per_owner))
    gain = gain_row(gain_ref)
    for first in range(0, owners, per_step):
        group = range(first, min(first + per_step, owners))
        normed = jnp.concatenate([normed_rows(slot_refs[at], gain) for at in group], axis=0)
        queries = silu(jnp.dot(normed, w_ref[0], preferred_element_type=jnp.float32)).astype(jnp.bfloat16)
        hide_rows = hide_rows_ref[first * per_owner : first * per_owner + queries.shape[0], :]
        for low in range(0, width, HD):
            lhs = jnp.concatenate([queries[:, low : low + HD], hide_rows], axis=1)
            total = None
            for start in range(0, hist_rows, span):
                rhs = jnp.concatenate(
                    [keys_ref[start : start + span, low : low + HD], hide_cols_ref[start : start + span, :]], axis=1
                )
                scores = lax.dot_general(lhs, rhs, (((1,), (1,)), ((), ())), preferred_element_type=jnp.float32)
                weights = silu_of_half(scores * (0.5 * SCALE)).astype(jnp.bfloat16)
                term = jnp.dot(
                    weights, values_ref[start : start + span, low : low + HD], preferred_element_type=jnp.float32
                )
                total = term if total is None else total + term
            total = total.astype(jnp.bfloat16)
            for place, at in enumerate(group):
                for out_ref, row, start, count in targets[at]:
                    low_row = place * per_owner + start
                    out_ref[row : row + count, low : low + HD] = total[low_row : low_row + count]


def output_kernel(owners, sess_ref, own_ref, keep_ref, got_ref, w_own_ref, w_other_ref, *refs):
    local_ref, given_ref, near_ref, their_near_ref, *back_refs = refs[:-2]
    out_ref, table_ref = refs[-2:]
    req_count, half_cands, model_width = own_ref.shape
    rows = req_count * half_cands
    width = model_width // 2
    serve = lax.axis_index("serve")
    part = CAP * half_cands
    messages = owners // 2 - 1

    def store(at, heads, block):
        table_ref[(at * 2 + heads) * CAP : (at * 2 + heads + 1) * CAP] = block.reshape(CAP, half_cands, width)

    store(0, 0, local_ref[...].astype(jnp.float32))
    store(0, 1, given_ref[given_ref.shape[0] - part :, :].astype(jnp.float32))
    store(1, 0, near_ref[:part, :].astype(jnp.float32))
    store(1, 1, their_near_ref[...].astype(jnp.float32))
    for order, at in enumerate(far_first(messages)):
        for side in range(2):
            block = back_refs[2 * order + side][: 2 * part, :].astype(jnp.float32)
            for heads in range(2):
                source = heads if side == 0 else 1 - heads
                store(2 + side * messages + at, heads, block[source * part : (source + 1) * part])
    own = own_slots(sess_ref, req_count)
    total = own_ref[...].astype(jnp.float32).reshape(rows, model_width)
    for heads, (terms_ref, w_ref) in enumerate(((keep_ref, w_own_ref), (got_ref, w_other_ref))):
        history = []
        for distance, place in own:
            history.append(table_ref[(position(distance, serve, owners) * 2 + heads) * CAP + place])
        attended = jnp.concatenate(history, axis=0) + terms_ref[0].astype(jnp.float32)
        gates = terms_ref[1].astype(jnp.float32)
        mixed = []
        for low in range(0, width, HD):
            head = attended[:, low : low + HD]
            level = lax.rsqrt(jnp.mean(head * head, axis=-1, keepdims=True) + EPS)
            mixed.append((head * level * gates[:, low : low + HD]).astype(jnp.bfloat16))
        total = total + jnp.dot(jnp.concatenate(mixed, axis=1), w_ref[...], preferred_element_type=jnp.float32)
    out_ref[...] = total.reshape(out_ref.shape).astype(jnp.bfloat16)


def far_first(count):
    return list(reversed(range(count)))


def swap(rows):
    return lax.ppermute(rows, "serve", [(0, 1), (1, 0)])


def cross(owners, messages):
    came = []
    for at in far_first(len(messages)):
        steps = [2 * (at + 1) + side for side in range(2)]
        pairs = [(place * 2 + core_of(step), (place ^ step) * 2 + core_of(step)) for place in range(owners) for step in steps]
        came.append(lax.ppermute(messages[at], ("cache", "serve"), pairs))
    return came


def to_neighbour(owners, rows):
    return lax.ppermute(rows, "cache", [(place, place ^ 1) for place in range(owners)])


def body(candidates, input_gain, w_in, w_out, hist_keys, hist_values, request_session, hist_len, block_mask):
    owners = lax.axis_size("cache")
    req_count, half_cands, model_width = candidates.shape
    width = w_in.shape[2]
    rows = req_count * half_cands
    hist_rows = hist_keys.shape[1]
    bf16 = functools.partial(jax.ShapeDtypeStruct, dtype=jnp.bfloat16)
    sessions = request_session.reshape(-1)
    gain = input_gain.reshape(-1, HD)
    messages = owners // 2 - 1
    piece = 2 * CAP * half_cands

    session_row = request_session.reshape(1, -1)
    chosen = kernel_call(
        functools.partial(front_kernel, owners, half_cands),
        bf16(((messages + 2) * piece, 2 * rows)),
        [vmem],
    )(session_row)
    other, w_out, chosen = lax.optimization_barrier((swap(candidates), w_out, chosen))
    w_other = swap(w_out)
    out = kernel_call(message_kernel, [bf16((piece, model_width))] * (messages + 2), [vmem] * 3)(chosen, candidates, other)
    (local, near, *out), w_in = lax.optimization_barrier((out, w_in))
    weights = jnp.transpose(w_in, (1, 0, 2))
    came = cross(owners, out)
    near = to_neighbour(owners, near)
    visible = kernel_call(
        visible_kernel,
        [bf16((owners * piece, HD)), bf16((hist_rows, HD))],
        [vmem] * 3,
        [pltpu.VMEM((HD, owners * req_count), jnp.bfloat16)],
    )(session_row, hist_len.reshape(1, -1), lax.optimization_barrier((block_mask.T, out))[0])
    came, weights, (hide_rows, hide_cols) = lax.optimization_barrier((came, weights, visible))
    swapped = [swap(message) for message in came]
    local, near, keep, give = kernel_call(
        functools.partial(history_kernel, owners),
        [bf16((rows_out, width)) for rows_out in (piece // 2, piece, messages * piece, messages * piece + piece // 2)],
        [vmem] * (6 + owners),
        flops=8 * owners * piece * hist_rows * width,
        moved=4 * hist_rows * width,
    )(
        gain,
        weights,
        hide_rows,
        hide_cols,
        hist_keys.reshape(hist_rows, width),
        hist_values.reshape(hist_rows, width),
        local,
        near,
        *reversed(came),
        *reversed(swapped),
    )
    near = to_neighbour(owners, near)
    keep, give, w_other = lax.optimization_barrier((keep, give, w_other))
    got = swap(give)
    terms = kernel_call(
        self_kernel,
        [bf16((2, rows, width))] * 2,
        [vmem] * 4,
        [pltpu.VMEM((2 * rows, model_width), jnp.bfloat16)],
        flops=16 * rows * model_width * width,
        moved=8 * model_width * width,
    )(candidates, lax.optimization_barrier((other, give))[0], gain, weights)
    got, (keep_terms, give_terms) = lax.optimization_barrier((got, terms))
    backs = cross(owners, kernel_call(pack_kernel, [bf16((2 * piece, width))] * messages, [vmem] * 2)(keep, got))
    their_near = swap(near[piece // 2 :])
    returned = [rows_of for back in backs for rows_of in (back, swap(back[piece:]))]
    return kernel_call(
        functools.partial(output_kernel, owners),
        bf16((req_count, half_cands, model_width)),
        [smem] + [vmem] * (9 + 2 * messages),
        [pltpu.VMEM((2 * owners * CAP, half_cands, width), jnp.float32)],
        flops=8 * rows * model_width * width,
        moved=4 * model_width * width,
    )(sessions, candidates, keep_terms, swap(give_terms), w_out, w_other, local, got, near, their_near, *returned)


def solution(mesh):
    placed = (
        P(("groups", "cache"), "serve", None),
        P(),
        P(None, None, "serve"),
        P("serve", None),
        P(("groups", "cache"), None, "serve"),
        P(("groups", "cache"), None, "serve"),
        P("groups", None),
        P("groups"),
        P("groups", None),
    )
    return jax.shard_map(
        body,
        mesh=mesh,
        in_specs=placed,
        out_specs=P(("groups", "cache"), "serve", None),
        check_vma=False,
    )
```

```python
import functools

import jax
import jax.numpy as jnp
from jax import lax
from jax.experimental import pallas as pl
from jax.experimental.pallas import tpu as pltpu
from jax.sharding import PartitionSpec as P

HD = 128
BLK = 64
CAP = 2
EPS = 1e-06
SCALE = HD ** (-0.5)
HIDE = -1e30
VMEM_LIMIT = 16 * 1024 * 1024

vmem = pl.BlockSpec(memory_space=pltpu.VMEM)
smem = pl.BlockSpec(memory_space=pltpu.SMEM)


def silu_of_half(half):
    return half + half * jnp.tanh(half)


def silu(x):
    return silu_of_half(x * 0.5)


def kernel_call(body, out_shape, in_specs, scratch_shapes=(), flops=0, moved=0):
    return pl.pallas_call(
        body,
        out_shape=out_shape,
        in_specs=in_specs,
        out_specs=jax.tree.map(lambda _: vmem, out_shape),
        scratch_shapes=scratch_shapes,
        cost_estimate=pl.CostEstimate(flops=flops, bytes_accessed=moved, transcendentals=0),
        compiler_params=pltpu.CompilerParams(vmem_limit_bytes=VMEM_LIMIT),
    )


def gain_row(gain_ref):
    gain = gain_ref[...].astype(jnp.float32)
    return jnp.concatenate([gain[at : at + 1] for at in range(gain.shape[0])], axis=1)


def normed_rows(rows_ref, gain):
    rows = rows_ref[...].astype(jnp.float32)
    rows = rows.reshape(-1, rows.shape[-1])
    mean_square = jnp.mean(rows * rows, axis=-1, keepdims=True)
    return (rows * lax.rsqrt(mean_square + EPS) * gain).astype(jnp.bfloat16)


def core_of(distance):
    parity = distance
    for shift in (16, 8, 4, 2, 1):
        parity = parity ^ (parity >> shift)
    return parity & 1


def position(distance, serve, owners):
    far = jnp.where(core_of(distance) == serve, 0, owners // 2 - 1) + distance // 2 + 1
    return jnp.where(distance < 2, distance, far)


def own_slots(sess_ref, req_count):
    me = lax.axis_index("cache")
    base = me * req_count
    sessions = [sess_ref[base + request] for request in range(req_count)]
    slots = []
    for request in range(req_count):
        place = 0
        for earlier in range(request):
            place = place + (sessions[earlier] == sessions[request]).astype(jnp.int32)
        slots.append((sessions[request] ^ me, place))
    return slots


def places(sessions, per_owner):
    lane = lax.broadcasted_iota(jnp.int32, sessions.shape, 1)
    place = jnp.zeros_like(sessions)
    for back in range(1, per_owner):
        same = (pltpu.roll(sessions, back, 1) == sessions) & (lane % per_owner >= back)
        place = place + same.astype(jnp.int32)
    return place


def front_kernel(owners, half_cands, sess_ref, chosen_ref):
    me, serve = lax.axis_index("cache"), lax.axis_index("serve")
    sessions = sess_ref[...]
    requests = sessions.shape[1]
    per_owner = requests // owners
    rows = per_owner * half_cands
    distance = sessions ^ me
    at = position(distance, serve, owners)
    sent = at <= owners // 2
    code = jnp.where(sent, at * (2 * CAP) + places(sessions, per_owner), owners * (2 * CAP))
    request = lax.broadcasted_iota(jnp.int32, (requests, 2 * rows), 0)
    column = lax.broadcasted_iota(jnp.int32, (requests, 2 * rows), 1)
    spread = (request == me * per_owner + (column % rows) // half_cands).astype(jnp.float32).astype(jnp.bfloat16)
    codes = jnp.broadcast_to(code, (8, requests)).astype(jnp.float32).astype(jnp.bfloat16)
    target = jnp.dot(codes, spread, preferred_element_type=jnp.float32)[:1].astype(jnp.int32)
    at = lax.broadcasted_iota(jnp.int32, chosen_ref.shape, 0)
    column = lax.broadcasted_iota(jnp.int32, chosen_ref.shape, 1)
    hit = (at // half_cands == target + (column // rows) * CAP) & (at % half_cands == column % half_cands)
    chosen_ref[...] = hit.astype(jnp.float32).astype(jnp.bfloat16)


def visible_kernel(sess_ref, len_ref, mask_ref, hide_rows_ref, hide_cols_ref, marks_ref):
    me, serve = lax.axis_index("cache"), lax.axis_index("serve")
    blocks, requests = mask_ref.shape
    owners = len_ref.shape[1]
    per_owner = requests // owners
    sessions = sess_ref[...]
    lane = lax.broadcasted_iota(jnp.int32, (1, requests), 1)
    at = position((lane // per_owner) ^ me, serve, owners)
    slot_of = jnp.where(sessions == me, at * CAP + places(sessions, per_owner), -1)
    slots = owners * CAP
    at_slot = lax.broadcasted_iota(jnp.int32, (slots, requests), 0)
    taken = (at_slot == slot_of).astype(jnp.float32).astype(jnp.bfloat16)
    marks_ref[...] = jnp.zeros_like(marks_ref)
    marks_ref[:blocks, :] = mask_ref[...].astype(jnp.float32).astype(jnp.bfloat16)
    seen = lax.dot_general(taken, marks_ref[...], (((1,), (1,)), ((), ())), preferred_element_type=jnp.float32)
    slot_lane = lax.broadcasted_iota(jnp.int32, (slots, HD), 1)
    hidden = jnp.where(slot_lane < blocks, (1.0 - seen) * HIDE, jnp.where(slot_lane == blocks, HIDE, 0.0))
    half = hide_rows_ref.shape[0] // slots // 2
    wide = jnp.broadcast_to(hidden.reshape(owners, 1, CAP, 1, HD), (owners, 2, CAP, half, HD))
    hide_rows_ref[...] = wide.reshape(hide_rows_ref.shape).astype(jnp.bfloat16)
    hist_rows = hide_cols_ref.shape[0]
    owner_lane = lax.broadcasted_iota(jnp.int32, (1, owners), 1)
    length = jnp.sum(jnp.where(owner_lane == me, len_ref[...], 0), axis=1, keepdims=True)
    at_row = lax.broadcasted_iota(jnp.int32, (hist_rows, HD), 0)
    at_lane = lax.broadcasted_iota(jnp.int32, (hist_rows, HD), 1)
    hide_cols_ref[...] = jnp.where(
        (at_lane == at_row // BLK) | ((at_lane == blocks) & (at_row >= length)), 1.0, 0.0
    ).astype(jnp.bfloat16)


def message_kernel(chosen_ref, own_ref, other_ref, *out_refs):
    model_width = own_ref.shape[2]
    source = jnp.concatenate(
        [ref[...].astype(jnp.float32).reshape(-1, model_width) for ref in (own_ref, other_ref)], axis=0
    ).astype(jnp.bfloat16)
    rows = jnp.dot(chosen_ref[...], source, preferred_element_type=jnp.float32)
    piece = out_refs[0].shape[0]
    for at, out_ref in enumerate(out_refs):
        out_ref[...] = rows[at * piece : (at + 1) * piece].astype(jnp.bfloat16)


def self_kernel(own_ref, other_ref, gain_ref, w_ref, keep_ref, give_ref, normed_ref):
    rows, width = keep_ref.shape[1:]
    gain = gain_row(gain_ref)
    normed_ref[:rows, :] = normed_rows(own_ref, gain)
    normed_ref[rows:, :] = normed_rows(other_ref, gain)
    normed = normed_ref[...]

    def activated(part):
        return silu(jnp.dot(normed, w_ref[part], preferred_element_type=jnp.float32)).astype(jnp.bfloat16)

    products = activated(0).astype(jnp.float32) * activated(1).astype(jnp.float32)
    values, gates = activated(2), activated(3)
    for low in range(0, width, HD):
        score = jnp.sum(products[:, low : low + HD], axis=-1, keepdims=True) * SCALE
        term = (silu(score) * values[:, low : low + HD].astype(jnp.float32)).astype(jnp.bfloat16)
        keep_ref[0, :, low : low + HD] = term[:rows]
        give_ref[0, :, low : low + HD] = term[rows:]
    keep_ref[1] = gates[:rows]
    give_ref[1] = gates[rows:]


def pack_kernel(keep_ref, got_ref, *out_refs):
    part = out_refs[0].shape[0] // 4
    for at, out_ref in enumerate(out_refs):
        for side in range(2):
            low = (2 * at + side) * part
            out_ref[2 * side * part : (2 * side + 1) * part, :] = keep_ref[low : low + part, :]
            out_ref[(2 * side + 1) * part : (2 * side + 2) * part, :] = got_ref[low : low + part, :]


def history_kernel(owners, gain_ref, w_ref, hide_rows_ref, hide_cols_ref, keys_ref, values_ref, *refs):
    slot_refs, (local_ref, near_ref, keep_ref, give_ref) = refs[:owners], refs[owners:]
    width = near_ref.shape[1]
    per_owner = near_ref.shape[0]
    half = per_owner // 2
    far = [(ref, at * per_owner, 0, per_owner) for ref in (keep_ref, give_ref) for at in range(owners // 2 - 1)]
    local = [(local_ref, 0, 0, half), (give_ref, (owners // 2 - 1) * per_owner, half, half)]
    targets = [local, [(near_ref, 0, 0, per_owner)]] + [[target] for target in far]
    hist_rows = keys_ref.shape[0]
    span = min(256, hist_rows)
    per_step = max(1, min(owners, 256 // per_owner))
    gain = gain_row(gain_ref)
    for first in range(0, owners, per_step):
        group = range(first, min(first + per_step, owners))
        normed = jnp.concatenate([normed_rows(slot_refs[at], gain) for at in group], axis=0)
        queries = silu(jnp.dot(normed, w_ref[0], preferred_element_type=jnp.float32)).astype(jnp.bfloat16)
        hide_rows = hide_rows_ref[first * per_owner : first * per_owner + queries.shape[0], :]
        for low in range(0, width, HD):
            lhs = jnp.concatenate([queries[:, low : low + HD], hide_rows], axis=1)
            total = None
            for start in range(0, hist_rows, span):
                rhs = jnp.concatenate(
                    [keys_ref[start : start + span, low : low + HD], hide_cols_ref[start : start + span, :]], axis=1
                )
                scores = lax.dot_general(lhs, rhs, (((1,), (1,)), ((), ())), preferred_element_type=jnp.float32)
                weights = silu_of_half(scores * (0.5 * SCALE)).astype(jnp.bfloat16)
                term = jnp.dot(
                    weights, values_ref[start : start + span, low : low + HD], preferred_element_type=jnp.float32
                )
                total = term if total is None else total + term
            total = total.astype(jnp.bfloat16)
            for place, at in enumerate(group):
                for out_ref, row, start, count in targets[at]:
                    low_row = place * per_owner + start
                    out_ref[row : row + count, low : low + HD] = total[low_row : low_row + count]


def output_kernel(owners, sess_ref, own_ref, keep_ref, got_ref, w_own_ref, w_other_ref, *refs):
    local_ref, given_ref, near_ref, their_near_ref, *back_refs = refs[:-2]
    out_ref, table_ref = refs[-2:]
    req_count, half_cands, model_width = own_ref.shape
    rows = req_count * half_cands
    width = model_width // 2
    serve = lax.axis_index("serve")
    part = CAP * half_cands
    messages = owners // 2 - 1

    def store(at, heads, block):
        table_ref[(at * 2 + heads) * CAP : (at * 2 + heads + 1) * CAP] = block.reshape(CAP, half_cands, width)

    store(0, 0, local_ref[...].astype(jnp.float32))
    store(0, 1, given_ref[given_ref.shape[0] - part :, :].astype(jnp.float32))
    store(1, 0, near_ref[:part, :].astype(jnp.float32))
    store(1, 1, their_near_ref[...].astype(jnp.float32))
    for order, at in enumerate(far_first(messages)):
        for side in range(2):
            block = back_refs[2 * order + side][: 2 * part, :].astype(jnp.float32)
            for heads in range(2):
                source = heads if side == 0 else 1 - heads
                store(2 + side * messages + at, heads, block[source * part : (source + 1) * part])
    own = own_slots(sess_ref, req_count)
    total = own_ref[...].astype(jnp.float32).reshape(rows, model_width)
    for heads, (terms_ref, w_ref) in enumerate(((keep_ref, w_own_ref), (got_ref, w_other_ref))):
        history = []
        for distance, place in own:
            history.append(table_ref[(position(distance, serve, owners) * 2 + heads) * CAP + place])
        attended = jnp.concatenate(history, axis=0) + terms_ref[0].astype(jnp.float32)
        gates = terms_ref[1].astype(jnp.float32)
        mixed = []
        for low in range(0, width, HD):
            head = attended[:, low : low + HD]
            level = lax.rsqrt(jnp.mean(head * head, axis=-1, keepdims=True) + EPS)
            mixed.append((head * level * gates[:, low : low + HD]).astype(jnp.bfloat16))
        total = total + jnp.dot(jnp.concatenate(mixed, axis=1), w_ref[...], preferred_element_type=jnp.float32)
    out_ref[...] = total.reshape(out_ref.shape).astype(jnp.bfloat16)


def far_first(count):
    return list(reversed(range(count)))


def swap(rows):
    return lax.ppermute(rows, "serve", [(0, 1), (1, 0)])


def cross(owners, messages):
    came = []
    for at in far_first(len(messages)):
        steps = [2 * (at + 1) + side for side in range(2)]
        pairs = [(place * 2 + core_of(step), (place ^ step) * 2 + core_of(step)) for place in range(owners) for step in steps]
        came.append(lax.ppermute(messages[at], ("cache", "serve"), pairs))
    return came


def to_neighbour(owners, rows):
    return lax.ppermute(rows, "cache", [(place, place ^ 1) for place in range(owners)])


def body(candidates, input_gain, w_in, w_out, hist_keys, hist_values, request_session, hist_len, block_mask):
    owners = lax.axis_size("cache")
    req_count, half_cands, model_width = candidates.shape
    width = w_in.shape[2]
    rows = req_count * half_cands
    hist_rows = hist_keys.shape[1]
    bf16 = functools.partial(jax.ShapeDtypeStruct, dtype=jnp.bfloat16)
    sessions = request_session.reshape(-1)
    gain = input_gain.reshape(-1, HD)
    messages = owners // 2 - 1
    piece = 2 * CAP * half_cands

    session_row = request_session.reshape(1, -1)
    chosen = kernel_call(
        functools.partial(front_kernel, owners, half_cands),
        bf16(((messages + 2) * piece, 2 * rows)),
        [vmem],
    )(session_row)
    other, w_out, chosen = lax.optimization_barrier((swap(candidates), w_out, chosen))
    w_other = swap(w_out)
    out = kernel_call(message_kernel, [bf16((piece, model_width))] * (messages + 2), [vmem] * 3)(chosen, candidates, other)
    (local, near, *out), w_in = lax.optimization_barrier((out, w_in))
    weights = jnp.transpose(w_in, (1, 0, 2))
    near = to_neighbour(owners, near)
    came = cross(owners, out)
    visible = kernel_call(
        visible_kernel,
        [bf16((owners * piece, HD)), bf16((hist_rows, HD))],
        [vmem] * 3,
        [pltpu.VMEM((HD, owners * req_count), jnp.bfloat16)],
    )(session_row, hist_len.reshape(1, -1), lax.optimization_barrier((block_mask.T, out))[0])
    near, came, weights, (hide_rows, hide_cols) = lax.optimization_barrier((near, came, weights, visible))
    swapped = [swap(message) for message in came]
    local, near, keep, give = kernel_call(
        functools.partial(history_kernel, owners),
        [bf16((rows_out, width)) for rows_out in (piece // 2, piece, messages * piece, messages * piece + piece // 2)],
        [vmem] * (6 + owners),
        flops=8 * owners * piece * hist_rows * width,
        moved=4 * hist_rows * width,
    )(
        gain,
        weights,
        hide_rows,
        hide_cols,
        hist_keys.reshape(hist_rows, width),
        hist_values.reshape(hist_rows, width),
        local,
        near,
        *reversed(came),
        *reversed(swapped),
    )
    near = to_neighbour(owners, near)
    keep, give, w_other = lax.optimization_barrier((keep, give, w_other))
    got = swap(give)
    terms = kernel_call(
        self_kernel,
        [bf16((2, rows, width))] * 2,
        [vmem] * 4,
        [pltpu.VMEM((2 * rows, model_width), jnp.bfloat16)],
        flops=16 * rows * model_width * width,
        moved=8 * model_width * width,
    )(candidates, lax.optimization_barrier((other, give))[0], gain, weights)
    got, (keep_terms, give_terms) = lax.optimization_barrier((got, terms))
    backs = cross(owners, kernel_call(pack_kernel, [bf16((2 * piece, width))] * messages, [vmem] * 2)(keep, got))
    their_near = swap(near[piece // 2 :])
    returned = [rows_of for back in backs for rows_of in (back, swap(back[piece:]))]
    return kernel_call(
        functools.partial(output_kernel, owners),
        bf16((req_count, half_cands, model_width)),
        [smem] + [vmem] * (9 + 2 * messages),
        [pltpu.VMEM((2 * owners * CAP, half_cands, width), jnp.float32)],
        flops=8 * rows * model_width * width,
        moved=4 * model_width * width,
    )(sessions, candidates, keep_terms, swap(give_terms), w_out, w_other, local, got, near, their_near, *returned)


def solution(mesh):
    placed = (
        P(("groups", "cache"), "serve", None),
        P(),
        P(None, None, "serve"),
        P("serve", None),
        P(("groups", "cache"), None, "serve"),
        P(("groups", "cache"), None, "serve"),
        P("groups", None),
        P("groups"),
        P("groups", None),
    )
    return jax.shard_map(
        body,
        mesh=mesh,
        in_specs=placed,
        out_specs=P(("groups", "cache"), "serve", None),
        check_vma=False,
    )
```

```python
import functools

import jax
import jax.numpy as jnp
from jax import lax
from jax.experimental import pallas as pl
from jax.experimental.pallas import tpu as pltpu
from jax.sharding import PartitionSpec as P

HD = 128
BLK = 64
CAP = 2
EPS = 1e-06
SCALE = HD ** (-0.5)
HIDE = -1e30
VMEM_LIMIT = 16 * 1024 * 1024

vmem = pl.BlockSpec(memory_space=pltpu.VMEM)
smem = pl.BlockSpec(memory_space=pltpu.SMEM)


def silu_of_half(half):
    return half + half * jnp.tanh(half)


def silu(x):
    return silu_of_half(x * 0.5)


def kernel_call(body, out_shape, in_specs, scratch_shapes=(), flops=0, moved=0):
    return pl.pallas_call(
        body,
        out_shape=out_shape,
        in_specs=in_specs,
        out_specs=jax.tree.map(lambda _: vmem, out_shape),
        scratch_shapes=scratch_shapes,
        cost_estimate=pl.CostEstimate(flops=flops, bytes_accessed=moved, transcendentals=0),
        compiler_params=pltpu.CompilerParams(vmem_limit_bytes=VMEM_LIMIT),
    )


def gain_row(gain_ref):
    gain = gain_ref[...].astype(jnp.float32)
    return jnp.concatenate([gain[at : at + 1] for at in range(gain.shape[0])], axis=1)


def normed_rows(rows_ref, start, count, gain):
    rows = rows_ref[start : start + count].astype(jnp.float32)
    rows = rows.reshape(-1, rows.shape[-1])
    mean_square = jnp.mean(rows * rows, axis=-1, keepdims=True)
    return (rows * lax.rsqrt(mean_square + EPS) * gain).astype(jnp.bfloat16)


def core_of(distance):
    parity = distance
    for shift in (16, 8, 4, 2, 1):
        parity = parity ^ (parity >> shift)
    return parity & 1


def position(distance, serve, owners):
    far = jnp.where(core_of(distance) == serve, 0, owners // 2 - 1) + distance // 2 + 1
    return jnp.where(distance < 2, distance, far)


def own_slots(sess_ref, req_count):
    me = lax.axis_index("cache")
    base = me * req_count
    sessions = [sess_ref[base + request] for request in range(req_count)]
    slots = []
    for request in range(req_count):
        place = 0
        for earlier in range(request):
            place = place + (sessions[earlier] == sessions[request]).astype(jnp.int32)
        slots.append((sessions[request] ^ me, place))
    return slots


def places(sessions, per_owner):
    lane = lax.broadcasted_iota(jnp.int32, sessions.shape, 1)
    place = jnp.zeros_like(sessions)
    for back in range(1, per_owner):
        same = (pltpu.roll(sessions, back, 1) == sessions) & (lane % per_owner >= back)
        place = place + same.astype(jnp.int32)
    return place


def front_kernel(owners, half_cands, sess_ref, chosen_ref):
    me, serve = lax.axis_index("cache"), lax.axis_index("serve")
    sessions = sess_ref[...]
    requests = sessions.shape[1]
    per_owner = requests // owners
    rows = per_owner * half_cands
    distance = sessions ^ me
    at = position(distance, serve, owners)
    sent = at <= owners // 2
    code = jnp.where(sent, at * (2 * CAP) + places(sessions, per_owner), owners * (2 * CAP))
    request = lax.broadcasted_iota(jnp.int32, (requests, 2 * rows), 0)
    column = lax.broadcasted_iota(jnp.int32, (requests, 2 * rows), 1)
    spread = (request == me * per_owner + (column % rows) // half_cands).astype(jnp.float32).astype(jnp.bfloat16)
    codes = jnp.broadcast_to(code, (8, requests)).astype(jnp.float32).astype(jnp.bfloat16)
    target = jnp.dot(codes, spread, preferred_element_type=jnp.float32)[:1].astype(jnp.int32)
    at = lax.broadcasted_iota(jnp.int32, chosen_ref.shape, 0)
    column = lax.broadcasted_iota(jnp.int32, chosen_ref.shape, 1)
    hit = (at // half_cands == target + (column // rows) * CAP) & (at % half_cands == column % half_cands)
    chosen_ref[...] = hit.astype(jnp.float32).astype(jnp.bfloat16)


def visible_kernel(sess_ref, len_ref, mask_ref, hide_rows_ref, hide_cols_ref, marks_ref):
    me, serve = lax.axis_index("cache"), lax.axis_index("serve")
    blocks, requests = mask_ref.shape
    owners = len_ref.shape[1]
    per_owner = requests // owners
    sessions = sess_ref[...]
    lane = lax.broadcasted_iota(jnp.int32, (1, requests), 1)
    at = position((lane // per_owner) ^ me, serve, owners)
    slot_of = jnp.where(sessions == me, at * CAP + places(sessions, per_owner), -1)
    slots = owners * CAP
    at_slot = lax.broadcasted_iota(jnp.int32, (slots, requests), 0)
    taken = (at_slot == slot_of).astype(jnp.float32).astype(jnp.bfloat16)
    marks_ref[...] = jnp.zeros_like(marks_ref)
    marks_ref[:blocks, :] = mask_ref[...].astype(jnp.float32).astype(jnp.bfloat16)
    seen = lax.dot_general(taken, marks_ref[...], (((1,), (1,)), ((), ())), preferred_element_type=jnp.float32)
    slot_lane = lax.broadcasted_iota(jnp.int32, (slots, HD), 1)
    hidden = jnp.where(slot_lane < blocks, (1.0 - seen) * HIDE, jnp.where(slot_lane == blocks, HIDE, 0.0))
    half = hide_rows_ref.shape[0] // slots // 2
    wide = jnp.broadcast_to(hidden.reshape(owners, 1, CAP, 1, HD), (owners, 2, CAP, half, HD))
    hide_rows_ref[...] = wide.reshape(hide_rows_ref.shape).astype(jnp.bfloat16)
    hist_rows = hide_cols_ref.shape[0]
    owner_lane = lax.broadcasted_iota(jnp.int32, (1, owners), 1)
    length = jnp.sum(jnp.where(owner_lane == me, len_ref[...], 0), axis=1, keepdims=True)
    at_row = lax.broadcasted_iota(jnp.int32, (hist_rows, HD), 0)
    at_lane = lax.broadcasted_iota(jnp.int32, (hist_rows, HD), 1)
    hide_cols_ref[...] = jnp.where(
        (at_lane == at_row // BLK) | ((at_lane == blocks) & (at_row >= length)), 1.0, 0.0
    ).astype(jnp.bfloat16)


def message_kernel(chosen_ref, own_ref, other_ref, *out_refs):
    model_width = own_ref.shape[2]
    source = jnp.concatenate(
        [ref[...].astype(jnp.float32).reshape(-1, model_width) for ref in (own_ref, other_ref)], axis=0
    ).astype(jnp.bfloat16)
    rows = jnp.dot(chosen_ref[...], source, preferred_element_type=jnp.float32)
    piece = out_refs[0].shape[0]
    for at, out_ref in enumerate(out_refs):
        out_ref[...] = rows[at * piece : (at + 1) * piece].astype(jnp.bfloat16)


def self_kernel(own_ref, other_ref, gain_ref, w_ref, keep_ref, give_ref, normed_ref):
    rows, width = keep_ref.shape[1:]
    gain = gain_row(gain_ref)
    normed_ref[:rows, :] = normed_rows(own_ref, 0, own_ref.shape[0], gain)
    normed_ref[rows:, :] = normed_rows(other_ref, 0, other_ref.shape[0], gain)
    normed = normed_ref[...]

    def activated(part):
        return silu(jnp.dot(normed, w_ref[part], preferred_element_type=jnp.float32)).astype(jnp.bfloat16)

    products = activated(0).astype(jnp.float32) * activated(1).astype(jnp.float32)
    values, gates = activated(2), activated(3)
    for low in range(0, width, HD):
        score = jnp.sum(products[:, low : low + HD], axis=-1, keepdims=True) * SCALE
        term = (silu(score) * values[:, low : low + HD].astype(jnp.float32)).astype(jnp.bfloat16)
        keep_ref[0, :, low : low + HD] = term[:rows]
        give_ref[0, :, low : low + HD] = term[rows:]
    keep_ref[1] = gates[:rows]
    give_ref[1] = gates[rows:]


def pack_kernel(keep_ref, got_ref, *out_refs):
    part = out_refs[0].shape[0] // 4
    for at, out_ref in enumerate(out_refs):
        for side in range(2):
            low = (2 * at + side) * part
            out_ref[2 * side * part : (2 * side + 1) * part, :] = keep_ref[low : low + part, :]
            out_ref[(2 * side + 1) * part : (2 * side + 2) * part, :] = got_ref[low : low + part, :]


def stack_kernel(*refs):
    *in_refs, out_ref = refs
    rows = in_refs[0].shape[0]
    for at, in_ref in enumerate(in_refs):
        out_ref[at * rows : (at + 1) * rows, :] = in_ref[...]


def history_kernel(owners, gain_ref, w_ref, hide_rows_ref, hide_cols_ref, keys_ref, values_ref, *refs):
    *slot_refs, swapped_ref, local_ref, near_ref, keep_ref, give_ref = refs
    width = near_ref.shape[1]
    per_owner = near_ref.shape[0]
    half = per_owner // 2
    far = [(ref, at * per_owner, 0, per_owner) for ref in (keep_ref, give_ref) for at in range(owners // 2 - 1)]
    local = [(local_ref, 0, 0, half), (give_ref, (owners // 2 - 1) * per_owner, half, half)]
    sources = [(ref, 0) for ref in slot_refs] + [(swapped_ref, at * per_owner) for at in range(owners // 2 - 1)]
    targets = [local, [(near_ref, 0, 0, per_owner)]] + [[target] for target in far]
    hist_rows = keys_ref.shape[0]
    span = min(256, hist_rows)
    per_step = max(1, min(owners, 256 // per_owner))
    gain = gain_row(gain_ref)
    for first in range(0, owners, per_step):
        group = range(first, min(first + per_step, owners))
        normed = jnp.concatenate([normed_rows(*sources[at], per_owner, gain) for at in group], axis=0)
        queries = silu(jnp.dot(normed, w_ref[0], preferred_element_type=jnp.float32)).astype(jnp.bfloat16)
        hide_rows = hide_rows_ref[first * per_owner : first * per_owner + queries.shape[0], :]
        for low in range(0, width, HD):
            lhs = jnp.concatenate([queries[:, low : low + HD], hide_rows], axis=1)
            total = None
            for start in range(0, hist_rows, span):
                rhs = jnp.concatenate(
                    [keys_ref[start : start + span, low : low + HD], hide_cols_ref[start : start + span, :]], axis=1
                )
                scores = lax.dot_general(lhs, rhs, (((1,), (1,)), ((), ())), preferred_element_type=jnp.float32)
                weights = silu_of_half(scores * (0.5 * SCALE)).astype(jnp.bfloat16)
                term = jnp.dot(
                    weights, values_ref[start : start + span, low : low + HD], preferred_element_type=jnp.float32
                )
                total = term if total is None else total + term
            total = total.astype(jnp.bfloat16)
            for place, at in enumerate(group):
                for out_ref, row, start, count in targets[at]:
                    low_row = place * per_owner + start
                    out_ref[row : row + count, low : low + HD] = total[low_row : low_row + count]


def output_kernel(owners, sess_ref, own_ref, keep_ref, got_ref, w_own_ref, w_other_ref, *refs):
    local_ref, given_ref, near_ref, their_near_ref, *back_refs = refs[:-2]
    out_ref, table_ref = refs[-2:]
    req_count, half_cands, model_width = own_ref.shape
    rows = req_count * half_cands
    width = model_width // 2
    serve = lax.axis_index("serve")
    part = CAP * half_cands
    messages = owners // 2 - 1

    def store(at, heads, block):
        table_ref[(at * 2 + heads) * CAP : (at * 2 + heads + 1) * CAP] = block.reshape(CAP, half_cands, width)

    store(0, 0, local_ref[...].astype(jnp.float32))
    store(0, 1, given_ref[given_ref.shape[0] - part :, :].astype(jnp.float32))
    store(1, 0, near_ref[:part, :].astype(jnp.float32))
    store(1, 1, their_near_ref[...].astype(jnp.float32))
    for order, at in enumerate(far_first(messages)):
        for side in range(2):
            block = back_refs[2 * order + side][: 2 * part, :].astype(jnp.float32)
            for heads in range(2):
                source = heads if side == 0 else 1 - heads
                store(2 + side * messages + at, heads, block[source * part : (source + 1) * part])
    own = own_slots(sess_ref, req_count)
    total = own_ref[...].astype(jnp.float32).reshape(rows, model_width)
    for heads, (terms_ref, w_ref) in enumerate(((keep_ref, w_own_ref), (got_ref, w_other_ref))):
        history = []
        for distance, place in own:
            history.append(table_ref[(position(distance, serve, owners) * 2 + heads) * CAP + place])
        attended = jnp.concatenate(history, axis=0) + terms_ref[0].astype(jnp.float32)
        gates = terms_ref[1].astype(jnp.float32)
        mixed = []
        for low in range(0, width, HD):
            head = attended[:, low : low + HD]
            level = lax.rsqrt(jnp.mean(head * head, axis=-1, keepdims=True) + EPS)
            mixed.append((head * level * gates[:, low : low + HD]).astype(jnp.bfloat16))
        total = total + jnp.dot(jnp.concatenate(mixed, axis=1), w_ref[...], preferred_element_type=jnp.float32)
    out_ref[...] = total.reshape(out_ref.shape).astype(jnp.bfloat16)


def far_first(count):
    return list(reversed(range(count)))


def swap(rows):
    return lax.ppermute(rows, "serve", [(0, 1), (1, 0)])


def cross(owners, messages):
    came = []
    for at in far_first(len(messages)):
        steps = [2 * (at + 1) + side for side in range(2)]
        pairs = [(place * 2 + core_of(step), (place ^ step) * 2 + core_of(step)) for place in range(owners) for step in steps]
        came.append(lax.ppermute(messages[at], ("cache", "serve"), pairs))
    return came


def to_neighbour(owners, rows):
    return lax.ppermute(rows, "cache", [(place, place ^ 1) for place in range(owners)])


def body(candidates, input_gain, w_in, w_out, hist_keys, hist_values, request_session, hist_len, block_mask):
    owners = lax.axis_size("cache")
    req_count, half_cands, model_width = candidates.shape
    width = w_in.shape[2]
    rows = req_count * half_cands
    hist_rows = hist_keys.shape[1]
    bf16 = functools.partial(jax.ShapeDtypeStruct, dtype=jnp.bfloat16)
    sessions = request_session.reshape(-1)
    gain = input_gain.reshape(-1, HD)
    messages = owners // 2 - 1
    piece = 2 * CAP * half_cands

    session_row = request_session.reshape(1, -1)
    chosen = kernel_call(
        functools.partial(front_kernel, owners, half_cands),
        bf16(((messages + 2) * piece, 2 * rows)),
        [vmem],
    )(session_row)
    other, w_out, chosen = lax.optimization_barrier((swap(candidates), w_out, chosen))
    w_other = swap(w_out)
    out = kernel_call(message_kernel, [bf16((piece, model_width))] * (messages + 2), [vmem] * 3)(chosen, candidates, other)
    (local, near, *out), w_in = lax.optimization_barrier((out, w_in))
    weights = jnp.transpose(w_in, (1, 0, 2))
    near = to_neighbour(owners, near)
    came = cross(owners, out)
    near, came, weights = lax.optimization_barrier((near, came, weights))
    stacked = kernel_call(stack_kernel, bf16((messages * piece, model_width)), [vmem] * messages)(*reversed(came))
    visible = kernel_call(
        visible_kernel,
        [bf16((owners * piece, HD)), bf16((hist_rows, HD))],
        [vmem] * 3,
        [pltpu.VMEM((HD, owners * req_count), jnp.bfloat16)],
        flops=2 * messages * piece * model_width * width,
    )(session_row, hist_len.reshape(1, -1), lax.optimization_barrier((block_mask.T, stacked))[0])
    swapped, (hide_rows, hide_cols) = lax.optimization_barrier((swap(stacked), visible))
    local, near, keep, give = kernel_call(
        functools.partial(history_kernel, owners),
        [bf16((rows_out, width)) for rows_out in (piece // 2, piece, messages * piece, messages * piece + piece // 2)],
        [vmem] * (6 + owners // 2 + 2),
        flops=8 * owners * piece * hist_rows * width,
        moved=4 * hist_rows * width,
    )(
        gain,
        weights,
        hide_rows,
        hide_cols,
        hist_keys.reshape(hist_rows, width),
        hist_values.reshape(hist_rows, width),
        local,
        near,
        *reversed(came),
        swapped,
    )
    near = to_neighbour(owners, near)
    keep, give, w_other = lax.optimization_barrier((keep, give, w_other))
    got = swap(give)
    terms = kernel_call(
        self_kernel,
        [bf16((2, rows, width))] * 2,
        [vmem] * 4,
        [pltpu.VMEM((2 * rows, model_width), jnp.bfloat16)],
        flops=16 * rows * model_width * width,
        moved=8 * model_width * width,
    )(candidates, lax.optimization_barrier((other, give))[0], gain, weights)
    got, (keep_terms, give_terms) = lax.optimization_barrier((got, terms))
    backs = cross(owners, kernel_call(pack_kernel, [bf16((2 * piece, width))] * messages, [vmem] * 2)(keep, got))
    their_near = swap(near[piece // 2 :])
    returned = [rows_of for back in backs for rows_of in (back, swap(back[piece:]))]
    return kernel_call(
        functools.partial(output_kernel, owners),
        bf16((req_count, half_cands, model_width)),
        [smem] + [vmem] * (9 + 2 * messages),
        [pltpu.VMEM((2 * owners * CAP, half_cands, width), jnp.float32)],
        flops=8 * rows * model_width * width,
        moved=4 * model_width * width,
    )(sessions, candidates, keep_terms, swap(give_terms), w_out, w_other, local, got, near, their_near, *returned)


def solution(mesh):
    placed = (
        P(("groups", "cache"), "serve", None),
        P(),
        P(None, None, "serve"),
        P("serve", None),
        P(("groups", "cache"), None, "serve"),
        P(("groups", "cache"), None, "serve"),
        P("groups", None),
        P("groups"),
        P("groups", None),
    )
    return jax.shard_map(
        body,
        mesh=mesh,
        in_specs=placed,
        out_specs=P(("groups", "cache"), "serve", None),
        check_vma=False,
    )
```

```python
import functools

import jax
import jax.numpy as jnp
from jax import lax
from jax.experimental import pallas as pl
from jax.experimental.pallas import tpu as pltpu
from jax.sharding import PartitionSpec as P

HD = 128
BLK = 64
CAP = 2
EPS = 1e-06
SCALE = HD ** (-0.5)
HIDE = -1e30
VMEM_LIMIT = 16 * 1024 * 1024

vmem = pl.BlockSpec(memory_space=pltpu.VMEM)
smem = pl.BlockSpec(memory_space=pltpu.SMEM)


def silu_of_half(half):
    return half + half * jnp.tanh(half)


def silu(x):
    return silu_of_half(x * 0.5)


def kernel_call(body, out_shape, in_specs, scratch_shapes=(), flops=0, moved=0):
    return pl.pallas_call(
        body,
        out_shape=out_shape,
        in_specs=in_specs,
        out_specs=jax.tree.map(lambda _: vmem, out_shape),
        scratch_shapes=scratch_shapes,
        cost_estimate=pl.CostEstimate(flops=flops, bytes_accessed=moved, transcendentals=0),
        compiler_params=pltpu.CompilerParams(vmem_limit_bytes=VMEM_LIMIT),
    )


def gain_row(gain_ref):
    gain = gain_ref[...].astype(jnp.float32)
    return jnp.concatenate([gain[at : at + 1] for at in range(gain.shape[0])], axis=1)


def normed_rows(rows_ref, start, count, gain):
    rows = rows_ref[start : start + count].astype(jnp.float32)
    rows = rows.reshape(-1, rows.shape[-1])
    mean_square = jnp.mean(rows * rows, axis=-1, keepdims=True)
    return (rows * lax.rsqrt(mean_square + EPS) * gain).astype(jnp.bfloat16)


def core_of(distance):
    parity = distance
    for shift in (16, 8, 4, 2, 1):
        parity = parity ^ (parity >> shift)
    return parity & 1


def position(distance, serve, owners):
    far = jnp.where(core_of(distance) == serve, 0, owners // 2 - 1) + distance // 2 + 1
    return jnp.where(distance < 2, distance, far)


def own_slots(sess_ref, req_count):
    me = lax.axis_index("cache")
    base = me * req_count
    sessions = [sess_ref[base + request] for request in range(req_count)]
    slots = []
    for request in range(req_count):
        place = 0
        for earlier in range(request):
            place = place + (sessions[earlier] == sessions[request]).astype(jnp.int32)
        slots.append((sessions[request] ^ me, place))
    return slots


def places(sessions, per_owner):
    lane = lax.broadcasted_iota(jnp.int32, sessions.shape, 1)
    place = jnp.zeros_like(sessions)
    for back in range(1, per_owner):
        same = (pltpu.roll(sessions, back, 1) == sessions) & (lane % per_owner >= back)
        place = place + same.astype(jnp.int32)
    return place


def front_kernel(owners, half_cands, sess_ref, chosen_ref):
    me, serve = lax.axis_index("cache"), lax.axis_index("serve")
    sessions = sess_ref[...]
    requests = sessions.shape[1]
    per_owner = requests // owners
    rows = per_owner * half_cands
    distance = sessions ^ me
    at = position(distance, serve, owners)
    sent = at <= owners // 2
    code = jnp.where(sent, at * (2 * CAP) + places(sessions, per_owner), owners * (2 * CAP))
    request = lax.broadcasted_iota(jnp.int32, (requests, 2 * rows), 0)
    column = lax.broadcasted_iota(jnp.int32, (requests, 2 * rows), 1)
    spread = (request == me * per_owner + (column % rows) // half_cands).astype(jnp.float32).astype(jnp.bfloat16)
    codes = jnp.broadcast_to(code, (8, requests)).astype(jnp.float32).astype(jnp.bfloat16)
    target = jnp.dot(codes, spread, preferred_element_type=jnp.float32)[:1].astype(jnp.int32)
    at = lax.broadcasted_iota(jnp.int32, chosen_ref.shape, 0)
    column = lax.broadcasted_iota(jnp.int32, chosen_ref.shape, 1)
    hit = (at // half_cands == target + (column // rows) * CAP) & (at % half_cands == column % half_cands)
    chosen_ref[...] = hit.astype(jnp.float32).astype(jnp.bfloat16)


def visible_kernel(sess_ref, len_ref, mask_ref, hide_rows_ref, hide_cols_ref, marks_ref):
    me, serve = lax.axis_index("cache"), lax.axis_index("serve")
    blocks, requests = mask_ref.shape
    owners = len_ref.shape[1]
    per_owner = requests // owners
    sessions = sess_ref[...]
    lane = lax.broadcasted_iota(jnp.int32, (1, requests), 1)
    at = position((lane // per_owner) ^ me, serve, owners)
    slot_of = jnp.where(sessions == me, at * CAP + places(sessions, per_owner), -1)
    slots = owners * CAP
    at_slot = lax.broadcasted_iota(jnp.int32, (slots, requests), 0)
    taken = (at_slot == slot_of).astype(jnp.float32).astype(jnp.bfloat16)
    marks_ref[...] = jnp.zeros_like(marks_ref)
    marks_ref[:blocks, :] = mask_ref[...].astype(jnp.float32).astype(jnp.bfloat16)
    seen = lax.dot_general(taken, marks_ref[...], (((1,), (1,)), ((), ())), preferred_element_type=jnp.float32)
    slot_lane = lax.broadcasted_iota(jnp.int32, (slots, HD), 1)
    hidden = jnp.where(slot_lane < blocks, (1.0 - seen) * HIDE, jnp.where(slot_lane == blocks, HIDE, 0.0))
    half = hide_rows_ref.shape[0] // slots // 2
    wide = jnp.broadcast_to(hidden.reshape(owners, 1, CAP, 1, HD), (owners, 2, CAP, half, HD))
    hide_rows_ref[...] = wide.reshape(hide_rows_ref.shape).astype(jnp.bfloat16)
    hist_rows = hide_cols_ref.shape[0]
    owner_lane = lax.broadcasted_iota(jnp.int32, (1, owners), 1)
    length = jnp.sum(jnp.where(owner_lane == me, len_ref[...], 0), axis=1, keepdims=True)
    at_row = lax.broadcasted_iota(jnp.int32, (hist_rows, HD), 0)
    at_lane = lax.broadcasted_iota(jnp.int32, (hist_rows, HD), 1)
    hide_cols_ref[...] = jnp.where(
        (at_lane == at_row // BLK) | ((at_lane == blocks) & (at_row >= length)), 1.0, 0.0
    ).astype(jnp.bfloat16)


def message_kernel(chosen_ref, own_ref, other_ref, *out_refs):
    model_width = own_ref.shape[2]
    source = jnp.concatenate(
        [ref[...].astype(jnp.float32).reshape(-1, model_width) for ref in (own_ref, other_ref)], axis=0
    ).astype(jnp.bfloat16)
    rows = jnp.dot(chosen_ref[...], source, preferred_element_type=jnp.float32)
    piece = out_refs[0].shape[0]
    for at, out_ref in enumerate(out_refs):
        out_ref[...] = rows[at * piece : (at + 1) * piece].astype(jnp.bfloat16)


def self_kernel(own_ref, other_ref, gain_ref, w_ref, keep_ref, give_ref, normed_ref):
    rows, width = keep_ref.shape[1:]
    gain = gain_row(gain_ref)
    normed_ref[:rows, :] = normed_rows(own_ref, 0, own_ref.shape[0], gain)
    normed_ref[rows:, :] = normed_rows(other_ref, 0, other_ref.shape[0], gain)
    normed = normed_ref[...]

    def activated(part):
        return silu(jnp.dot(normed, w_ref[part], preferred_element_type=jnp.float32)).astype(jnp.bfloat16)

    products = activated(0).astype(jnp.float32) * activated(1).astype(jnp.float32)
    values, gates = activated(2), activated(3)
    for low in range(0, width, HD):
        score = jnp.sum(products[:, low : low + HD], axis=-1, keepdims=True) * SCALE
        term = (silu(score) * values[:, low : low + HD].astype(jnp.float32)).astype(jnp.bfloat16)
        keep_ref[0, :, low : low + HD] = term[:rows]
        give_ref[0, :, low : low + HD] = term[rows:]
    keep_ref[1] = gates[:rows]
    give_ref[1] = gates[rows:]


def pack_kernel(keep_ref, got_ref, *out_refs):
    part = out_refs[0].shape[0] // 4
    for at, out_ref in enumerate(out_refs):
        for side in range(2):
            low = (2 * at + side) * part
            out_ref[2 * side * part : (2 * side + 1) * part, :] = keep_ref[low : low + part, :]
            out_ref[(2 * side + 1) * part : (2 * side + 2) * part, :] = got_ref[low : low + part, :]


def stack_kernel(*refs):
    *in_refs, out_ref = refs
    rows = in_refs[0].shape[0]
    for at, in_ref in zip(far_first(len(in_refs)), in_refs):
        out_ref[at * rows : (at + 1) * rows, :] = in_ref[...]


def history_kernel(owners, gain_ref, w_ref, hide_rows_ref, hide_cols_ref, keys_ref, values_ref, *refs):
    *slot_refs, swapped_ref, local_ref, near_ref, keep_ref, give_ref = refs
    width = near_ref.shape[1]
    per_owner = near_ref.shape[0]
    half = per_owner // 2
    far = [(ref, at * per_owner, 0, per_owner) for ref in (keep_ref, give_ref) for at in range(owners // 2 - 1)]
    local = [(local_ref, 0, 0, half), (give_ref, (owners // 2 - 1) * per_owner, half, half)]
    sources = [(ref, 0) for ref in slot_refs] + [(swapped_ref, at * per_owner) for at in range(owners // 2 - 1)]
    targets = [local, [(near_ref, 0, 0, per_owner)]] + [[target] for target in far]
    hist_rows = keys_ref.shape[0]
    span = min(256, hist_rows)
    per_step = max(1, min(owners, 256 // per_owner))
    gain = gain_row(gain_ref)
    for first in range(0, owners, per_step):
        group = range(first, min(first + per_step, owners))
        normed = jnp.concatenate([normed_rows(*sources[at], per_owner, gain) for at in group], axis=0)
        queries = silu(jnp.dot(normed, w_ref[0], preferred_element_type=jnp.float32)).astype(jnp.bfloat16)
        hide_rows = hide_rows_ref[first * per_owner : first * per_owner + queries.shape[0], :]
        for low in range(0, width, HD):
            lhs = jnp.concatenate([queries[:, low : low + HD], hide_rows], axis=1)
            total = None
            for start in range(0, hist_rows, span):
                rhs = jnp.concatenate(
                    [keys_ref[start : start + span, low : low + HD], hide_cols_ref[start : start + span, :]], axis=1
                )
                scores = lax.dot_general(lhs, rhs, (((1,), (1,)), ((), ())), preferred_element_type=jnp.float32)
                weights = silu_of_half(scores * (0.5 * SCALE)).astype(jnp.bfloat16)
                term = jnp.dot(
                    weights, values_ref[start : start + span, low : low + HD], preferred_element_type=jnp.float32
                )
                total = term if total is None else total + term
            total = total.astype(jnp.bfloat16)
            for place, at in enumerate(group):
                for out_ref, row, start, count in targets[at]:
                    low_row = place * per_owner + start
                    out_ref[row : row + count, low : low + HD] = total[low_row : low_row + count]


def output_kernel(owners, sess_ref, own_ref, keep_ref, got_ref, w_own_ref, w_other_ref, *refs):
    local_ref, given_ref, near_ref, their_near_ref, *back_refs = refs[:-2]
    out_ref, table_ref = refs[-2:]
    req_count, half_cands, model_width = own_ref.shape
    rows = req_count * half_cands
    width = model_width // 2
    serve = lax.axis_index("serve")
    part = CAP * half_cands
    messages = owners // 2 - 1

    def store(at, heads, block):
        table_ref[(at * 2 + heads) * CAP : (at * 2 + heads + 1) * CAP] = block.reshape(CAP, half_cands, width)

    store(0, 0, local_ref[...].astype(jnp.float32))
    store(0, 1, given_ref[given_ref.shape[0] - part :, :].astype(jnp.float32))
    store(1, 0, near_ref[:part, :].astype(jnp.float32))
    store(1, 1, their_near_ref[...].astype(jnp.float32))
    for order, at in enumerate(far_first(messages)):
        for side in range(2):
            block = back_refs[2 * order + side][: 2 * part, :].astype(jnp.float32)
            for heads in range(2):
                source = heads if side == 0 else 1 - heads
                store(2 + side * messages + at, heads, block[source * part : (source + 1) * part])
    own = own_slots(sess_ref, req_count)
    total = own_ref[...].astype(jnp.float32).reshape(rows, model_width)
    for heads, (terms_ref, w_ref) in enumerate(((keep_ref, w_own_ref), (got_ref, w_other_ref))):
        history = []
        for distance, place in own:
            history.append(table_ref[(position(distance, serve, owners) * 2 + heads) * CAP + place])
        attended = jnp.concatenate(history, axis=0) + terms_ref[0].astype(jnp.float32)
        gates = terms_ref[1].astype(jnp.float32)
        mixed = []
        for low in range(0, width, HD):
            head = attended[:, low : low + HD]
            level = lax.rsqrt(jnp.mean(head * head, axis=-1, keepdims=True) + EPS)
            mixed.append((head * level * gates[:, low : low + HD]).astype(jnp.bfloat16))
        total = total + jnp.dot(jnp.concatenate(mixed, axis=1), w_ref[...], preferred_element_type=jnp.float32)
    out_ref[...] = total.reshape(out_ref.shape).astype(jnp.bfloat16)


def far_first(count):
    return list(reversed(range(count)))


def swap(rows):
    return lax.ppermute(rows, "serve", [(0, 1), (1, 0)])


def cross(owners, messages):
    came = []
    for at in far_first(len(messages)):
        steps = [2 * (at + 1) + side for side in range(2)]
        pairs = [(place * 2 + core_of(step), (place ^ step) * 2 + core_of(step)) for place in range(owners) for step in steps]
        came.append(lax.ppermute(messages[at], ("cache", "serve"), pairs))
    return came


def to_neighbour(owners, rows):
    return lax.ppermute(rows, "cache", [(place, place ^ 1) for place in range(owners)])


def body(candidates, input_gain, w_in, w_out, hist_keys, hist_values, request_session, hist_len, block_mask):
    owners = lax.axis_size("cache")
    req_count, half_cands, model_width = candidates.shape
    width = w_in.shape[2]
    rows = req_count * half_cands
    hist_rows = hist_keys.shape[1]
    bf16 = functools.partial(jax.ShapeDtypeStruct, dtype=jnp.bfloat16)
    sessions = request_session.reshape(-1)
    gain = input_gain.reshape(-1, HD)
    messages = owners // 2 - 1
    piece = 2 * CAP * half_cands

    session_row = request_session.reshape(1, -1)
    chosen = kernel_call(
        functools.partial(front_kernel, owners, half_cands),
        bf16(((messages + 2) * piece, 2 * rows)),
        [vmem],
    )(session_row)
    other, w_out, chosen = lax.optimization_barrier((swap(candidates), w_out, chosen))
    w_other = swap(w_out)
    out = kernel_call(message_kernel, [bf16((piece, model_width))] * (messages + 2), [vmem] * 3)(chosen, candidates, other)
    (local, near, *out), w_in = lax.optimization_barrier((out, w_in))
    weights = jnp.transpose(w_in, (1, 0, 2))
    near = to_neighbour(owners, near)
    came = cross(owners, out)
    came, near, weights = lax.optimization_barrier((came, near, weights))
    stacked = kernel_call(stack_kernel, bf16((messages * piece, model_width)), [vmem] * messages)(*came)
    visible = kernel_call(
        visible_kernel,
        [bf16((owners * piece, HD)), bf16((hist_rows, HD))],
        [vmem] * 3,
        [pltpu.VMEM((HD, owners * req_count), jnp.bfloat16)],
        flops=2 * messages * piece * model_width * width,
    )(session_row, hist_len.reshape(1, -1), lax.optimization_barrier((block_mask.T, stacked))[0])
    swapped, (hide_rows, hide_cols) = lax.optimization_barrier((swap(stacked), visible))
    local, near, keep, give = kernel_call(
        functools.partial(history_kernel, owners),
        [bf16((rows_out, width)) for rows_out in (piece // 2, piece, messages * piece, messages * piece + piece // 2)],
        [vmem] * (6 + owners // 2 + 2),
        flops=8 * owners * piece * hist_rows * width,
        moved=4 * hist_rows * width,
    )(
        gain,
        weights,
        hide_rows,
        hide_cols,
        hist_keys.reshape(hist_rows, width),
        hist_values.reshape(hist_rows, width),
        local,
        near,
        *reversed(came),
        swapped,
    )
    near = to_neighbour(owners, near)
    keep, give, w_other = lax.optimization_barrier((keep, give, w_other))
    got = swap(give)
    terms = kernel_call(
        self_kernel,
        [bf16((2, rows, width))] * 2,
        [vmem] * 4,
        [pltpu.VMEM((2 * rows, model_width), jnp.bfloat16)],
        flops=16 * rows * model_width * width,
        moved=8 * model_width * width,
    )(candidates, lax.optimization_barrier((other, give))[0], gain, weights)
    got, (keep_terms, give_terms) = lax.optimization_barrier((got, terms))
    backs = cross(owners, kernel_call(pack_kernel, [bf16((2 * piece, width))] * messages, [vmem] * 2)(keep, got))
    their_near = swap(near[piece // 2 :])
    returned = [rows_of for back in backs for rows_of in (back, swap(back[piece:]))]
    return kernel_call(
        functools.partial(output_kernel, owners),
        bf16((req_count, half_cands, model_width)),
        [smem] + [vmem] * (9 + 2 * messages),
        [pltpu.VMEM((2 * owners * CAP, half_cands, width), jnp.float32)],
        flops=8 * rows * model_width * width,
        moved=4 * model_width * width,
    )(sessions, candidates, keep_terms, swap(give_terms), w_out, w_other, local, got, near, their_near, *returned)


def solution(mesh):
    placed = (
        P(("groups", "cache"), "serve", None),
        P(),
        P(None, None, "serve"),
        P("serve", None),
        P(("groups", "cache"), None, "serve"),
        P(("groups", "cache"), None, "serve"),
        P("groups", None),
        P("groups"),
        P("groups", None),
    )
    return jax.shard_map(
        body,
        mesh=mesh,
        in_specs=placed,
        out_specs=P(("groups", "cache"), "serve", None),
        check_vma=False,
    )
```

```python
import functools

import jax
import jax.numpy as jnp
from jax import lax
from jax.experimental import pallas as pl
from jax.experimental.pallas import tpu as pltpu
from jax.sharding import PartitionSpec as P

HD = 128
BLK = 64
CAP = 2
EPS = 1e-06
SCALE = HD ** (-0.5)
HIDE = -1e30
VMEM_LIMIT = 16 * 1024 * 1024

vmem = pl.BlockSpec(memory_space=pltpu.VMEM)
smem = pl.BlockSpec(memory_space=pltpu.SMEM)


def silu_of_half(half):
    return half + half * jnp.tanh(half)


def silu(x):
    return silu_of_half(x * 0.5)


def kernel_call(body, out_shape, in_specs, scratch_shapes=(), flops=0, moved=0):
    return pl.pallas_call(
        body,
        out_shape=out_shape,
        in_specs=in_specs,
        out_specs=jax.tree.map(lambda _: vmem, out_shape),
        scratch_shapes=scratch_shapes,
        cost_estimate=pl.CostEstimate(flops=flops, bytes_accessed=moved, transcendentals=0),
        compiler_params=pltpu.CompilerParams(vmem_limit_bytes=VMEM_LIMIT),
    )


def gain_row(gain_ref):
    gain = gain_ref[...].astype(jnp.float32)
    return jnp.concatenate([gain[at : at + 1] for at in range(gain.shape[0])], axis=1)


def normed_rows(rows_ref, start, count, gain):
    rows = rows_ref[start : start + count].astype(jnp.float32)
    rows = rows.reshape(-1, rows.shape[-1])
    mean_square = jnp.mean(rows * rows, axis=-1, keepdims=True)
    return (rows * lax.rsqrt(mean_square + EPS) * gain).astype(jnp.bfloat16)


def core_of(distance):
    parity = distance
    for shift in (16, 8, 4, 2, 1):
        parity = parity ^ (parity >> shift)
    return parity & 1


def position(distance, serve, owners):
    far = jnp.where(core_of(distance) == serve, 0, owners // 2 - 1) + distance // 2 + 1
    return jnp.where(distance < 2, distance, far)


def own_slots(sess_ref, req_count):
    me = lax.axis_index("cache")
    base = me * req_count
    sessions = [sess_ref[base + request] for request in range(req_count)]
    slots = []
    for request in range(req_count):
        place = 0
        for earlier in range(request):
            place = place + (sessions[earlier] == sessions[request]).astype(jnp.int32)
        slots.append((sessions[request] ^ me, place))
    return slots


def places(sessions, per_owner):
    lane = lax.broadcasted_iota(jnp.int32, sessions.shape, 1)
    place = jnp.zeros_like(sessions)
    for back in range(1, per_owner):
        same = (pltpu.roll(sessions, back, 1) == sessions) & (lane % per_owner >= back)
        place = place + same.astype(jnp.int32)
    return place


def front_kernel(owners, sess_ref, own_ref, moved_ref, chosen_ref):
    half_cands, model_width = own_ref.shape[1:]
    me, serve = lax.axis_index("cache"), lax.axis_index("serve")
    sessions = sess_ref[...]
    requests = sessions.shape[1]
    per_owner = requests // owners
    rows = per_owner * half_cands
    distance = sessions ^ me
    at = position(distance, serve, owners)
    sent = at <= owners // 2
    code = jnp.where(sent, at * (2 * CAP) + places(sessions, per_owner), owners * (2 * CAP))
    request = lax.broadcasted_iota(jnp.int32, (requests, rows), 0)
    column = lax.broadcasted_iota(jnp.int32, (requests, rows), 1)
    spread = (request == me * per_owner + column // half_cands).astype(jnp.float32).astype(jnp.bfloat16)
    codes = jnp.broadcast_to(code, (8, requests)).astype(jnp.float32).astype(jnp.bfloat16)
    target = jnp.dot(codes, spread, preferred_element_type=jnp.float32)[:1].astype(jnp.int32)
    at = lax.broadcasted_iota(jnp.int32, chosen_ref.shape, 0)
    column = lax.broadcasted_iota(jnp.int32, chosen_ref.shape, 1)
    same = at % half_cands == column % half_cands
    own = ((at // half_cands == target) & same).astype(jnp.float32).astype(jnp.bfloat16)
    chosen_ref[...] = ((at // half_cands == target + CAP) & same).astype(jnp.float32).astype(jnp.bfloat16)
    source = own_ref[...].astype(jnp.float32).reshape(-1, model_width).astype(jnp.bfloat16)
    moved_ref[...] = jnp.dot(own, source, preferred_element_type=jnp.float32).astype(jnp.bfloat16)


def visible_kernel(sess_ref, len_ref, mask_ref, hide_rows_ref, hide_cols_ref, marks_ref):
    me, serve = lax.axis_index("cache"), lax.axis_index("serve")
    blocks, requests = mask_ref.shape
    owners = len_ref.shape[1]
    per_owner = requests // owners
    sessions = sess_ref[...]
    lane = lax.broadcasted_iota(jnp.int32, (1, requests), 1)
    at = position((lane // per_owner) ^ me, serve, owners)
    slot_of = jnp.where(sessions == me, at * CAP + places(sessions, per_owner), -1)
    slots = owners * CAP
    at_slot = lax.broadcasted_iota(jnp.int32, (slots, requests), 0)
    taken = (at_slot == slot_of).astype(jnp.float32).astype(jnp.bfloat16)
    marks_ref[...] = jnp.zeros_like(marks_ref)
    marks_ref[:blocks, :] = mask_ref[...].astype(jnp.float32).astype(jnp.bfloat16)
    seen = lax.dot_general(taken, marks_ref[...], (((1,), (1,)), ((), ())), preferred_element_type=jnp.float32)
    slot_lane = lax.broadcasted_iota(jnp.int32, (slots, HD), 1)
    hidden = jnp.where(slot_lane < blocks, (1.0 - seen) * HIDE, jnp.where(slot_lane == blocks, HIDE, 0.0))
    half = hide_rows_ref.shape[0] // slots // 2
    wide = jnp.broadcast_to(hidden.reshape(owners, 1, CAP, 1, HD), (owners, 2, CAP, half, HD))
    hide_rows_ref[...] = wide.reshape(hide_rows_ref.shape).astype(jnp.bfloat16)
    hist_rows = hide_cols_ref.shape[0]
    owner_lane = lax.broadcasted_iota(jnp.int32, (1, owners), 1)
    length = jnp.sum(jnp.where(owner_lane == me, len_ref[...], 0), axis=1, keepdims=True)
    at_row = lax.broadcasted_iota(jnp.int32, (hist_rows, HD), 0)
    at_lane = lax.broadcasted_iota(jnp.int32, (hist_rows, HD), 1)
    hide_cols_ref[...] = jnp.where(
        (at_lane == at_row // BLK) | ((at_lane == blocks) & (at_row >= length)), 1.0, 0.0
    ).astype(jnp.bfloat16)


def message_kernel(moved_ref, chosen_ref, other_ref, *out_refs):
    model_width = other_ref.shape[2]
    source = other_ref[...].astype(jnp.float32).reshape(-1, model_width).astype(jnp.bfloat16)
    rows = moved_ref[...].astype(jnp.float32) + jnp.dot(chosen_ref[...], source, preferred_element_type=jnp.float32)
    piece = out_refs[0].shape[0]
    for at, out_ref in enumerate(out_refs):
        out_ref[...] = rows[at * piece : (at + 1) * piece].astype(jnp.bfloat16)


def self_kernel(own_ref, other_ref, gain_ref, w_ref, keep_ref, give_ref, normed_ref):
    rows, width = keep_ref.shape[1:]
    gain = gain_row(gain_ref)
    normed_ref[:rows, :] = normed_rows(own_ref, 0, own_ref.shape[0], gain)
    normed_ref[rows:, :] = normed_rows(other_ref, 0, other_ref.shape[0], gain)
    normed = normed_ref[...]

    def activated(part):
        return silu(jnp.dot(normed, w_ref[part], preferred_element_type=jnp.float32)).astype(jnp.bfloat16)

    products = activated(0).astype(jnp.float32) * activated(1).astype(jnp.float32)
    values, gates = activated(2), activated(3)
    for low in range(0, width, HD):
        score = jnp.sum(products[:, low : low + HD], axis=-1, keepdims=True) * SCALE
        term = (silu(score) * values[:, low : low + HD].astype(jnp.float32)).astype(jnp.bfloat16)
        keep_ref[0, :, low : low + HD] = term[:rows]
        give_ref[0, :, low : low + HD] = term[rows:]
    keep_ref[1] = gates[:rows]
    give_ref[1] = gates[rows:]


def pack_kernel(keep_ref, got_ref, *out_refs):
    part = out_refs[0].shape[0] // 4
    for at, out_ref in enumerate(out_refs):
        for side in range(2):
            low = (2 * at + side) * part
            out_ref[2 * side * part : (2 * side + 1) * part, :] = keep_ref[low : low + part, :]
            out_ref[(2 * side + 1) * part : (2 * side + 2) * part, :] = got_ref[low : low + part, :]


def stack_kernel(*refs):
    *in_refs, out_ref = refs
    rows = in_refs[0].shape[0]
    for at, in_ref in zip(far_first(len(in_refs)), in_refs):
        out_ref[at * rows : (at + 1) * rows, :] = in_ref[...]


def history_kernel(owners, gain_ref, w_ref, hide_rows_ref, hide_cols_ref, keys_ref, values_ref, *refs):
    *slot_refs, swapped_ref, local_ref, near_ref, keep_ref, give_ref = refs
    width = near_ref.shape[1]
    per_owner = near_ref.shape[0]
    half = per_owner // 2
    far = [(ref, at * per_owner, 0, per_owner) for ref in (keep_ref, give_ref) for at in range(owners // 2 - 1)]
    local = [(local_ref, 0, 0, half), (give_ref, (owners // 2 - 1) * per_owner, half, half)]
    sources = [(ref, 0) for ref in slot_refs] + [(swapped_ref, at * per_owner) for at in range(owners // 2 - 1)]
    targets = [local, [(near_ref, 0, 0, per_owner)]] + [[target] for target in far]
    hist_rows = keys_ref.shape[0]
    span = min(256, hist_rows)
    per_step = max(1, min(owners, 256 // per_owner))
    gain = gain_row(gain_ref)
    for first in range(0, owners, per_step):
        group = range(first, min(first + per_step, owners))
        normed = jnp.concatenate([normed_rows(*sources[at], per_owner, gain) for at in group], axis=0)
        queries = silu(jnp.dot(normed, w_ref[0], preferred_element_type=jnp.float32)).astype(jnp.bfloat16)
        hide_rows = hide_rows_ref[first * per_owner : first * per_owner + queries.shape[0], :]
        for low in range(0, width, HD):
            lhs = jnp.concatenate([queries[:, low : low + HD], hide_rows], axis=1)
            total = None
            for start in range(0, hist_rows, span):
                rhs = jnp.concatenate(
                    [keys_ref[start : start + span, low : low + HD], hide_cols_ref[start : start + span, :]], axis=1
                )
                scores = lax.dot_general(lhs, rhs, (((1,), (1,)), ((), ())), preferred_element_type=jnp.float32)
                weights = silu_of_half(scores * (0.5 * SCALE)).astype(jnp.bfloat16)
                term = jnp.dot(
                    weights, values_ref[start : start + span, low : low + HD], preferred_element_type=jnp.float32
                )
                total = term if total is None else total + term
            total = total.astype(jnp.bfloat16)
            for place, at in enumerate(group):
                for out_ref, row, start, count in targets[at]:
                    low_row = place * per_owner + start
                    out_ref[row : row + count, low : low + HD] = total[low_row : low_row + count]


def output_kernel(owners, sess_ref, own_ref, keep_ref, got_ref, w_own_ref, w_other_ref, *refs):
    local_ref, given_ref, near_ref, their_near_ref, *back_refs = refs[:-2]
    out_ref, table_ref = refs[-2:]
    req_count, half_cands, model_width = own_ref.shape
    rows = req_count * half_cands
    width = model_width // 2
    serve = lax.axis_index("serve")
    part = CAP * half_cands
    messages = owners // 2 - 1

    def store(at, heads, block):
        table_ref[(at * 2 + heads) * CAP : (at * 2 + heads + 1) * CAP] = block.reshape(CAP, half_cands, width)

    store(0, 0, local_ref[...].astype(jnp.float32))
    store(0, 1, given_ref[given_ref.shape[0] - part :, :].astype(jnp.float32))
    store(1, 0, near_ref[:part, :].astype(jnp.float32))
    store(1, 1, their_near_ref[...].astype(jnp.float32))
    for order, at in enumerate(far_first(messages)):
        for side in range(2):
            block = back_refs[2 * order + side][: 2 * part, :].astype(jnp.float32)
            for heads in range(2):
                source = heads if side == 0 else 1 - heads
                store(2 + side * messages + at, heads, block[source * part : (source + 1) * part])
    own = own_slots(sess_ref, req_count)
    total = own_ref[...].astype(jnp.float32).reshape(rows, model_width)
    for heads, (terms_ref, w_ref) in enumerate(((keep_ref, w_own_ref), (got_ref, w_other_ref))):
        history = []
        for distance, place in own:
            history.append(table_ref[(position(distance, serve, owners) * 2 + heads) * CAP + place])
        attended = jnp.concatenate(history, axis=0) + terms_ref[0].astype(jnp.float32)
        gates = terms_ref[1].astype(jnp.float32)
        mixed = []
        for low in range(0, width, HD):
            head = attended[:, low : low + HD]
            level = lax.rsqrt(jnp.mean(head * head, axis=-1, keepdims=True) + EPS)
            mixed.append((head * level * gates[:, low : low + HD]).astype(jnp.bfloat16))
        total = total + jnp.dot(jnp.concatenate(mixed, axis=1), w_ref[...], preferred_element_type=jnp.float32)
    out_ref[...] = total.reshape(out_ref.shape).astype(jnp.bfloat16)


def far_first(count):
    return list(reversed(range(count)))


def swap(rows):
    return lax.ppermute(rows, "serve", [(0, 1), (1, 0)])


def cross(owners, messages):
    came = []
    for at in far_first(len(messages)):
        steps = [2 * (at + 1) + side for side in range(2)]
        pairs = [(place * 2 + core_of(step), (place ^ step) * 2 + core_of(step)) for place in range(owners) for step in steps]
        came.append(lax.ppermute(messages[at], ("cache", "serve"), pairs))
    return came


def to_neighbour(owners, rows):
    return lax.ppermute(rows, "cache", [(place, place ^ 1) for place in range(owners)])


def body(candidates, input_gain, w_in, w_out, hist_keys, hist_values, request_session, hist_len, block_mask):
    owners = lax.axis_size("cache")
    req_count, half_cands, model_width = candidates.shape
    width = w_in.shape[2]
    rows = req_count * half_cands
    hist_rows = hist_keys.shape[1]
    bf16 = functools.partial(jax.ShapeDtypeStruct, dtype=jnp.bfloat16)
    sessions = request_session.reshape(-1)
    gain = input_gain.reshape(-1, HD)
    messages = owners // 2 - 1
    piece = 2 * CAP * half_cands

    session_row = request_session.reshape(1, -1)
    placed = kernel_call(
        functools.partial(front_kernel, owners),
        [bf16(((messages + 2) * piece, columns)) for columns in (model_width, rows)],
        [vmem] * 2,
    )(session_row, candidates)
    other, placed = lax.optimization_barrier((swap(candidates), placed))
    out = kernel_call(message_kernel, [bf16((piece, model_width))] * (messages + 2), [vmem] * 3)(*placed, other)
    (local, near, *out), w_in = lax.optimization_barrier((out, w_in))
    weights = jnp.transpose(w_in, (1, 0, 2))
    near = to_neighbour(owners, near)
    came = cross(owners, out)
    came, near, weights = lax.optimization_barrier((came, near, weights))
    stacked = kernel_call(stack_kernel, bf16((messages * piece, model_width)), [vmem] * messages)(*came)
    visible = kernel_call(
        visible_kernel,
        [bf16((owners * piece, HD)), bf16((hist_rows, HD))],
        [vmem] * 3,
        [pltpu.VMEM((HD, owners * req_count), jnp.bfloat16)],
        flops=2 * messages * piece * model_width * width,
    )(session_row, hist_len.reshape(1, -1), lax.optimization_barrier((block_mask.T, stacked))[0])
    swapped, (hide_rows, hide_cols), w_out = lax.optimization_barrier((swap(stacked), visible, w_out))
    w_other = swap(w_out)
    local, near, keep, give = kernel_call(
        functools.partial(history_kernel, owners),
        [bf16((rows_out, width)) for rows_out in (piece // 2, piece, messages * piece, messages * piece + piece // 2)],
        [vmem] * (6 + owners // 2 + 2),
        flops=8 * owners * piece * hist_rows * width,
        moved=4 * hist_rows * width,
    )(
        gain,
        weights,
        hide_rows,
        hide_cols,
        hist_keys.reshape(hist_rows, width),
        hist_values.reshape(hist_rows, width),
        local,
        near,
        *reversed(came),
        swapped,
    )
    near = to_neighbour(owners, near)
    keep, give, w_other = lax.optimization_barrier((keep, give, w_other))
    got = swap(give)
    terms = kernel_call(
        self_kernel,
        [bf16((2, rows, width))] * 2,
        [vmem] * 4,
        [pltpu.VMEM((2 * rows, model_width), jnp.bfloat16)],
        flops=16 * rows * model_width * width,
        moved=8 * model_width * width,
    )(candidates, lax.optimization_barrier((other, give))[0], gain, weights)
    got, (keep_terms, give_terms) = lax.optimization_barrier((got, terms))
    backs = cross(owners, kernel_call(pack_kernel, [bf16((2 * piece, width))] * messages, [vmem] * 2)(keep, got))
    their_near = swap(near[piece // 2 :])
    returned = [rows_of for back in backs for rows_of in (back, swap(back[piece:]))]
    return kernel_call(
        functools.partial(output_kernel, owners),
        bf16((req_count, half_cands, model_width)),
        [smem] + [vmem] * (9 + 2 * messages),
        [pltpu.VMEM((2 * owners * CAP, half_cands, width), jnp.float32)],
        flops=8 * rows * model_width * width,
        moved=4 * model_width * width,
    )(sessions, candidates, keep_terms, swap(give_terms), w_out, w_other, local, got, near, their_near, *returned)


def solution(mesh):
    placed = (
        P(("groups", "cache"), "serve", None),
        P(),
        P(None, None, "serve"),
        P("serve", None),
        P(("groups", "cache"), None, "serve"),
        P(("groups", "cache"), None, "serve"),
        P("groups", None),
        P("groups"),
        P("groups", None),
    )
    return jax.shard_map(
        body,
        mesh=mesh,
        in_specs=placed,
        out_specs=P(("groups", "cache"), "serve", None),
        check_vma=False,
    )
```

```python
import functools

import jax
import jax.numpy as jnp
from jax import lax
from jax.experimental import pallas as pl
from jax.experimental.pallas import tpu as pltpu
from jax.sharding import PartitionSpec as P

HD = 128
BLK = 64
CAP = 2
EPS = 1e-06
SCALE = HD ** (-0.5)
HIDE = -1e30
VMEM_LIMIT = 16 * 1024 * 1024

vmem = pl.BlockSpec(memory_space=pltpu.VMEM)
smem = pl.BlockSpec(memory_space=pltpu.SMEM)


def silu_of_half(half):
    return half + half * jnp.tanh(half)


def silu(x):
    return silu_of_half(x * 0.5)


def kernel_call(body, out_shape, in_specs, scratch_shapes=(), flops=0, moved=0):
    return pl.pallas_call(
        body,
        out_shape=out_shape,
        in_specs=in_specs,
        out_specs=jax.tree.map(lambda _: vmem, out_shape),
        scratch_shapes=scratch_shapes,
        cost_estimate=pl.CostEstimate(flops=flops, bytes_accessed=moved, transcendentals=0),
        compiler_params=pltpu.CompilerParams(vmem_limit_bytes=VMEM_LIMIT),
    )


def gain_row(gain_ref):
    gain = gain_ref[...].astype(jnp.float32)
    return jnp.concatenate([gain[at : at + 1] for at in range(gain.shape[0])], axis=1)


def normed_rows(rows_ref, start, count, gain):
    rows = rows_ref[start : start + count].astype(jnp.float32)
    rows = rows.reshape(-1, rows.shape[-1])
    mean_square = jnp.mean(rows * rows, axis=-1, keepdims=True)
    return (rows * lax.rsqrt(mean_square + EPS) * gain).astype(jnp.bfloat16)


def core_of(distance):
    parity = distance
    for shift in (16, 8, 4, 2, 1):
        parity = parity ^ (parity >> shift)
    return parity & 1


def position(distance, serve, owners):
    far = jnp.where(core_of(distance) == serve, 0, owners // 2 - 1) + distance // 2 + 1
    return jnp.where(distance < 2, distance, far)


def own_slots(sess_ref, req_count):
    me = lax.axis_index("cache")
    base = me * req_count
    sessions = [sess_ref[base + request] for request in range(req_count)]
    slots = []
    for request in range(req_count):
        place = 0
        for earlier in range(request):
            place = place + (sessions[earlier] == sessions[request]).astype(jnp.int32)
        slots.append((sessions[request] ^ me, place))
    return slots


def places(sessions, per_owner):
    lane = lax.broadcasted_iota(jnp.int32, sessions.shape, 1)
    place = jnp.zeros_like(sessions)
    for back in range(1, per_owner):
        same = (pltpu.roll(sessions, back, 1) == sessions) & (lane % per_owner >= back)
        place = place + same.astype(jnp.int32)
    return place


def front_kernel(owners, sess_ref, own_ref, moved_ref, chosen_ref):
    half_cands, model_width = own_ref.shape[1:]
    me, serve = lax.axis_index("cache"), lax.axis_index("serve")
    sessions = sess_ref[...]
    requests = sessions.shape[1]
    per_owner = requests // owners
    rows = per_owner * half_cands
    distance = sessions ^ me
    at = position(distance, serve, owners)
    sent = at <= owners // 2
    code = jnp.where(sent, at * (2 * CAP) + places(sessions, per_owner), owners * (2 * CAP))
    request = lax.broadcasted_iota(jnp.int32, (requests, rows), 0)
    column = lax.broadcasted_iota(jnp.int32, (requests, rows), 1)
    spread = (request == me * per_owner + column // half_cands).astype(jnp.float32).astype(jnp.bfloat16)
    codes = jnp.broadcast_to(code, (8, requests)).astype(jnp.float32).astype(jnp.bfloat16)
    target = jnp.dot(codes, spread, preferred_element_type=jnp.float32)[:1].astype(jnp.int32)
    at = lax.broadcasted_iota(jnp.int32, chosen_ref.shape, 0)
    column = lax.broadcasted_iota(jnp.int32, chosen_ref.shape, 1)
    same = at % half_cands == column % half_cands
    own = ((at // half_cands == target) & same).astype(jnp.float32).astype(jnp.bfloat16)
    chosen_ref[...] = ((at // half_cands == target + CAP) & same).astype(jnp.float32).astype(jnp.bfloat16)
    source = own_ref[...].astype(jnp.float32).reshape(-1, model_width).astype(jnp.bfloat16)
    moved_ref[...] = jnp.dot(own, source, preferred_element_type=jnp.float32).astype(jnp.bfloat16)


def visible_kernel(sess_ref, len_ref, mask_ref, hide_rows_ref, hide_cols_ref, marks_ref):
    me, serve = lax.axis_index("cache"), lax.axis_index("serve")
    blocks, requests = mask_ref.shape
    owners = len_ref.shape[1]
    per_owner = requests // owners
    sessions = sess_ref[...]
    lane = lax.broadcasted_iota(jnp.int32, (1, requests), 1)
    at = position((lane // per_owner) ^ me, serve, owners)
    slot_of = jnp.where(sessions == me, at * CAP + places(sessions, per_owner), -1)
    slots = owners * CAP
    at_slot = lax.broadcasted_iota(jnp.int32, (slots, requests), 0)
    taken = (at_slot == slot_of).astype(jnp.float32).astype(jnp.bfloat16)
    marks_ref[...] = jnp.zeros_like(marks_ref)
    marks_ref[:blocks, :] = mask_ref[...].astype(jnp.float32).astype(jnp.bfloat16)
    seen = lax.dot_general(taken, marks_ref[...], (((1,), (1,)), ((), ())), preferred_element_type=jnp.float32)
    slot_lane = lax.broadcasted_iota(jnp.int32, (slots, HD), 1)
    hidden = jnp.where(slot_lane < blocks, (1.0 - seen) * HIDE, jnp.where(slot_lane == blocks, HIDE, 0.0))
    half = hide_rows_ref.shape[0] // slots // 2
    wide = jnp.broadcast_to(hidden.reshape(owners, 1, CAP, 1, HD), (owners, 2, CAP, half, HD))
    hide_rows_ref[...] = wide.reshape(hide_rows_ref.shape).astype(jnp.bfloat16)
    hist_rows = hide_cols_ref.shape[0]
    owner_lane = lax.broadcasted_iota(jnp.int32, (1, owners), 1)
    length = jnp.sum(jnp.where(owner_lane == me, len_ref[...], 0), axis=1, keepdims=True)
    at_row = lax.broadcasted_iota(jnp.int32, (hist_rows, HD), 0)
    at_lane = lax.broadcasted_iota(jnp.int32, (hist_rows, HD), 1)
    hide_cols_ref[...] = jnp.where(
        (at_lane == at_row // BLK) | ((at_lane == blocks) & (at_row >= length)), 1.0, 0.0
    ).astype(jnp.bfloat16)


def message_kernel(moved_ref, chosen_ref, other_ref, *out_refs):
    model_width = other_ref.shape[2]
    source = other_ref[...].astype(jnp.float32).reshape(-1, model_width).astype(jnp.bfloat16)
    rows = moved_ref[...].astype(jnp.float32) + jnp.dot(chosen_ref[...], source, preferred_element_type=jnp.float32)
    piece = out_refs[0].shape[0]
    for at, out_ref in enumerate(out_refs):
        out_ref[...] = rows[at * piece : (at + 1) * piece].astype(jnp.bfloat16)


def self_kernel(own_ref, other_ref, gain_ref, w_ref, keep_ref, give_ref, normed_ref):
    rows, width = keep_ref.shape[1:]
    gain = gain_row(gain_ref)
    normed_ref[:rows, :] = normed_rows(own_ref, 0, own_ref.shape[0], gain)
    normed_ref[rows:, :] = normed_rows(other_ref, 0, other_ref.shape[0], gain)
    normed = normed_ref[...]

    def activated(part):
        return silu(jnp.dot(normed, w_ref[part], preferred_element_type=jnp.float32)).astype(jnp.bfloat16)

    products = activated(0).astype(jnp.float32) * activated(1).astype(jnp.float32)
    values, gates = activated(2), activated(3)
    for low in range(0, width, HD):
        score = jnp.sum(products[:, low : low + HD], axis=-1, keepdims=True) * SCALE
        term = (silu(score) * values[:, low : low + HD].astype(jnp.float32)).astype(jnp.bfloat16)
        keep_ref[0, :, low : low + HD] = term[:rows]
        give_ref[0, :, low : low + HD] = term[rows:]
    keep_ref[1] = gates[:rows]
    give_ref[1] = gates[rows:]


def pack_kernel(keep_ref, got_ref, *out_refs):
    part = out_refs[0].shape[0] // 4
    for at, out_ref in enumerate(out_refs):
        for side in range(2):
            low = (2 * at + side) * part
            out_ref[2 * side * part : (2 * side + 1) * part, :] = keep_ref[low : low + part, :]
            out_ref[(2 * side + 1) * part : (2 * side + 2) * part, :] = got_ref[low : low + part, :]


def stack_kernel(*refs):
    *in_refs, out_ref = refs
    rows = in_refs[0].shape[0]
    for at, in_ref in zip(far_first(len(in_refs)), in_refs):
        out_ref[at * rows : (at + 1) * rows, :] = in_ref[...]


def history_kernel(owners, gain_ref, w_ref, hide_rows_ref, hide_cols_ref, keys_ref, values_ref, *refs):
    *slot_refs, swapped_ref, local_ref, near_ref, keep_ref, give_ref = refs
    width = near_ref.shape[1]
    per_owner = near_ref.shape[0]
    half = per_owner // 2
    far = [(ref, at * per_owner, 0, per_owner) for ref in (keep_ref, give_ref) for at in range(owners // 2 - 1)]
    local = [(local_ref, 0, 0, half), (give_ref, (owners // 2 - 1) * per_owner, half, half)]
    sources = [(ref, 0) for ref in slot_refs] + [(swapped_ref, at * per_owner) for at in range(owners // 2 - 1)]
    targets = [local, [(near_ref, 0, 0, per_owner)]] + [[target] for target in far]
    hist_rows = keys_ref.shape[0]
    span = min(256, hist_rows)
    per_step = max(1, min(owners, 256 // per_owner))
    gain = gain_row(gain_ref)
    for first in range(0, owners, per_step):
        group = range(first, min(first + per_step, owners))
        normed = jnp.concatenate([normed_rows(*sources[at], per_owner, gain) for at in group], axis=0)
        queries = silu(jnp.dot(normed, w_ref[0], preferred_element_type=jnp.float32))
        queries = (queries * (0.5 * SCALE)).astype(jnp.bfloat16)
        hide_rows = hide_rows_ref[first * per_owner : first * per_owner + queries.shape[0], :]
        for low in range(0, width, HD):
            lhs = jnp.concatenate([queries[:, low : low + HD], hide_rows], axis=1)
            total = None
            for start in range(0, hist_rows, span):
                rhs = jnp.concatenate(
                    [keys_ref[start : start + span, low : low + HD], hide_cols_ref[start : start + span, :]], axis=1
                )
                half_scores = lax.dot_general(lhs, rhs, (((1,), (1,)), ((), ())), preferred_element_type=jnp.float32)
                weights = silu_of_half(half_scores.astype(jnp.bfloat16))
                term = jnp.dot(
                    weights, values_ref[start : start + span, low : low + HD], preferred_element_type=jnp.float32
                )
                total = term if total is None else total + term
            total = total.astype(jnp.bfloat16)
            for place, at in enumerate(group):
                for out_ref, row, start, count in targets[at]:
                    low_row = place * per_owner + start
                    out_ref[row : row + count, low : low + HD] = total[low_row : low_row + count]


def output_kernel(owners, sess_ref, own_ref, keep_ref, got_ref, w_own_ref, w_other_ref, *refs):
    local_ref, given_ref, near_ref, their_near_ref, *back_refs = refs[:-2]
    out_ref, table_ref = refs[-2:]
    req_count, half_cands, model_width = own_ref.shape
    rows = req_count * half_cands
    width = model_width // 2
    serve = lax.axis_index("serve")
    part = CAP * half_cands
    messages = owners // 2 - 1

    def store(at, heads, block):
        table_ref[(at * 2 + heads) * CAP : (at * 2 + heads + 1) * CAP] = block.reshape(CAP, half_cands, width)

    store(0, 0, local_ref[...].astype(jnp.float32))
    store(0, 1, given_ref[given_ref.shape[0] - part :, :].astype(jnp.float32))
    store(1, 0, near_ref[:part, :].astype(jnp.float32))
    store(1, 1, their_near_ref[...].astype(jnp.float32))
    for order, at in enumerate(far_first(messages)):
        for side in range(2):
            block = back_refs[2 * order + side][: 2 * part, :].astype(jnp.float32)
            for heads in range(2):
                source = heads if side == 0 else 1 - heads
                store(2 + side * messages + at, heads, block[source * part : (source + 1) * part])
    own = own_slots(sess_ref, req_count)
    total = own_ref[...].astype(jnp.float32).reshape(rows, model_width)
    for heads, (terms_ref, w_ref) in enumerate(((keep_ref, w_own_ref), (got_ref, w_other_ref))):
        history = []
        for distance, place in own:
            history.append(table_ref[(position(distance, serve, owners) * 2 + heads) * CAP + place])
        attended = jnp.concatenate(history, axis=0) + terms_ref[0].astype(jnp.float32)
        gates = terms_ref[1].astype(jnp.float32)
        mixed = []
        for low in range(0, width, HD):
            head = attended[:, low : low + HD]
            level = lax.rsqrt(jnp.mean(head * head, axis=-1, keepdims=True) + EPS)
            mixed.append((head * level * gates[:, low : low + HD]).astype(jnp.bfloat16))
        total = total + jnp.dot(jnp.concatenate(mixed, axis=1), w_ref[...], preferred_element_type=jnp.float32)
    out_ref[...] = total.reshape(out_ref.shape).astype(jnp.bfloat16)


def far_first(count):
    return list(reversed(range(count)))


def swap(rows):
    return lax.ppermute(rows, "serve", [(0, 1), (1, 0)])


def cross(owners, messages):
    came = []
    for at in far_first(len(messages)):
        steps = [2 * (at + 1) + side for side in range(2)]
        pairs = [(place * 2 + core_of(step), (place ^ step) * 2 + core_of(step)) for place in range(owners) for step in steps]
        came.append(lax.ppermute(messages[at], ("cache", "serve"), pairs))
    return came


def to_neighbour(owners, rows):
    return lax.ppermute(rows, "cache", [(place, place ^ 1) for place in range(owners)])


def body(candidates, input_gain, w_in, w_out, hist_keys, hist_values, request_session, hist_len, block_mask):
    owners = lax.axis_size("cache")
    req_count, half_cands, model_width = candidates.shape
    width = w_in.shape[2]
    rows = req_count * half_cands
    hist_rows = hist_keys.shape[1]
    bf16 = functools.partial(jax.ShapeDtypeStruct, dtype=jnp.bfloat16)
    sessions = request_session.reshape(-1)
    gain = input_gain.reshape(-1, HD)
    messages = owners // 2 - 1
    piece = 2 * CAP * half_cands

    session_row = request_session.reshape(1, -1)
    placed = kernel_call(
        functools.partial(front_kernel, owners),
        [bf16(((messages + 2) * piece, columns)) for columns in (model_width, rows)],
        [vmem] * 2,
    )(session_row, candidates)
    other, placed = lax.optimization_barrier((swap(candidates), placed))
    out = kernel_call(message_kernel, [bf16((piece, model_width))] * (messages + 2), [vmem] * 3)(*placed, other)
    (local, near, *out), w_in = lax.optimization_barrier((out, w_in))
    weights = jnp.transpose(w_in, (1, 0, 2))
    near = to_neighbour(owners, near)
    came = cross(owners, out)
    came, near, weights = lax.optimization_barrier((came, near, weights))
    stacked = kernel_call(stack_kernel, bf16((messages * piece, model_width)), [vmem] * messages)(*came)
    visible = kernel_call(
        visible_kernel,
        [bf16((owners * piece, HD)), bf16((hist_rows, HD))],
        [vmem] * 3,
        [pltpu.VMEM((HD, owners * req_count), jnp.bfloat16)],
        flops=2 * messages * piece * model_width * width,
    )(session_row, hist_len.reshape(1, -1), lax.optimization_barrier((block_mask.T, stacked))[0])
    swapped, (hide_rows, hide_cols), w_out = lax.optimization_barrier((swap(stacked), visible, w_out))
    w_other = swap(w_out)
    local, near, keep, give = kernel_call(
        functools.partial(history_kernel, owners),
        [bf16((rows_out, width)) for rows_out in (piece // 2, piece, messages * piece, messages * piece + piece // 2)],
        [vmem] * (6 + owners // 2 + 2),
        flops=8 * owners * piece * hist_rows * width,
        moved=4 * hist_rows * width,
    )(
        gain,
        weights,
        hide_rows,
        hide_cols,
        hist_keys.reshape(hist_rows, width),
        hist_values.reshape(hist_rows, width),
        local,
        near,
        *reversed(came),
        swapped,
    )
    near = to_neighbour(owners, near)
    keep, give, w_other = lax.optimization_barrier((keep, give, w_other))
    got = swap(give)
    terms = kernel_call(
        self_kernel,
        [bf16((2, rows, width))] * 2,
        [vmem] * 4,
        [pltpu.VMEM((2 * rows, model_width), jnp.bfloat16)],
        flops=16 * rows * model_width * width,
        moved=8 * model_width * width,
    )(candidates, lax.optimization_barrier((other, give))[0], gain, weights)
    got, (keep_terms, give_terms) = lax.optimization_barrier((got, terms))
    backs = cross(owners, kernel_call(pack_kernel, [bf16((2 * piece, width))] * messages, [vmem] * 2)(keep, got))
    their_near = swap(near[piece // 2 :])
    returned = [rows_of for back in backs for rows_of in (back, swap(back[piece:]))]
    return kernel_call(
        functools.partial(output_kernel, owners),
        bf16((req_count, half_cands, model_width)),
        [smem] + [vmem] * (9 + 2 * messages),
        [pltpu.VMEM((2 * owners * CAP, half_cands, width), jnp.float32)],
        flops=8 * rows * model_width * width,
        moved=4 * model_width * width,
    )(sessions, candidates, keep_terms, swap(give_terms), w_out, w_other, local, got, near, their_near, *returned)


def solution(mesh):
    placed = (
        P(("groups", "cache"), "serve", None),
        P(),
        P(None, None, "serve"),
        P("serve", None),
        P(("groups", "cache"), None, "serve"),
        P(("groups", "cache"), None, "serve"),
        P("groups", None),
        P("groups"),
        P("groups", None),
    )
    return jax.shard_map(
        body,
        mesh=mesh,
        in_specs=placed,
        out_specs=P(("groups", "cache"), "serve", None),
        check_vma=False,
    )
```

```python
import functools

import jax
import jax.numpy as jnp
from jax import lax
from jax.experimental import pallas as pl
from jax.experimental.pallas import tpu as pltpu
from jax.sharding import PartitionSpec as P

HD = 128
BLK = 64
CAP = 2
EPS = 1e-06
SCALE = HD ** (-0.5)
HIDE = -1e30
VMEM_LIMIT = 16 * 1024 * 1024

vmem = pl.BlockSpec(memory_space=pltpu.VMEM)
smem = pl.BlockSpec(memory_space=pltpu.SMEM)


def silu_of_half(half):
    return half + half * jnp.tanh(half)


def silu(x):
    return silu_of_half(x * 0.5)


def kernel_call(body, out_shape, in_specs, scratch_shapes=(), flops=0, moved=0):
    return pl.pallas_call(
        body,
        out_shape=out_shape,
        in_specs=in_specs,
        out_specs=jax.tree.map(lambda _: vmem, out_shape),
        scratch_shapes=scratch_shapes,
        cost_estimate=pl.CostEstimate(flops=flops, bytes_accessed=moved, transcendentals=0),
        compiler_params=pltpu.CompilerParams(vmem_limit_bytes=VMEM_LIMIT),
    )


def gain_row(gain_ref):
    gain = gain_ref[...].astype(jnp.float32)
    return jnp.concatenate([gain[at : at + 1] for at in range(gain.shape[0])], axis=1)


def normed_rows(rows_ref, start, count, gain):
    rows = rows_ref[start : start + count].astype(jnp.float32)
    rows = rows.reshape(-1, rows.shape[-1])
    mean_square = jnp.mean(rows * rows, axis=-1, keepdims=True)
    return (rows * lax.rsqrt(mean_square + EPS) * gain).astype(jnp.bfloat16)


def core_of(distance):
    parity = distance
    for shift in (16, 8, 4, 2, 1):
        parity = parity ^ (parity >> shift)
    return parity & 1


def position(distance, serve, owners):
    far = jnp.where(core_of(distance) == serve, 0, owners // 2 - 1) + distance // 2 + 1
    return jnp.where(distance < 2, distance, far)


def own_slots(sess_ref, req_count):
    me = lax.axis_index("cache")
    base = me * req_count
    sessions = [sess_ref[base + request] for request in range(req_count)]
    slots = []
    for request in range(req_count):
        place = 0
        for earlier in range(request):
            place = place + (sessions[earlier] == sessions[request]).astype(jnp.int32)
        slots.append((sessions[request] ^ me, place))
    return slots


def places(sessions, per_owner):
    lane = lax.broadcasted_iota(jnp.int32, sessions.shape, 1)
    place = jnp.zeros_like(sessions)
    for back in range(1, per_owner):
        same = (pltpu.roll(sessions, back, 1) == sessions) & (lane % per_owner >= back)
        place = place + same.astype(jnp.int32)
    return place


def front_kernel(owners, sess_ref, own_ref, moved_ref, chosen_ref):
    half_cands, model_width = own_ref.shape[1:]
    me, serve = lax.axis_index("cache"), lax.axis_index("serve")
    sessions = sess_ref[...]
    requests = sessions.shape[1]
    per_owner = requests // owners
    rows = per_owner * half_cands
    distance = sessions ^ me
    at = position(distance, serve, owners)
    sent = at <= owners // 2
    code = jnp.where(sent, at * (2 * CAP) + places(sessions, per_owner), owners * (2 * CAP))
    request = lax.broadcasted_iota(jnp.int32, (requests, rows), 0)
    column = lax.broadcasted_iota(jnp.int32, (requests, rows), 1)
    spread = (request == me * per_owner + column // half_cands).astype(jnp.float32).astype(jnp.bfloat16)
    codes = jnp.broadcast_to(code, (8, requests)).astype(jnp.float32).astype(jnp.bfloat16)
    target = jnp.dot(codes, spread, preferred_element_type=jnp.float32)[:1].astype(jnp.int32)
    at = lax.broadcasted_iota(jnp.int32, chosen_ref.shape, 0)
    column = lax.broadcasted_iota(jnp.int32, chosen_ref.shape, 1)
    same = at % half_cands == column % half_cands
    own = ((at // half_cands == target) & same).astype(jnp.float32).astype(jnp.bfloat16)
    chosen_ref[...] = ((at // half_cands == target + CAP) & same).astype(jnp.float32).astype(jnp.bfloat16)
    source = own_ref[...].astype(jnp.float32).reshape(-1, model_width).astype(jnp.bfloat16)
    moved_ref[...] = jnp.dot(own, source, preferred_element_type=jnp.float32).astype(jnp.bfloat16)


def visible_kernel(sess_ref, len_ref, mask_ref, hide_rows_ref, hide_cols_ref, marks_ref):
    me, serve = lax.axis_index("cache"), lax.axis_index("serve")
    blocks, requests = mask_ref.shape
    owners = len_ref.shape[1]
    per_owner = requests // owners
    sessions = sess_ref[...]
    lane = lax.broadcasted_iota(jnp.int32, (1, requests), 1)
    at = position((lane // per_owner) ^ me, serve, owners)
    slot_of = jnp.where(sessions == me, at * CAP + places(sessions, per_owner), -1)
    slots = owners * CAP
    at_slot = lax.broadcasted_iota(jnp.int32, (slots, requests), 0)
    taken = (at_slot == slot_of).astype(jnp.float32).astype(jnp.bfloat16)
    marks_ref[...] = jnp.zeros_like(marks_ref)
    marks_ref[:blocks, :] = mask_ref[...].astype(jnp.float32).astype(jnp.bfloat16)
    seen = lax.dot_general(taken, marks_ref[...], (((1,), (1,)), ((), ())), preferred_element_type=jnp.float32)
    slot_lane = lax.broadcasted_iota(jnp.int32, (slots, HD), 1)
    hidden = jnp.where(slot_lane < blocks, (1.0 - seen) * HIDE, jnp.where(slot_lane == blocks, HIDE, 0.0))
    half = hide_rows_ref.shape[0] // slots // 2
    wide = jnp.broadcast_to(hidden.reshape(owners, 1, CAP, 1, HD), (owners, 2, CAP, half, HD))
    hide_rows_ref[...] = wide.reshape(hide_rows_ref.shape).astype(jnp.bfloat16)
    hist_rows = hide_cols_ref.shape[0]
    owner_lane = lax.broadcasted_iota(jnp.int32, (1, owners), 1)
    length = jnp.sum(jnp.where(owner_lane == me, len_ref[...], 0), axis=1, keepdims=True)
    at_row = lax.broadcasted_iota(jnp.int32, (hist_rows, HD), 0)
    at_lane = lax.broadcasted_iota(jnp.int32, (hist_rows, HD), 1)
    hide_cols_ref[...] = jnp.where(
        (at_lane == at_row // BLK) | ((at_lane == blocks) & (at_row >= length)), 1.0, 0.0
    ).astype(jnp.bfloat16)


def message_kernel(moved_ref, chosen_ref, other_ref, *out_refs):
    model_width = other_ref.shape[2]
    source = other_ref[...].astype(jnp.float32).reshape(-1, model_width).astype(jnp.bfloat16)
    rows = moved_ref[...].astype(jnp.float32) + jnp.dot(chosen_ref[...], source, preferred_element_type=jnp.float32)
    piece = out_refs[0].shape[0]
    for at, out_ref in enumerate(out_refs):
        out_ref[...] = rows[at * piece : (at + 1) * piece].astype(jnp.bfloat16)


def self_kernel(own_ref, other_ref, gain_ref, w_ref, keep_ref, give_ref, normed_ref):
    rows, width = keep_ref.shape[1:]
    gain = gain_row(gain_ref)
    normed_ref[:rows, :] = normed_rows(own_ref, 0, own_ref.shape[0], gain)
    normed_ref[rows:, :] = normed_rows(other_ref, 0, other_ref.shape[0], gain)
    normed = normed_ref[...]

    def activated(part):
        return silu(jnp.dot(normed, w_ref[part], preferred_element_type=jnp.float32)).astype(jnp.bfloat16)

    products = activated(0).astype(jnp.float32) * activated(1).astype(jnp.float32)
    values, gates = activated(2), activated(3)
    for low in range(0, width, HD):
        score = jnp.sum(products[:, low : low + HD], axis=-1, keepdims=True) * SCALE
        term = (silu(score) * values[:, low : low + HD].astype(jnp.float32)).astype(jnp.bfloat16)
        keep_ref[0, :, low : low + HD] = term[:rows]
        give_ref[0, :, low : low + HD] = term[rows:]
    keep_ref[1] = gates[:rows]
    give_ref[1] = gates[rows:]


def pack_kernel(keep_ref, got_ref, *out_refs):
    part = out_refs[0].shape[0] // 4
    for at, out_ref in enumerate(out_refs):
        for side in range(2):
            low = (2 * at + side) * part
            out_ref[2 * side * part : (2 * side + 1) * part, :] = keep_ref[low : low + part, :]
            out_ref[(2 * side + 1) * part : (2 * side + 2) * part, :] = got_ref[low : low + part, :]


def stack_kernel(*refs):
    *in_refs, out_ref = refs
    rows = in_refs[0].shape[0]
    for at, in_ref in zip(far_first(len(in_refs)), in_refs):
        out_ref[at * rows : (at + 1) * rows, :] = in_ref[...]


def history_kernel(owners, gain_ref, w_ref, hide_rows_ref, hide_cols_ref, keys_ref, values_ref, *refs):
    *slot_refs, swapped_ref, local_ref, near_ref, keep_ref, give_ref = refs
    width = near_ref.shape[1]
    per_owner = near_ref.shape[0]
    half = per_owner // 2
    far = [(ref, at * per_owner, 0, per_owner) for ref in (keep_ref, give_ref) for at in range(owners // 2 - 1)]
    local = [(local_ref, 0, 0, half), (give_ref, (owners // 2 - 1) * per_owner, half, half)]
    sources = [(ref, 0) for ref in slot_refs] + [(swapped_ref, at * per_owner) for at in range(owners // 2 - 1)]
    targets = [local, [(near_ref, 0, 0, per_owner)]] + [[target] for target in far]
    hist_rows = keys_ref.shape[0]
    span = min(256, hist_rows)
    per_step = max(1, min(owners, 256 // per_owner))
    gain = gain_row(gain_ref)
    for first in range(0, owners, per_step):
        group = range(first, min(first + per_step, owners))
        normed = jnp.concatenate([normed_rows(*sources[at], per_owner, gain) for at in group], axis=0)
        queries = silu(jnp.dot(normed, w_ref[0], preferred_element_type=jnp.float32)).astype(jnp.bfloat16)
        hide_rows = hide_rows_ref[first * per_owner : first * per_owner + queries.shape[0], :]
        for low in range(0, width, HD):
            asked = jnp.concatenate([queries[:, low : low + HD], hide_rows], axis=1)
            total = None
            for start in range(0, hist_rows, span):
                kept = jnp.concatenate(
                    [keys_ref[start : start + span, low : low + HD], hide_cols_ref[start : start + span, :]], axis=1
                )
                scores = lax.dot_general(kept, asked, (((1,), (1,)), ((), ())), preferred_element_type=jnp.float32)
                weights = silu_of_half(scores * (0.5 * SCALE)).astype(jnp.bfloat16)
                term = lax.dot_general(
                    values_ref[start : start + span, low : low + HD],
                    weights,
                    (((0,), (0,)), ((), ())),
                    preferred_element_type=jnp.float32,
                )
                total = term if total is None else total + term
            total = total.T.astype(jnp.bfloat16)
            for place, at in enumerate(group):
                for out_ref, row, start, count in targets[at]:
                    low_row = place * per_owner + start
                    out_ref[row : row + count, low : low + HD] = total[low_row : low_row + count]


def output_kernel(owners, sess_ref, own_ref, keep_ref, got_ref, w_own_ref, w_other_ref, *refs):
    local_ref, given_ref, near_ref, their_near_ref, *back_refs = refs[:-2]
    out_ref, table_ref = refs[-2:]
    req_count, half_cands, model_width = own_ref.shape
    rows = req_count * half_cands
    width = model_width // 2
    serve = lax.axis_index("serve")
    part = CAP * half_cands
    messages = owners // 2 - 1

    def store(at, heads, block):
        table_ref[(at * 2 + heads) * CAP : (at * 2 + heads + 1) * CAP] = block.reshape(CAP, half_cands, width)

    store(0, 0, local_ref[...].astype(jnp.float32))
    store(0, 1, given_ref[given_ref.shape[0] - part :, :].astype(jnp.float32))
    store(1, 0, near_ref[:part, :].astype(jnp.float32))
    store(1, 1, their_near_ref[...].astype(jnp.float32))
    for order, at in enumerate(far_first(messages)):
        for side in range(2):
            block = back_refs[2 * order + side][: 2 * part, :].astype(jnp.float32)
            for heads in range(2):
                source = heads if side == 0 else 1 - heads
                store(2 + side * messages + at, heads, block[source * part : (source + 1) * part])
    own = own_slots(sess_ref, req_count)
    total = own_ref[...].astype(jnp.float32).reshape(rows, model_width)
    for heads, (terms_ref, w_ref) in enumerate(((keep_ref, w_own_ref), (got_ref, w_other_ref))):
        history = []
        for distance, place in own:
            history.append(table_ref[(position(distance, serve, owners) * 2 + heads) * CAP + place])
        attended = jnp.concatenate(history, axis=0) + terms_ref[0].astype(jnp.float32)
        gates = terms_ref[1].astype(jnp.float32)
        mixed = []
        for low in range(0, width, HD):
            head = attended[:, low : low + HD]
            level = lax.rsqrt(jnp.mean(head * head, axis=-1, keepdims=True) + EPS)
            mixed.append((head * level * gates[:, low : low + HD]).astype(jnp.bfloat16))
        total = total + jnp.dot(jnp.concatenate(mixed, axis=1), w_ref[...], preferred_element_type=jnp.float32)
    out_ref[...] = total.reshape(out_ref.shape).astype(jnp.bfloat16)


def far_first(count):
    return list(reversed(range(count)))


def swap(rows):
    return lax.ppermute(rows, "serve", [(0, 1), (1, 0)])


def cross(owners, messages):
    came = []
    for at in far_first(len(messages)):
        steps = [2 * (at + 1) + side for side in range(2)]
        pairs = [(place * 2 + core_of(step), (place ^ step) * 2 + core_of(step)) for place in range(owners) for step in steps]
        came.append(lax.ppermute(messages[at], ("cache", "serve"), pairs))
    return came


def to_neighbour(owners, rows):
    return lax.ppermute(rows, "cache", [(place, place ^ 1) for place in range(owners)])


def body(candidates, input_gain, w_in, w_out, hist_keys, hist_values, request_session, hist_len, block_mask):
    owners = lax.axis_size("cache")
    req_count, half_cands, model_width = candidates.shape
    width = w_in.shape[2]
    rows = req_count * half_cands
    hist_rows = hist_keys.shape[1]
    bf16 = functools.partial(jax.ShapeDtypeStruct, dtype=jnp.bfloat16)
    sessions = request_session.reshape(-1)
    gain = input_gain.reshape(-1, HD)
    messages = owners // 2 - 1
    piece = 2 * CAP * half_cands

    session_row = request_session.reshape(1, -1)
    placed = kernel_call(
        functools.partial(front_kernel, owners),
        [bf16(((messages + 2) * piece, columns)) for columns in (model_width, rows)],
        [vmem] * 2,
    )(session_row, candidates)
    other, placed = lax.optimization_barrier((swap(candidates), placed))
    out = kernel_call(message_kernel, [bf16((piece, model_width))] * (messages + 2), [vmem] * 3)(*placed, other)
    (local, near, *out), w_in = lax.optimization_barrier((out, w_in))
    weights = jnp.transpose(w_in, (1, 0, 2))
    near = to_neighbour(owners, near)
    came = cross(owners, out)
    came, near, weights = lax.optimization_barrier((came, near, weights))
    stacked = kernel_call(stack_kernel, bf16((messages * piece, model_width)), [vmem] * messages)(*came)
    visible = kernel_call(
        visible_kernel,
        [bf16((owners * piece, HD)), bf16((hist_rows, HD))],
        [vmem] * 3,
        [pltpu.VMEM((HD, owners * req_count), jnp.bfloat16)],
        flops=2 * messages * piece * model_width * width,
    )(session_row, hist_len.reshape(1, -1), lax.optimization_barrier((block_mask.T, stacked))[0])
    swapped, (hide_rows, hide_cols), w_out = lax.optimization_barrier((swap(stacked), visible, w_out))
    w_other = swap(w_out)
    local, near, keep, give = kernel_call(
        functools.partial(history_kernel, owners),
        [bf16((rows_out, width)) for rows_out in (piece // 2, piece, messages * piece, messages * piece + piece // 2)],
        [vmem] * (6 + owners // 2 + 2),
        flops=8 * owners * piece * hist_rows * width,
        moved=4 * hist_rows * width,
    )(
        gain,
        weights,
        hide_rows,
        hide_cols,
        hist_keys.reshape(hist_rows, width),
        hist_values.reshape(hist_rows, width),
        local,
        near,
        *reversed(came),
        swapped,
    )
    near = to_neighbour(owners, near)
    keep, give, w_other = lax.optimization_barrier((keep, give, w_other))
    got = swap(give)
    terms = kernel_call(
        self_kernel,
        [bf16((2, rows, width))] * 2,
        [vmem] * 4,
        [pltpu.VMEM((2 * rows, model_width), jnp.bfloat16)],
        flops=16 * rows * model_width * width,
        moved=8 * model_width * width,
    )(candidates, lax.optimization_barrier((other, give))[0], gain, weights)
    got, (keep_terms, give_terms) = lax.optimization_barrier((got, terms))
    backs = cross(owners, kernel_call(pack_kernel, [bf16((2 * piece, width))] * messages, [vmem] * 2)(keep, got))
    their_near = swap(near[piece // 2 :])
    returned = [rows_of for back in backs for rows_of in (back, swap(back[piece:]))]
    return kernel_call(
        functools.partial(output_kernel, owners),
        bf16((req_count, half_cands, model_width)),
        [smem] + [vmem] * (9 + 2 * messages),
        [pltpu.VMEM((2 * owners * CAP, half_cands, width), jnp.float32)],
        flops=8 * rows * model_width * width,
        moved=4 * model_width * width,
    )(sessions, candidates, keep_terms, swap(give_terms), w_out, w_other, local, got, near, their_near, *returned)


def solution(mesh):
    placed = (
        P(("groups", "cache"), "serve", None),
        P(),
        P(None, None, "serve"),
        P("serve", None),
        P(("groups", "cache"), None, "serve"),
        P(("groups", "cache"), None, "serve"),
        P("groups", None),
        P("groups"),
        P("groups", None),
    )
    return jax.shard_map(
        body,
        mesh=mesh,
        in_specs=placed,
        out_specs=P(("groups", "cache"), "serve", None),
        check_vma=False,
    )
```

```python
import functools

import jax
import jax.numpy as jnp
from jax import lax
from jax.experimental import pallas as pl
from jax.experimental.pallas import tpu as pltpu
from jax.sharding import PartitionSpec as P

HD = 128
BLK = 64
CAP = 2
EPS = 1e-06
SCALE = HD ** (-0.5)
HIDE = -1e30
VMEM_LIMIT = 16 * 1024 * 1024

vmem = pl.BlockSpec(memory_space=pltpu.VMEM)
smem = pl.BlockSpec(memory_space=pltpu.SMEM)


def silu_of_half(half):
    return half + half * jnp.tanh(half)


def silu(x):
    return silu_of_half(x * 0.5)


def kernel_call(body, out_shape, in_specs, scratch_shapes=(), flops=0, moved=0):
    return pl.pallas_call(
        body,
        out_shape=out_shape,
        in_specs=in_specs,
        out_specs=jax.tree.map(lambda _: vmem, out_shape),
        scratch_shapes=scratch_shapes,
        cost_estimate=pl.CostEstimate(flops=flops, bytes_accessed=moved, transcendentals=0),
        compiler_params=pltpu.CompilerParams(vmem_limit_bytes=VMEM_LIMIT),
    )


def gain_row(gain_ref):
    gain = gain_ref[...].astype(jnp.float32)
    return jnp.concatenate([gain[at : at + 1] for at in range(gain.shape[0])], axis=1)


def normed_rows(rows_ref, start, count, gain):
    rows = rows_ref[start : start + count].astype(jnp.float32)
    rows = rows.reshape(-1, rows.shape[-1])
    mean_square = jnp.mean(rows * rows, axis=-1, keepdims=True)
    return (rows * lax.rsqrt(mean_square + EPS) * gain).astype(jnp.bfloat16)


def core_of(distance):
    parity = distance
    for shift in (16, 8, 4, 2, 1):
        parity = parity ^ (parity >> shift)
    return parity & 1


def position(distance, serve, owners):
    far = jnp.where(core_of(distance) == serve, 0, owners // 2 - 1) + distance // 2 + 1
    return jnp.where(distance < 2, distance, far)


def own_slots(sess_ref, req_count):
    me = lax.axis_index("cache")
    base = me * req_count
    sessions = [sess_ref[base + request] for request in range(req_count)]
    slots = []
    for request in range(req_count):
        place = 0
        for earlier in range(request):
            place = place + (sessions[earlier] == sessions[request]).astype(jnp.int32)
        slots.append((sessions[request] ^ me, place))
    return slots


def places(sessions, per_owner):
    lane = lax.broadcasted_iota(jnp.int32, sessions.shape, 1)
    place = jnp.zeros_like(sessions)
    for back in range(1, per_owner):
        same = (pltpu.roll(sessions, back, 1) == sessions) & (lane % per_owner >= back)
        place = place + same.astype(jnp.int32)
    return place


def front_kernel(owners, sess_ref, own_ref, moved_ref, chosen_ref):
    half_cands, model_width = own_ref.shape[1:]
    me, serve = lax.axis_index("cache"), lax.axis_index("serve")
    sessions = sess_ref[...]
    requests = sessions.shape[1]
    per_owner = requests // owners
    rows = per_owner * half_cands
    distance = sessions ^ me
    at = position(distance, serve, owners)
    sent = at <= owners // 2
    code = jnp.where(sent, at * (2 * CAP) + places(sessions, per_owner), owners * (2 * CAP))
    request = lax.broadcasted_iota(jnp.int32, (requests, rows), 0)
    column = lax.broadcasted_iota(jnp.int32, (requests, rows), 1)
    spread = (request == me * per_owner + column // half_cands).astype(jnp.float32).astype(jnp.bfloat16)
    codes = jnp.broadcast_to(code, (8, requests)).astype(jnp.float32).astype(jnp.bfloat16)
    target = jnp.dot(codes, spread, preferred_element_type=jnp.float32)[:1].astype(jnp.int32)
    at = lax.broadcasted_iota(jnp.int32, chosen_ref.shape, 0)
    column = lax.broadcasted_iota(jnp.int32, chosen_ref.shape, 1)
    same = at % half_cands == column % half_cands
    own = ((at // half_cands == target) & same).astype(jnp.float32).astype(jnp.bfloat16)
    chosen_ref[...] = ((at // half_cands == target + CAP) & same).astype(jnp.float32).astype(jnp.bfloat16)
    source = own_ref[...].astype(jnp.float32).reshape(-1, model_width).astype(jnp.bfloat16)
    moved_ref[...] = jnp.dot(own, source, preferred_element_type=jnp.float32).astype(jnp.bfloat16)


def visible_kernel(sess_ref, len_ref, mask_ref, hide_rows_ref, hide_cols_ref, marks_ref):
    me, serve = lax.axis_index("cache"), lax.axis_index("serve")
    blocks, requests = mask_ref.shape
    owners = len_ref.shape[1]
    per_owner = requests // owners
    sessions = sess_ref[...]
    lane = lax.broadcasted_iota(jnp.int32, (1, requests), 1)
    at = position((lane // per_owner) ^ me, serve, owners)
    slot_of = jnp.where(sessions == me, at * CAP + places(sessions, per_owner), -1)
    slots = owners * CAP
    at_slot = lax.broadcasted_iota(jnp.int32, (slots, requests), 0)
    taken = (at_slot == slot_of).astype(jnp.float32).astype(jnp.bfloat16)
    marks_ref[...] = jnp.zeros_like(marks_ref)
    marks_ref[:blocks, :] = mask_ref[...].astype(jnp.float32).astype(jnp.bfloat16)
    seen = lax.dot_general(taken, marks_ref[...], (((1,), (1,)), ((), ())), preferred_element_type=jnp.float32)
    slot_lane = lax.broadcasted_iota(jnp.int32, (slots, HD), 1)
    hidden = jnp.where(slot_lane < blocks, (1.0 - seen) * HIDE, jnp.where(slot_lane == blocks, HIDE, 0.0))
    half = hide_rows_ref.shape[0] // slots // 2
    wide = jnp.broadcast_to(hidden.reshape(owners, 1, CAP, 1, HD), (owners, 2, CAP, half, HD))
    hide_rows_ref[...] = wide.reshape(hide_rows_ref.shape).astype(jnp.bfloat16)
    hist_rows = hide_cols_ref.shape[0]
    owner_lane = lax.broadcasted_iota(jnp.int32, (1, owners), 1)
    length = jnp.sum(jnp.where(owner_lane == me, len_ref[...], 0), axis=1, keepdims=True)
    at_row = lax.broadcasted_iota(jnp.int32, (hist_rows, HD), 0)
    at_lane = lax.broadcasted_iota(jnp.int32, (hist_rows, HD), 1)
    hide_cols_ref[...] = jnp.where(
        (at_lane == at_row // BLK) | ((at_lane == blocks) & (at_row >= length)), 1.0, 0.0
    ).astype(jnp.bfloat16)


def message_kernel(moved_ref, chosen_ref, other_ref, *out_refs):
    model_width = other_ref.shape[2]
    source = other_ref[...].astype(jnp.float32).reshape(-1, model_width).astype(jnp.bfloat16)
    rows = moved_ref[...].astype(jnp.float32) + jnp.dot(chosen_ref[...], source, preferred_element_type=jnp.float32)
    piece = out_refs[0].shape[0]
    for at, out_ref in enumerate(out_refs):
        out_ref[...] = rows[at * piece : (at + 1) * piece].astype(jnp.bfloat16)


def self_kernel(own_ref, other_ref, gain_ref, w_ref, keep_ref, give_ref, normed_ref):
    rows, width = keep_ref.shape[1:]
    gain = gain_row(gain_ref)
    normed_ref[:rows, :] = normed_rows(own_ref, 0, own_ref.shape[0], gain)
    normed_ref[rows:, :] = normed_rows(other_ref, 0, other_ref.shape[0], gain)
    normed = normed_ref[...]

    def activated(part):
        return silu(jnp.dot(normed, w_ref[part], preferred_element_type=jnp.float32)).astype(jnp.bfloat16)

    products = activated(0).astype(jnp.float32) * activated(1).astype(jnp.float32)
    values, gates = activated(2), activated(3)
    for low in range(0, width, HD):
        score = jnp.sum(products[:, low : low + HD], axis=-1, keepdims=True) * SCALE
        term = (silu(score) * values[:, low : low + HD].astype(jnp.float32)).astype(jnp.bfloat16)
        keep_ref[0, :, low : low + HD] = term[:rows]
        give_ref[0, :, low : low + HD] = term[rows:]
    keep_ref[1] = gates[:rows]
    give_ref[1] = gates[rows:]


def pack_kernel(keep_ref, got_ref, *out_refs):
    part = out_refs[0].shape[0] // 4
    for at, out_ref in enumerate(out_refs):
        for side in range(2):
            low = (2 * at + side) * part
            out_ref[2 * side * part : (2 * side + 1) * part, :] = keep_ref[low : low + part, :]
            out_ref[(2 * side + 1) * part : (2 * side + 2) * part, :] = got_ref[low : low + part, :]


def stack_kernel(*refs):
    *in_refs, out_ref = refs
    rows = in_refs[0].shape[0]
    for at, in_ref in zip(far_first(len(in_refs)), in_refs):
        out_ref[at * rows : (at + 1) * rows, :] = in_ref[...]


def history_kernel(owners, gain_ref, w_ref, hide_rows_ref, hide_cols_ref, keys_ref, values_ref, *refs):
    *slot_refs, swapped_ref, local_ref, near_ref, keep_ref, give_ref = refs
    width = near_ref.shape[1]
    per_owner = near_ref.shape[0]
    half = per_owner // 2
    far = [(ref, at * per_owner, 0, per_owner) for ref in (keep_ref, give_ref) for at in range(owners // 2 - 1)]
    local = [(local_ref, 0, 0, half), (give_ref, (owners // 2 - 1) * per_owner, half, half)]
    sources = [(ref, 0) for ref in slot_refs] + [(swapped_ref, at * per_owner) for at in range(owners // 2 - 1)]
    targets = [local, [(near_ref, 0, 0, per_owner)]] + [[target] for target in far]
    hist_rows = keys_ref.shape[0]
    span = min(512, hist_rows)
    per_step = max(1, min(owners, 256 // per_owner))
    gain = gain_row(gain_ref)
    for first in range(0, owners, per_step):
        group = range(first, min(first + per_step, owners))
        normed = jnp.concatenate([normed_rows(*sources[at], per_owner, gain) for at in group], axis=0)
        queries = silu(jnp.dot(normed, w_ref[0], preferred_element_type=jnp.float32)).astype(jnp.bfloat16)
        hide_rows = hide_rows_ref[first * per_owner : first * per_owner + queries.shape[0], :]
        for low in range(0, width, HD):
            lhs = jnp.concatenate([queries[:, low : low + HD], hide_rows], axis=1)
            total = None
            for start in range(0, hist_rows, span):
                rhs = jnp.concatenate(
                    [keys_ref[start : start + span, low : low + HD], hide_cols_ref[start : start + span, :]], axis=1
                )
                scores = lax.dot_general(lhs, rhs, (((1,), (1,)), ((), ())), preferred_element_type=jnp.float32)
                weights = silu_of_half(scores * (0.5 * SCALE)).astype(jnp.bfloat16)
                term = jnp.dot(
                    weights, values_ref[start : start + span, low : low + HD], preferred_element_type=jnp.float32
                )
                total = term if total is None else total + term
            total = total.astype(jnp.bfloat16)
            for place, at in enumerate(group):
                for out_ref, row, start, count in targets[at]:
                    low_row = place * per_owner + start
                    out_ref[row : row + count, low : low + HD] = total[low_row : low_row + count]


def output_kernel(owners, sess_ref, own_ref, keep_ref, got_ref, w_own_ref, w_other_ref, *refs):
    local_ref, given_ref, near_ref, their_near_ref, *back_refs = refs[:-2]
    out_ref, table_ref = refs[-2:]
    req_count, half_cands, model_width = own_ref.shape
    rows = req_count * half_cands
    width = model_width // 2
    serve = lax.axis_index("serve")
    part = CAP * half_cands
    messages = owners // 2 - 1

    def store(at, heads, block):
        table_ref[(at * 2 + heads) * CAP : (at * 2 + heads + 1) * CAP] = block.reshape(CAP, half_cands, width)

    store(0, 0, local_ref[...].astype(jnp.float32))
    store(0, 1, given_ref[given_ref.shape[0] - part :, :].astype(jnp.float32))
    store(1, 0, near_ref[:part, :].astype(jnp.float32))
    store(1, 1, their_near_ref[...].astype(jnp.float32))
    for order, at in enumerate(far_first(messages)):
        for side in range(2):
            block = back_refs[2 * order + side][: 2 * part, :].astype(jnp.float32)
            for heads in range(2):
                source = heads if side == 0 else 1 - heads
                store(2 + side * messages + at, heads, block[source * part : (source + 1) * part])
    own = own_slots(sess_ref, req_count)
    total = own_ref[...].astype(jnp.float32).reshape(rows, model_width)
    for heads, (terms_ref, w_ref) in enumerate(((keep_ref, w_own_ref), (got_ref, w_other_ref))):
        history = []
        for distance, place in own:
            history.append(table_ref[(position(distance, serve, owners) * 2 + heads) * CAP + place])
        attended = jnp.concatenate(history, axis=0) + terms_ref[0].astype(jnp.float32)
        gates = terms_ref[1].astype(jnp.float32)
        mixed = []
        for low in range(0, width, HD):
            head = attended[:, low : low + HD]
            level = lax.rsqrt(jnp.mean(head * head, axis=-1, keepdims=True) + EPS)
            mixed.append((head * level * gates[:, low : low + HD]).astype(jnp.bfloat16))
        total = total + jnp.dot(jnp.concatenate(mixed, axis=1), w_ref[...], preferred_element_type=jnp.float32)
    out_ref[...] = total.reshape(out_ref.shape).astype(jnp.bfloat16)


def far_first(count):
    return list(reversed(range(count)))


def swap(rows):
    return lax.ppermute(rows, "serve", [(0, 1), (1, 0)])


def cross(owners, messages):
    came = []
    for at in far_first(len(messages)):
        steps = [2 * (at + 1) + side for side in range(2)]
        pairs = [(place * 2 + core_of(step), (place ^ step) * 2 + core_of(step)) for place in range(owners) for step in steps]
        came.append(lax.ppermute(messages[at], ("cache", "serve"), pairs))
    return came


def to_neighbour(owners, rows):
    return lax.ppermute(rows, "cache", [(place, place ^ 1) for place in range(owners)])


def body(candidates, input_gain, w_in, w_out, hist_keys, hist_values, request_session, hist_len, block_mask):
    owners = lax.axis_size("cache")
    req_count, half_cands, model_width = candidates.shape
    width = w_in.shape[2]
    rows = req_count * half_cands
    hist_rows = hist_keys.shape[1]
    bf16 = functools.partial(jax.ShapeDtypeStruct, dtype=jnp.bfloat16)
    sessions = request_session.reshape(-1)
    gain = input_gain.reshape(-1, HD)
    messages = owners // 2 - 1
    piece = 2 * CAP * half_cands

    session_row = request_session.reshape(1, -1)
    placed = kernel_call(
        functools.partial(front_kernel, owners),
        [bf16(((messages + 2) * piece, columns)) for columns in (model_width, rows)],
        [vmem] * 2,
    )(session_row, candidates)
    other, placed = lax.optimization_barrier((swap(candidates), placed))
    out = kernel_call(message_kernel, [bf16((piece, model_width))] * (messages + 2), [vmem] * 3)(*placed, other)
    (local, near, *out), w_in = lax.optimization_barrier((out, w_in))
    weights = jnp.transpose(w_in, (1, 0, 2))
    near = to_neighbour(owners, near)
    came = cross(owners, out)
    came, near, weights = lax.optimization_barrier((came, near, weights))
    stacked = kernel_call(stack_kernel, bf16((messages * piece, model_width)), [vmem] * messages)(*came)
    visible = kernel_call(
        visible_kernel,
        [bf16((owners * piece, HD)), bf16((hist_rows, HD))],
        [vmem] * 3,
        [pltpu.VMEM((HD, owners * req_count), jnp.bfloat16)],
        flops=2 * messages * piece * model_width * width,
    )(session_row, hist_len.reshape(1, -1), lax.optimization_barrier((block_mask.T, stacked))[0])
    swapped, (hide_rows, hide_cols), w_out = lax.optimization_barrier((swap(stacked), visible, w_out))
    w_other = swap(w_out)
    local, near, keep, give = kernel_call(
        functools.partial(history_kernel, owners),
        [bf16((rows_out, width)) for rows_out in (piece // 2, piece, messages * piece, messages * piece + piece // 2)],
        [vmem] * (6 + owners // 2 + 2),
        flops=8 * owners * piece * hist_rows * width,
        moved=4 * hist_rows * width,
    )(
        gain,
        weights,
        hide_rows,
        hide_cols,
        hist_keys.reshape(hist_rows, width),
        hist_values.reshape(hist_rows, width),
        local,
        near,
        *reversed(came),
        swapped,
    )
    near = to_neighbour(owners, near)
    keep, give, w_other = lax.optimization_barrier((keep, give, w_other))
    got = swap(give)
    terms = kernel_call(
        self_kernel,
        [bf16((2, rows, width))] * 2,
        [vmem] * 4,
        [pltpu.VMEM((2 * rows, model_width), jnp.bfloat16)],
        flops=16 * rows * model_width * width,
        moved=8 * model_width * width,
    )(candidates, lax.optimization_barrier((other, give))[0], gain, weights)
    got, (keep_terms, give_terms) = lax.optimization_barrier((got, terms))
    backs = cross(owners, kernel_call(pack_kernel, [bf16((2 * piece, width))] * messages, [vmem] * 2)(keep, got))
    their_near = swap(near[piece // 2 :])
    returned = [rows_of for back in backs for rows_of in (back, swap(back[piece:]))]
    return kernel_call(
        functools.partial(output_kernel, owners),
        bf16((req_count, half_cands, model_width)),
        [smem] + [vmem] * (9 + 2 * messages),
        [pltpu.VMEM((2 * owners * CAP, half_cands, width), jnp.float32)],
        flops=8 * rows * model_width * width,
        moved=4 * model_width * width,
    )(sessions, candidates, keep_terms, swap(give_terms), w_out, w_other, local, got, near, their_near, *returned)


def solution(mesh):
    placed = (
        P(("groups", "cache"), "serve", None),
        P(),
        P(None, None, "serve"),
        P("serve", None),
        P(("groups", "cache"), None, "serve"),
        P(("groups", "cache"), None, "serve"),
        P("groups", None),
        P("groups"),
        P("groups", None),
    )
    return jax.shard_map(
        body,
        mesh=mesh,
        in_specs=placed,
        out_specs=P(("groups", "cache"), "serve", None),
        check_vma=False,
    )
```

```python
import functools

import jax
import jax.numpy as jnp
from jax import lax
from jax.experimental import pallas as pl
from jax.experimental.pallas import tpu as pltpu
from jax.sharding import PartitionSpec as P

HD = 128
BLK = 64
CAP = 2
EPS = 1e-06
SCALE = HD ** (-0.5)
HIDE = -1e30
VMEM_LIMIT = 16 * 1024 * 1024

vmem = pl.BlockSpec(memory_space=pltpu.VMEM)
smem = pl.BlockSpec(memory_space=pltpu.SMEM)


def silu_of_half(half):
    return half + half * jnp.tanh(half)


def silu(x):
    return silu_of_half(x * 0.5)


def kernel_call(body, out_shape, in_specs, scratch_shapes=(), flops=0, moved=0):
    return pl.pallas_call(
        body,
        out_shape=out_shape,
        in_specs=in_specs,
        out_specs=jax.tree.map(lambda _: vmem, out_shape),
        scratch_shapes=scratch_shapes,
        cost_estimate=pl.CostEstimate(flops=flops, bytes_accessed=moved, transcendentals=0),
        compiler_params=pltpu.CompilerParams(vmem_limit_bytes=VMEM_LIMIT),
    )


def gain_row(gain_ref):
    gain = gain_ref[...].astype(jnp.float32)
    return jnp.concatenate([gain[at : at + 1] for at in range(gain.shape[0])], axis=1)


def normed_rows(rows_ref, start, count, gain):
    rows = rows_ref[start : start + count].astype(jnp.float32)
    rows = rows.reshape(-1, rows.shape[-1])
    mean_square = jnp.mean(rows * rows, axis=-1, keepdims=True)
    return (rows * lax.rsqrt(mean_square + EPS) * gain).astype(jnp.bfloat16)


def core_of(distance):
    parity = distance
    for shift in (16, 8, 4, 2, 1):
        parity = parity ^ (parity >> shift)
    return parity & 1


def position(distance, serve, owners):
    far = jnp.where(core_of(distance) == serve, 0, owners // 2 - 1) + distance // 2 + 1
    return jnp.where(distance < 2, distance, far)


def own_slots(sess_ref, req_count):
    me = lax.axis_index("cache")
    base = me * req_count
    sessions = [sess_ref[base + request] for request in range(req_count)]
    slots = []
    for request in range(req_count):
        place = 0
        for earlier in range(request):
            place = place + (sessions[earlier] == sessions[request]).astype(jnp.int32)
        slots.append((sessions[request] ^ me, place))
    return slots


def places(sessions, per_owner):
    lane = lax.broadcasted_iota(jnp.int32, sessions.shape, 1)
    place = jnp.zeros_like(sessions)
    for back in range(1, per_owner):
        same = (pltpu.roll(sessions, back, 1) == sessions) & (lane % per_owner >= back)
        place = place + same.astype(jnp.int32)
    return place


def front_kernel(owners, sess_ref, own_ref, moved_ref, chosen_ref):
    half_cands, model_width = own_ref.shape[1:]
    me, serve = lax.axis_index("cache"), lax.axis_index("serve")
    sessions = sess_ref[...]
    requests = sessions.shape[1]
    per_owner = requests // owners
    rows = per_owner * half_cands
    distance = sessions ^ me
    at = position(distance, serve, owners)
    sent = at <= owners // 2
    code = jnp.where(sent, at * (2 * CAP) + places(sessions, per_owner), owners * (2 * CAP))
    request = lax.broadcasted_iota(jnp.int32, (requests, rows), 0)
    column = lax.broadcasted_iota(jnp.int32, (requests, rows), 1)
    spread = (request == me * per_owner + column // half_cands).astype(jnp.float32).astype(jnp.bfloat16)
    codes = jnp.broadcast_to(code, (8, requests)).astype(jnp.float32).astype(jnp.bfloat16)
    target = jnp.dot(codes, spread, preferred_element_type=jnp.float32)[:1].astype(jnp.int32)
    at = lax.broadcasted_iota(jnp.int32, chosen_ref.shape, 0)
    column = lax.broadcasted_iota(jnp.int32, chosen_ref.shape, 1)
    same = at % half_cands == column % half_cands
    own = ((at // half_cands == target) & same).astype(jnp.float32).astype(jnp.bfloat16)
    chosen_ref[...] = ((at // half_cands == target + CAP) & same).astype(jnp.float32).astype(jnp.bfloat16)
    source = own_ref[...].astype(jnp.float32).reshape(-1, model_width).astype(jnp.bfloat16)
    moved_ref[...] = jnp.dot(own, source, preferred_element_type=jnp.float32).astype(jnp.bfloat16)


def visible_kernel(sess_ref, len_ref, mask_ref, hide_rows_ref, hide_cols_ref, marks_ref):
    me, serve = lax.axis_index("cache"), lax.axis_index("serve")
    blocks, requests = mask_ref.shape
    owners = len_ref.shape[1]
    per_owner = requests // owners
    sessions = sess_ref[...]
    lane = lax.broadcasted_iota(jnp.int32, (1, requests), 1)
    at = position((lane // per_owner) ^ me, serve, owners)
    slot_of = jnp.where(sessions == me, at * CAP + places(sessions, per_owner), -1)
    slots = owners * CAP
    at_slot = lax.broadcasted_iota(jnp.int32, (slots, requests), 0)
    taken = (at_slot == slot_of).astype(jnp.float32).astype(jnp.bfloat16)
    marks_ref[...] = jnp.zeros_like(marks_ref)
    marks_ref[:blocks, :] = mask_ref[...].astype(jnp.float32).astype(jnp.bfloat16)
    seen = lax.dot_general(taken, marks_ref[...], (((1,), (1,)), ((), ())), preferred_element_type=jnp.float32)
    slot_lane = lax.broadcasted_iota(jnp.int32, (slots, HD), 1)
    hidden = jnp.where(slot_lane < blocks, (1.0 - seen) * HIDE, jnp.where(slot_lane == blocks, HIDE, 0.0))
    half = hide_rows_ref.shape[0] // slots // 2
    wide = jnp.broadcast_to(hidden.reshape(owners, 1, CAP, 1, HD), (owners, 2, CAP, half, HD))
    hide_rows_ref[...] = wide.reshape(hide_rows_ref.shape).astype(jnp.bfloat16)
    hist_rows = hide_cols_ref.shape[0]
    owner_lane = lax.broadcasted_iota(jnp.int32, (1, owners), 1)
    length = jnp.sum(jnp.where(owner_lane == me, len_ref[...], 0), axis=1, keepdims=True)
    at_row = lax.broadcasted_iota(jnp.int32, (hist_rows, HD), 0)
    at_lane = lax.broadcasted_iota(jnp.int32, (hist_rows, HD), 1)
    hide_cols_ref[...] = jnp.where(
        (at_lane == at_row // BLK) | ((at_lane == blocks) & (at_row >= length)), 1.0, 0.0
    ).astype(jnp.bfloat16)


def message_kernel(moved_ref, chosen_ref, other_ref, *out_refs):
    model_width = other_ref.shape[2]
    source = other_ref[...].astype(jnp.float32).reshape(-1, model_width).astype(jnp.bfloat16)
    rows = moved_ref[...].astype(jnp.float32) + jnp.dot(chosen_ref[...], source, preferred_element_type=jnp.float32)
    piece = out_refs[0].shape[0]
    for at, out_ref in enumerate(out_refs):
        out_ref[...] = rows[at * piece : (at + 1) * piece].astype(jnp.bfloat16)


def self_kernel(own_ref, other_ref, gain_ref, w_ref, keep_ref, give_ref, normed_ref):
    rows, width = keep_ref.shape[1:]
    gain = gain_row(gain_ref)
    normed_ref[:rows, :] = normed_rows(own_ref, 0, own_ref.shape[0], gain)
    normed_ref[rows:, :] = normed_rows(other_ref, 0, other_ref.shape[0], gain)
    normed = normed_ref[...]

    def activated(part):
        return silu(jnp.dot(normed, w_ref[part], preferred_element_type=jnp.float32)).astype(jnp.bfloat16)

    products = activated(0).astype(jnp.float32) * activated(1).astype(jnp.float32)
    values, gates = activated(2), activated(3)
    for low in range(0, width, HD):
        score = jnp.sum(products[:, low : low + HD], axis=-1, keepdims=True) * SCALE
        term = (silu(score) * values[:, low : low + HD].astype(jnp.float32)).astype(jnp.bfloat16)
        keep_ref[0, :, low : low + HD] = term[:rows]
        give_ref[0, :, low : low + HD] = term[rows:]
    keep_ref[1] = gates[:rows]
    give_ref[1] = gates[rows:]


def pack_kernel(keep_ref, got_ref, *out_refs):
    part = out_refs[0].shape[0] // 4
    for at, out_ref in enumerate(out_refs):
        for side in range(2):
            low = (2 * at + side) * part
            out_ref[2 * side * part : (2 * side + 1) * part, :] = keep_ref[low : low + part, :]
            out_ref[(2 * side + 1) * part : (2 * side + 2) * part, :] = got_ref[low : low + part, :]


def stack_kernel(*refs):
    *in_refs, out_ref = refs
    rows = in_refs[0].shape[0]
    for at, in_ref in zip(far_first(len(in_refs)), in_refs):
        out_ref[at * rows : (at + 1) * rows, :] = in_ref[...]


def history_kernel(owners, gain_ref, w_ref, hide_rows_ref, hide_cols_ref, keys_ref, values_ref, *refs):
    *slot_refs, swapped_ref, local_ref, near_ref, keep_ref, give_ref, hidden_ref = refs
    width = near_ref.shape[1]
    per_owner = near_ref.shape[0]
    half_rows = per_owner // 2
    far = [(ref, at * per_owner, 0, per_owner) for ref in (keep_ref, give_ref) for at in range(owners // 2 - 1)]
    local = [(local_ref, 0, 0, half_rows), (give_ref, (owners // 2 - 1) * per_owner, half_rows, half_rows)]
    sources = [(ref, 0) for ref in slot_refs] + [(swapped_ref, at * per_owner) for at in range(owners // 2 - 1)]
    targets = [local, [(near_ref, 0, 0, per_owner)]] + [[target] for target in far]
    hist_rows = keys_ref.shape[0]
    span = min(256, hist_rows)
    per_step = max(1, min(owners, 256 // per_owner))
    gain = gain_row(gain_ref)
    for first in range(0, owners, per_step):
        group = range(first, min(first + per_step, owners))
        normed = jnp.concatenate([normed_rows(*sources[at], per_owner, gain) for at in group], axis=0)
        queries = silu(jnp.dot(normed, w_ref[0], preferred_element_type=jnp.float32)).astype(jnp.bfloat16)
        hide_rows = hide_rows_ref[first * per_owner : first * per_owner + queries.shape[0], :]
        for start in range(0, hist_rows, span):
            hidden_ref[:, start : start + span] = lax.dot_general(
                hide_rows, hide_cols_ref[start : start + span, :], (((1,), (1,)), ((), ())), preferred_element_type=jnp.float32
            )
        for low in range(0, width, HD):
            total = None
            for start in range(0, hist_rows, span):
                scores = lax.dot_general(
                    queries[:, low : low + HD],
                    keys_ref[start : start + span, low : low + HD],
                    (((1,), (1,)), ((), ())),
                    preferred_element_type=jnp.float32,
                )
                half = scores * (0.5 * SCALE) + hidden_ref[:, start : start + span]
                weights = silu_of_half(half).astype(jnp.bfloat16)
                term = jnp.dot(
                    weights, values_ref[start : start + span, low : low + HD], preferred_element_type=jnp.float32
                )
                total = term if total is None else total + term
            total = total.astype(jnp.bfloat16)
            for place, at in enumerate(group):
                for out_ref, row, start, count in targets[at]:
                    low_row = place * per_owner + start
                    out_ref[row : row + count, low : low + HD] = total[low_row : low_row + count]


def output_kernel(owners, sess_ref, own_ref, keep_ref, got_ref, w_own_ref, w_other_ref, *refs):
    local_ref, given_ref, near_ref, their_near_ref, *back_refs = refs[:-2]
    out_ref, table_ref = refs[-2:]
    req_count, half_cands, model_width = own_ref.shape
    rows = req_count * half_cands
    width = model_width // 2
    serve = lax.axis_index("serve")
    part = CAP * half_cands
    messages = owners // 2 - 1

    def store(at, heads, block):
        table_ref[(at * 2 + heads) * CAP : (at * 2 + heads + 1) * CAP] = block.reshape(CAP, half_cands, width)

    store(0, 0, local_ref[...].astype(jnp.float32))
    store(0, 1, given_ref[given_ref.shape[0] - part :, :].astype(jnp.float32))
    store(1, 0, near_ref[:part, :].astype(jnp.float32))
    store(1, 1, their_near_ref[...].astype(jnp.float32))
    for order, at in enumerate(far_first(messages)):
        for side in range(2):
            block = back_refs[2 * order + side][: 2 * part, :].astype(jnp.float32)
            for heads in range(2):
                source = heads if side == 0 else 1 - heads
                store(2 + side * messages + at, heads, block[source * part : (source + 1) * part])
    own = own_slots(sess_ref, req_count)
    total = own_ref[...].astype(jnp.float32).reshape(rows, model_width)
    for heads, (terms_ref, w_ref) in enumerate(((keep_ref, w_own_ref), (got_ref, w_other_ref))):
        history = []
        for distance, place in own:
            history.append(table_ref[(position(distance, serve, owners) * 2 + heads) * CAP + place])
        attended = jnp.concatenate(history, axis=0) + terms_ref[0].astype(jnp.float32)
        gates = terms_ref[1].astype(jnp.float32)
        mixed = []
        for low in range(0, width, HD):
            head = attended[:, low : low + HD]
            level = lax.rsqrt(jnp.mean(head * head, axis=-1, keepdims=True) + EPS)
            mixed.append((head * level * gates[:, low : low + HD]).astype(jnp.bfloat16))
        total = total + jnp.dot(jnp.concatenate(mixed, axis=1), w_ref[...], preferred_element_type=jnp.float32)
    out_ref[...] = total.reshape(out_ref.shape).astype(jnp.bfloat16)


def far_first(count):
    return list(reversed(range(count)))


def swap(rows):
    return lax.ppermute(rows, "serve", [(0, 1), (1, 0)])


def cross(owners, messages):
    came = []
    for at in far_first(len(messages)):
        steps = [2 * (at + 1) + side for side in range(2)]
        pairs = [(place * 2 + core_of(step), (place ^ step) * 2 + core_of(step)) for place in range(owners) for step in steps]
        came.append(lax.ppermute(messages[at], ("cache", "serve"), pairs))
    return came


def to_neighbour(owners, rows):
    return lax.ppermute(rows, "cache", [(place, place ^ 1) for place in range(owners)])


def body(candidates, input_gain, w_in, w_out, hist_keys, hist_values, request_session, hist_len, block_mask):
    owners = lax.axis_size("cache")
    req_count, half_cands, model_width = candidates.shape
    width = w_in.shape[2]
    rows = req_count * half_cands
    hist_rows = hist_keys.shape[1]
    bf16 = functools.partial(jax.ShapeDtypeStruct, dtype=jnp.bfloat16)
    sessions = request_session.reshape(-1)
    gain = input_gain.reshape(-1, HD)
    messages = owners // 2 - 1
    piece = 2 * CAP * half_cands

    session_row = request_session.reshape(1, -1)
    placed = kernel_call(
        functools.partial(front_kernel, owners),
        [bf16(((messages + 2) * piece, columns)) for columns in (model_width, rows)],
        [vmem] * 2,
    )(session_row, candidates)
    other, placed = lax.optimization_barrier((swap(candidates), placed))
    out = kernel_call(message_kernel, [bf16((piece, model_width))] * (messages + 2), [vmem] * 3)(*placed, other)
    (local, near, *out), w_in = lax.optimization_barrier((out, w_in))
    weights = jnp.transpose(w_in, (1, 0, 2))
    near = to_neighbour(owners, near)
    came = cross(owners, out)
    came, near, weights = lax.optimization_barrier((came, near, weights))
    stacked = kernel_call(stack_kernel, bf16((messages * piece, model_width)), [vmem] * messages)(*came)
    visible = kernel_call(
        visible_kernel,
        [bf16((owners * piece, HD)), bf16((hist_rows, HD))],
        [vmem] * 3,
        [pltpu.VMEM((HD, owners * req_count), jnp.bfloat16)],
        flops=2 * messages * piece * model_width * width,
    )(session_row, hist_len.reshape(1, -1), lax.optimization_barrier((block_mask.T, stacked))[0])
    swapped, (hide_rows, hide_cols), w_out = lax.optimization_barrier((swap(stacked), visible, w_out))
    w_other = swap(w_out)
    local, near, keep, give = kernel_call(
        functools.partial(history_kernel, owners),
        [bf16((rows_out, width)) for rows_out in (piece // 2, piece, messages * piece, messages * piece + piece // 2)],
        [vmem] * (6 + owners // 2 + 2),
        [pltpu.VMEM((min(owners * piece, 256), hist_rows), jnp.float32)],
        flops=8 * owners * piece * hist_rows * width,
        moved=4 * hist_rows * width,
    )(
        gain,
        weights,
        hide_rows,
        hide_cols,
        hist_keys.reshape(hist_rows, width),
        hist_values.reshape(hist_rows, width),
        local,
        near,
        *reversed(came),
        swapped,
    )
    near = to_neighbour(owners, near)
    keep, give, w_other = lax.optimization_barrier((keep, give, w_other))
    got = swap(give)
    terms = kernel_call(
        self_kernel,
        [bf16((2, rows, width))] * 2,
        [vmem] * 4,
        [pltpu.VMEM((2 * rows, model_width), jnp.bfloat16)],
        flops=16 * rows * model_width * width,
        moved=8 * model_width * width,
    )(candidates, lax.optimization_barrier((other, give))[0], gain, weights)
    got, (keep_terms, give_terms) = lax.optimization_barrier((got, terms))
    backs = cross(owners, kernel_call(pack_kernel, [bf16((2 * piece, width))] * messages, [vmem] * 2)(keep, got))
    their_near = swap(near[piece // 2 :])
    returned = [rows_of for back in backs for rows_of in (back, swap(back[piece:]))]
    return kernel_call(
        functools.partial(output_kernel, owners),
        bf16((req_count, half_cands, model_width)),
        [smem] + [vmem] * (9 + 2 * messages),
        [pltpu.VMEM((2 * owners * CAP, half_cands, width), jnp.float32)],
        flops=8 * rows * model_width * width,
        moved=4 * model_width * width,
    )(sessions, candidates, keep_terms, swap(give_terms), w_out, w_other, local, got, near, their_near, *returned)


def solution(mesh):
    placed = (
        P(("groups", "cache"), "serve", None),
        P(),
        P(None, None, "serve"),
        P("serve", None),
        P(("groups", "cache"), None, "serve"),
        P(("groups", "cache"), None, "serve"),
        P("groups", None),
        P("groups"),
        P("groups", None),
    )
    return jax.shard_map(
        body,
        mesh=mesh,
        in_specs=placed,
        out_specs=P(("groups", "cache"), "serve", None),
        check_vma=False,
    )
```

```python
import functools

import jax
import jax.numpy as jnp
from jax import lax
from jax.experimental import pallas as pl
from jax.experimental.pallas import tpu as pltpu
from jax.sharding import PartitionSpec as P

HD = 128
BLK = 64
CAP = 2
EPS = 1e-06
SCALE = HD ** (-0.5)
HIDE = -1e30
VMEM_LIMIT = 16 * 1024 * 1024

vmem = pl.BlockSpec(memory_space=pltpu.VMEM)
smem = pl.BlockSpec(memory_space=pltpu.SMEM)


def silu_of_half(half):
    return half + half * jnp.tanh(half)


def silu(x):
    return silu_of_half(x * 0.5)


def kernel_call(body, out_shape, in_specs, scratch_shapes=(), flops=0, moved=0):
    return pl.pallas_call(
        body,
        out_shape=out_shape,
        in_specs=in_specs,
        out_specs=jax.tree.map(lambda _: vmem, out_shape),
        scratch_shapes=scratch_shapes,
        cost_estimate=pl.CostEstimate(flops=flops, bytes_accessed=moved, transcendentals=0),
        compiler_params=pltpu.CompilerParams(vmem_limit_bytes=VMEM_LIMIT),
    )


def gain_row(gain_ref):
    gain = gain_ref[...].astype(jnp.float32)
    return jnp.concatenate([gain[at : at + 1] for at in range(gain.shape[0])], axis=1)


def normed_rows(rows_ref, start, count, gain):
    rows = rows_ref[start : start + count].astype(jnp.float32)
    rows = rows.reshape(-1, rows.shape[-1])
    mean_square = jnp.mean(rows * rows, axis=-1, keepdims=True)
    return (rows * lax.rsqrt(mean_square + EPS) * gain).astype(jnp.bfloat16)


def core_of(distance):
    parity = distance
    for shift in (16, 8, 4, 2, 1):
        parity = parity ^ (parity >> shift)
    return parity & 1


def position(distance, serve, owners):
    far = jnp.where(core_of(distance) == serve, 0, owners // 2 - 1) + distance // 2 + 1
    return jnp.where(distance < 2, distance, far)


def own_slots(sess_ref, req_count):
    me = lax.axis_index("cache")
    base = me * req_count
    sessions = [sess_ref[base + request] for request in range(req_count)]
    slots = []
    for request in range(req_count):
        place = 0
        for earlier in range(request):
            place = place + (sessions[earlier] == sessions[request]).astype(jnp.int32)
        slots.append((sessions[request] ^ me, place))
    return slots


def places(sessions, per_owner):
    lane = lax.broadcasted_iota(jnp.int32, sessions.shape, 1)
    place = jnp.zeros_like(sessions)
    for back in range(1, per_owner):
        same = (pltpu.roll(sessions, back, 1) == sessions) & (lane % per_owner >= back)
        place = place + same.astype(jnp.int32)
    return place


def front_kernel(owners, sess_ref, own_ref, moved_ref, chosen_ref):
    half_cands, model_width = own_ref.shape[1:]
    me, serve = lax.axis_index("cache"), lax.axis_index("serve")
    sessions = sess_ref[...]
    requests = sessions.shape[1]
    per_owner = requests // owners
    rows = per_owner * half_cands
    distance = sessions ^ me
    at = position(distance, serve, owners)
    sent = at <= owners // 2
    code = jnp.where(sent, at * (2 * CAP) + places(sessions, per_owner), owners * (2 * CAP))
    request = lax.broadcasted_iota(jnp.int32, (requests, rows), 0)
    column = lax.broadcasted_iota(jnp.int32, (requests, rows), 1)
    spread = (request == me * per_owner + column // half_cands).astype(jnp.float32).astype(jnp.bfloat16)
    codes = jnp.broadcast_to(code, (8, requests)).astype(jnp.float32).astype(jnp.bfloat16)
    target = jnp.dot(codes, spread, preferred_element_type=jnp.float32)[:1].astype(jnp.int32)
    at = lax.broadcasted_iota(jnp.int32, chosen_ref.shape, 0)
    column = lax.broadcasted_iota(jnp.int32, chosen_ref.shape, 1)
    same = at % half_cands == column % half_cands
    own = ((at // half_cands == target) & same).astype(jnp.float32).astype(jnp.bfloat16)
    chosen_ref[...] = ((at // half_cands == target + CAP) & same).astype(jnp.float32).astype(jnp.bfloat16)
    source = own_ref[...].astype(jnp.float32).reshape(-1, model_width).astype(jnp.bfloat16)
    moved_ref[...] = jnp.dot(own, source, preferred_element_type=jnp.float32).astype(jnp.bfloat16)


def visible_kernel(sess_ref, len_ref, mask_ref, hide_rows_ref, hide_cols_ref, marks_ref):
    me, serve = lax.axis_index("cache"), lax.axis_index("serve")
    blocks, requests = mask_ref.shape
    owners = len_ref.shape[1]
    per_owner = requests // owners
    sessions = sess_ref[...]
    lane = lax.broadcasted_iota(jnp.int32, (1, requests), 1)
    at = position((lane // per_owner) ^ me, serve, owners)
    slot_of = jnp.where(sessions == me, at * CAP + places(sessions, per_owner), -1)
    slots = owners * CAP
    at_slot = lax.broadcasted_iota(jnp.int32, (slots, requests), 0)
    taken = (at_slot == slot_of).astype(jnp.float32).astype(jnp.bfloat16)
    marks_ref[...] = jnp.zeros_like(marks_ref)
    marks_ref[:blocks, :] = mask_ref[...].astype(jnp.float32).astype(jnp.bfloat16)
    seen = lax.dot_general(taken, marks_ref[...], (((1,), (1,)), ((), ())), preferred_element_type=jnp.float32)
    slot_lane = lax.broadcasted_iota(jnp.int32, (slots, HD), 1)
    hidden = jnp.where(slot_lane < blocks, (1.0 - seen) * HIDE, jnp.where(slot_lane == blocks, HIDE, 0.0))
    half = hide_rows_ref.shape[0] // slots // 2
    wide = jnp.broadcast_to(hidden.reshape(owners, 1, CAP, 1, HD), (owners, 2, CAP, half, HD))
    hide_rows_ref[...] = wide.reshape(hide_rows_ref.shape).astype(jnp.bfloat16)
    hist_rows = hide_cols_ref.shape[0]
    owner_lane = lax.broadcasted_iota(jnp.int32, (1, owners), 1)
    length = jnp.sum(jnp.where(owner_lane == me, len_ref[...], 0), axis=1, keepdims=True)
    at_row = lax.broadcasted_iota(jnp.int32, (hist_rows, HD), 0)
    at_lane = lax.broadcasted_iota(jnp.int32, (hist_rows, HD), 1)
    hide_cols_ref[...] = jnp.where(
        (at_lane == at_row // BLK) | ((at_lane == blocks) & (at_row >= length)), 1.0, 0.0
    ).astype(jnp.bfloat16)


def message_kernel(moved_ref, chosen_ref, other_ref, *out_refs):
    model_width = other_ref.shape[2]
    source = other_ref[...].astype(jnp.float32).reshape(-1, model_width).astype(jnp.bfloat16)
    rows = moved_ref[...].astype(jnp.float32) + jnp.dot(chosen_ref[...], source, preferred_element_type=jnp.float32)
    piece = out_refs[0].shape[0]
    for at, out_ref in enumerate(out_refs):
        out_ref[...] = rows[at * piece : (at + 1) * piece].astype(jnp.bfloat16)


def self_kernel(own_ref, other_ref, gain_ref, w_ref, keep_ref, give_ref, normed_ref):
    rows, width = keep_ref.shape[1:]
    gain = gain_row(gain_ref)
    normed_ref[:rows, :] = normed_rows(own_ref, 0, own_ref.shape[0], gain)
    normed_ref[rows:, :] = normed_rows(other_ref, 0, other_ref.shape[0], gain)
    normed = normed_ref[...]

    def activated(part):
        return silu(jnp.dot(normed, w_ref[part], preferred_element_type=jnp.float32)).astype(jnp.bfloat16)

    products = activated(0).astype(jnp.float32) * activated(1).astype(jnp.float32)
    values, gates = activated(2), activated(3)
    for low in range(0, width, HD):
        score = jnp.sum(products[:, low : low + HD], axis=-1, keepdims=True) * SCALE
        term = (silu(score) * values[:, low : low + HD].astype(jnp.float32)).astype(jnp.bfloat16)
        keep_ref[0, :, low : low + HD] = term[:rows]
        give_ref[0, :, low : low + HD] = term[rows:]
    keep_ref[1] = gates[:rows]
    give_ref[1] = gates[rows:]


def pack_kernel(keep_ref, got_ref, *out_refs):
    part = out_refs[0].shape[0] // 4
    for at, out_ref in enumerate(out_refs):
        for side in range(2):
            low = (2 * at + side) * part
            out_ref[2 * side * part : (2 * side + 1) * part, :] = keep_ref[low : low + part, :]
            out_ref[(2 * side + 1) * part : (2 * side + 2) * part, :] = got_ref[low : low + part, :]


def stack_kernel(*refs):
    *in_refs, out_ref = refs
    rows = in_refs[0].shape[0]
    for at, in_ref in zip(far_first(len(in_refs)), in_refs):
        out_ref[at * rows : (at + 1) * rows, :] = in_ref[...]


def history_kernel(owners, gain_ref, w_ref, hide_rows_ref, hide_cols_ref, keys_ref, values_ref, *refs):
    *slot_refs, swapped_ref, local_ref, near_ref, keep_ref, give_ref = refs
    width = near_ref.shape[1]
    per_owner = near_ref.shape[0]
    half = per_owner // 2
    far = [(ref, at * per_owner, 0, per_owner) for ref in (keep_ref, give_ref) for at in range(owners // 2 - 1)]
    local = [(local_ref, 0, 0, half), (give_ref, (owners // 2 - 1) * per_owner, half, half)]
    sources = [(ref, 0) for ref in slot_refs] + [(swapped_ref, at * per_owner) for at in range(owners // 2 - 1)]
    targets = [local, [(near_ref, 0, 0, per_owner)]] + [[target] for target in far]
    hist_rows = keys_ref.shape[0]
    span = min(128, hist_rows)
    per_step = max(1, min(owners, 256 // per_owner))
    gain = gain_row(gain_ref)
    for first in range(0, owners, per_step):
        group = range(first, min(first + per_step, owners))
        normed = jnp.concatenate([normed_rows(*sources[at], per_owner, gain) for at in group], axis=0)
        queries = silu(jnp.dot(normed, w_ref[0], preferred_element_type=jnp.float32)).astype(jnp.bfloat16)
        hide_rows = hide_rows_ref[first * per_owner : first * per_owner + queries.shape[0], :]
        for low in range(0, width, HD):
            lhs = jnp.concatenate([queries[:, low : low + HD], hide_rows], axis=1)
            total = None
            for start in range(0, hist_rows, span):
                rhs = jnp.concatenate(
                    [keys_ref[start : start + span, low : low + HD], hide_cols_ref[start : start + span, :]], axis=1
                )
                scores = lax.dot_general(lhs, rhs, (((1,), (1,)), ((), ())), preferred_element_type=jnp.float32)
                weights = silu_of_half(scores * (0.5 * SCALE)).astype(jnp.bfloat16)
                term = jnp.dot(
                    weights, values_ref[start : start + span, low : low + HD], preferred_element_type=jnp.float32
                )
                total = term if total is None else total + term
            total = total.astype(jnp.bfloat16)
            for place, at in enumerate(group):
                for out_ref, row, start, count in targets[at]:
                    low_row = place * per_owner + start
                    out_ref[row : row + count, low : low + HD] = total[low_row : low_row + count]


def output_kernel(owners, sess_ref, own_ref, keep_ref, got_ref, w_own_ref, w_other_ref, *refs):
    local_ref, given_ref, near_ref, their_near_ref, *back_refs = refs[:-2]
    out_ref, table_ref = refs[-2:]
    req_count, half_cands, model_width = own_ref.shape
    rows = req_count * half_cands
    width = model_width // 2
    serve = lax.axis_index("serve")
    part = CAP * half_cands
    messages = owners // 2 - 1

    def store(at, heads, block):
        table_ref[(at * 2 + heads) * CAP : (at * 2 + heads + 1) * CAP] = block.reshape(CAP, half_cands, width)

    store(0, 0, local_ref[...].astype(jnp.float32))
    store(0, 1, given_ref[given_ref.shape[0] - part :, :].astype(jnp.float32))
    store(1, 0, near_ref[:part, :].astype(jnp.float32))
    store(1, 1, their_near_ref[...].astype(jnp.float32))
    for order, at in enumerate(far_first(messages)):
        for side in range(2):
            block = back_refs[2 * order + side][: 2 * part, :].astype(jnp.float32)
            for heads in range(2):
                source = heads if side == 0 else 1 - heads
                store(2 + side * messages + at, heads, block[source * part : (source + 1) * part])
    own = own_slots(sess_ref, req_count)
    total = own_ref[...].astype(jnp.float32).reshape(rows, model_width)
    for heads, (terms_ref, w_ref) in enumerate(((keep_ref, w_own_ref), (got_ref, w_other_ref))):
        history = []
        for distance, place in own:
            history.append(table_ref[(position(distance, serve, owners) * 2 + heads) * CAP + place])
        attended = jnp.concatenate(history, axis=0) + terms_ref[0].astype(jnp.float32)
        gates = terms_ref[1].astype(jnp.float32)
        mixed = []
        for low in range(0, width, HD):
            head = attended[:, low : low + HD]
            level = lax.rsqrt(jnp.mean(head * head, axis=-1, keepdims=True) + EPS)
            mixed.append((head * level * gates[:, low : low + HD]).astype(jnp.bfloat16))
        total = total + jnp.dot(jnp.concatenate(mixed, axis=1), w_ref[...], preferred_element_type=jnp.float32)
    out_ref[...] = total.reshape(out_ref.shape).astype(jnp.bfloat16)


def far_first(count):
    return list(reversed(range(count)))


def swap(rows):
    return lax.ppermute(rows, "serve", [(0, 1), (1, 0)])


def cross(owners, messages):
    came = []
    for at in far_first(len(messages)):
        steps = [2 * (at + 1) + side for side in range(2)]
        pairs = [(place * 2 + core_of(step), (place ^ step) * 2 + core_of(step)) for place in range(owners) for step in steps]
        came.append(lax.ppermute(messages[at], ("cache", "serve"), pairs))
    return came


def to_neighbour(owners, rows):
    return lax.ppermute(rows, "cache", [(place, place ^ 1) for place in range(owners)])


def body(candidates, input_gain, w_in, w_out, hist_keys, hist_values, request_session, hist_len, block_mask):
    owners = lax.axis_size("cache")
    req_count, half_cands, model_width = candidates.shape
    width = w_in.shape[2]
    rows = req_count * half_cands
    hist_rows = hist_keys.shape[1]
    bf16 = functools.partial(jax.ShapeDtypeStruct, dtype=jnp.bfloat16)
    sessions = request_session.reshape(-1)
    gain = input_gain.reshape(-1, HD)
    messages = owners // 2 - 1
    piece = 2 * CAP * half_cands

    session_row = request_session.reshape(1, -1)
    placed = kernel_call(
        functools.partial(front_kernel, owners),
        [bf16(((messages + 2) * piece, columns)) for columns in (model_width, rows)],
        [vmem] * 2,
    )(session_row, candidates)
    other, placed = lax.optimization_barrier((swap(candidates), placed))
    out = kernel_call(message_kernel, [bf16((piece, model_width))] * (messages + 2), [vmem] * 3)(*placed, other)
    (local, near, *out), w_in = lax.optimization_barrier((out, w_in))
    weights = jnp.transpose(w_in, (1, 0, 2))
    near = to_neighbour(owners, near)
    came = cross(owners, out)
    came, near, weights = lax.optimization_barrier((came, near, weights))
    stacked = kernel_call(stack_kernel, bf16((messages * piece, model_width)), [vmem] * messages)(*came)
    visible = kernel_call(
        visible_kernel,
        [bf16((owners * piece, HD)), bf16((hist_rows, HD))],
        [vmem] * 3,
        [pltpu.VMEM((HD, owners * req_count), jnp.bfloat16)],
        flops=2 * messages * piece * model_width * width,
    )(session_row, hist_len.reshape(1, -1), lax.optimization_barrier((block_mask.T, stacked))[0])
    swapped, (hide_rows, hide_cols), w_out = lax.optimization_barrier((swap(stacked), visible, w_out))
    w_other = swap(w_out)
    local, near, keep, give = kernel_call(
        functools.partial(history_kernel, owners),
        [bf16((rows_out, width)) for rows_out in (piece // 2, piece, messages * piece, messages * piece + piece // 2)],
        [vmem] * (6 + owners // 2 + 2),
        flops=8 * owners * piece * hist_rows * width,
        moved=4 * hist_rows * width,
    )(
        gain,
        weights,
        hide_rows,
        hide_cols,
        hist_keys.reshape(hist_rows, width),
        hist_values.reshape(hist_rows, width),
        local,
        near,
        *reversed(came),
        swapped,
    )
    near = to_neighbour(owners, near)
    keep, give, w_other = lax.optimization_barrier((keep, give, w_other))
    got = swap(give)
    terms = kernel_call(
        self_kernel,
        [bf16((2, rows, width))] * 2,
        [vmem] * 4,
        [pltpu.VMEM((2 * rows, model_width), jnp.bfloat16)],
        flops=16 * rows * model_width * width,
        moved=8 * model_width * width,
    )(candidates, lax.optimization_barrier((other, give))[0], gain, weights)
    got, (keep_terms, give_terms) = lax.optimization_barrier((got, terms))
    backs = cross(owners, kernel_call(pack_kernel, [bf16((2 * piece, width))] * messages, [vmem] * 2)(keep, got))
    their_near = swap(near[piece // 2 :])
    returned = [rows_of for back in backs for rows_of in (back, swap(back[piece:]))]
    return kernel_call(
        functools.partial(output_kernel, owners),
        bf16((req_count, half_cands, model_width)),
        [smem] + [vmem] * (9 + 2 * messages),
        [pltpu.VMEM((2 * owners * CAP, half_cands, width), jnp.float32)],
        flops=8 * rows * model_width * width,
        moved=4 * model_width * width,
    )(sessions, candidates, keep_terms, swap(give_terms), w_out, w_other, local, got, near, their_near, *returned)


def solution(mesh):
    placed = (
        P(("groups", "cache"), "serve", None),
        P(),
        P(None, None, "serve"),
        P("serve", None),
        P(("groups", "cache"), None, "serve"),
        P(("groups", "cache"), None, "serve"),
        P("groups", None),
        P("groups"),
        P("groups", None),
    )
    return jax.shard_map(
        body,
        mesh=mesh,
        in_specs=placed,
        out_specs=P(("groups", "cache"), "serve", None),
        check_vma=False,
    )
```
